32 devices in a mesh: seq: 4 (over y, core), fsdp: 8 (over z, x).
Axes of the slice: x: 2, y: 2, z: 4, core: 2. Of those that a mesh axis runs over, the one named last changes fastest.
Arguments:
- inputs: bfloat16 [16, 1024, 1152], P('fsdp', 'seq'), may hold values from -6 to 6
- cotangent: bfloat16 [16, 1024, 1152], P('fsdp', 'seq'), may hold values from -6 to 6
- segments: int32 [16, 1024], P('fsdp', 'seq'), may hold values from 0 to 2, as said below
- exits: int32 [16, 1024], P('fsdp', 'seq'), may hold values from 0 to 2, as said below
- confidence: float32 [16, 1024], P('fsdp', 'seq'), may hold values from 0.05 to 1
- attn_gain: bfloat16 [1152], P('fsdp'), may hold values from 0.099609375 to 1.8984375
- q_weight: bfloat16 [1152, 1024], P('fsdp'), may hold values from -0.1875 to 0.1875
- k_weight: bfloat16 [1152, 256], P('fsdp'), may hold values from -0.1875 to 0.1875
- v_weight: bfloat16 [1152, 256], P('fsdp'), may hold values from -0.1875 to 0.1875
- o_weight: bfloat16 [1024, 1152], P('fsdp'), may hold values from -1 to 1
- q_down: bfloat16 [1152, 256], P('fsdp'), may hold values from -0.1875 to 0.1875
- q_up: bfloat16 [256, 1024], P('fsdp'), may hold values from -0.1875 to 0.1875
- k_down: bfloat16 [1152, 256], P('fsdp'), may hold values from -0.1875 to 0.1875
- k_up: bfloat16 [256, 256], P('fsdp'), may hold values from -0.1875 to 0.1875
- v_down: bfloat16 [1152, 256], P('fsdp'), may hold values from -0.1875 to 0.1875
- v_up: bfloat16 [256, 256], P('fsdp'), may hold values from -0.1875 to 0.1875
- o_down: bfloat16 [1024, 256], P('fsdp'), may hold values from -1 to 1
- o_up: bfloat16 [256, 1152], P('fsdp'), may hold values from -0.1875 to 0.1875
- mlp_gain: bfloat16 [1152], P('fsdp'), may hold values from 0.099609375 to 1.8984375
- gate_weight: bfloat16 [1152, 6912], P('fsdp'), may hold values from -0.1875 to 0.1875
- up_weight: bfloat16 [1152, 6912], P('fsdp'), may hold values from -0.1875 to 0.1875
- down_weight: bfloat16 [6912, 1152], P('fsdp'), may hold values from -0.078125 to 0.078125
- gate_down: bfloat16 [1152, 256], P('fsdp'), may hold values from -0.1875 to 0.1875
- gate_up: bfloat16 [256, 6912], P('fsdp'), may hold values from -0.1875 to 0.1875
- up_down: bfloat16 [1152, 256], P('fsdp'), may hold values from -0.1875 to 0.1875
- up_up: bfloat16 [256, 6912], P('fsdp'), may hold values from -0.1875 to 0.1875
- down_down: bfloat16 [6912, 256], P('fsdp'), may hold values from -0.078125 to 0.078125
- down_up: bfloat16 [256, 1152], P('fsdp'), may hold values from -0.1875 to 0.1875
Outputs:
- outputs: bfloat16 [16, 1024, 1152], P('fsdp', 'seq')
- input_grad: bfloat16 [16, 1024, 1152], P('fsdp', 'seq')
- grad_attn_gain: float32 [1152], P('fsdp')
- grad_q_weight: float32 [1152, 1024], P('fsdp')
- grad_k_weight: float32 [1152, 256], P('fsdp')
- grad_v_weight: float32 [1152, 256], P('fsdp')
- grad_o_weight: float32 [1024, 1152], P('fsdp')
- grad_q_down: float32 [1152, 256], P('fsdp')
- grad_q_up: float32 [256, 1024], P('fsdp')
- grad_k_down: float32 [1152, 256], P('fsdp')
- grad_k_up: float32 [256, 256], P('fsdp')
- grad_v_down: float32 [1152, 256], P('fsdp')
- grad_v_up: float32 [256, 256], P('fsdp')
- grad_o_down: float32 [1024, 256], P('fsdp')
- grad_o_up: float32 [256, 1152], P('fsdp')
- grad_mlp_gain: float32 [1152], P('fsdp')
- grad_gate_weight: float32 [1152, 6912], P('fsdp')
- grad_up_weight: float32 [1152, 6912], P('fsdp')
- grad_down_weight: float32 [6912, 1152], P('fsdp')
- grad_gate_down: float32 [1152, 256], P('fsdp')
- grad_gate_up: float32 [256, 6912], P('fsdp')
- grad_up_down: float32 [1152, 256], P('fsdp')
- grad_up_up: float32 [256, 6912], P('fsdp')
- grad_down_down: float32 [6912, 256], P('fsdp')
- grad_down_up: float32 [256, 1152], P('fsdp')
- exit_counts: int32 [3], replicated
- mean_confidence: float32 [3], replicated
The draws below stay inside these ranges and needn't reach their ends.
Inputs may be any that keep to these rules, and one draw needn't show every extreme that they name: `segments`: along each row, with places counted from 0, the document numbers never fall and take the values 0, 1, 2, each on at least one token; document 1 begins at a place from 1 to 128, and document 2 begins at a place from 896 to 1023. The first token of row r exits at depth r mod 3, so every depth is the exit depth of some token of the batch.
All inputs are finite; a program needn't handle non-finite values.
Results may differ from the reference program's by a relative error of at most 0.025.
Values may be sent and summed in bfloat16 or wider, within the bound.
A program may use at most 320 MiB of HBM per device.

```python
import jax
import jax.numpy as jnp
from jax import lax

D = 1152
FF = 6912
H = 4
HD = 256
R = 256
DEPTHS = 3
LOOP = 1
GROUP = 256
HQ = 1024
LEN = 1024
ROWS = 16


def draw_segments(key, part):
    key = jax.random.fold_in(key, 11)
    first_key, last_key = jax.random.split(key)
    begin = jax.random.randint(first_key, (ROWS, 1), 1, GROUP // 2 + 1)
    finish = jax.random.randint(last_key, (ROWS, 1), LEN - GROUP // 2, LEN)
    places = jnp.arange(LEN, dtype=jnp.int32)[None, :]
    return (places >= begin).astype(jnp.int32) + (places >= finish).astype(jnp.int32)


def draw_exits(key, part):
    key = jax.random.fold_in(key, 13)
    base_depths = jax.random.randint(key, (ROWS, LEN), 0, DEPTHS, dtype=jnp.int32)
    leading = jnp.arange(ROWS, dtype=jnp.int32) % DEPTHS
    return base_depths.at[:, 0].set(leading)


def block_scale(key, dims, cuts, least, top_value):
    loudness = 1.0
    for position, parts in cuts:
        draws = jax.random.uniform(jax.random.fold_in(jax.random.fold_in(key, 6), position), (parts,), jnp.float32, least / len(cuts), top_value / len(cuts))
        loudness = loudness * jnp.repeat(jnp.exp(draws), dims[position] // parts).reshape((-1,) + (1,) * (len(dims) - 1 - position))
    return loudness


def bell_draw(stream_key, extent, spread, limit, shards=(), held_as=jnp.bfloat16):
    array = spread * jax.random.normal(stream_key, extent, jnp.float32)
    if shards:
        array = array * block_scale(stream_key, extent, shards, -0.22, 0.18)
    return jnp.clip(array, -limit, limit).astype(held_as)


def setup_inputs(seed: int = 0) -> dict:
    streams_of = jax.random.split(jax.random.key(seed), 29)
    return {
        "inputs": bell_draw(streams_of[0], (ROWS, LEN, D), 1.0, 6.0, ((0, 8), (1, 4))),
        "cotangent": bell_draw(streams_of[1], (ROWS, LEN, D), 1.0, 6.0, ((0, 8), (1, 4))),
        "segments": draw_segments(jax.random.fold_in(streams_of[28], 71), 0),
        "exits": draw_exits(jax.random.fold_in(streams_of[28], 71), 0),
        "confidence": jnp.clip(0.05 + 0.95 * jax.random.uniform(streams_of[4], (ROWS, LEN), jnp.float32) ** block_scale(streams_of[4], (ROWS, LEN), ((0, 8), (1, 4)), -0.2, 0.2), 0.05, 1.0),
        "attn_gain": jnp.clip(1.0 + 0.18 * jax.random.normal(streams_of[5], (D,), jnp.float32), 0.099609375, 1.8984375).astype(jnp.bfloat16),
        "q_weight": bell_draw(streams_of[6], (D, HQ), D ** -0.5, 0.1875, ((0, 8),)),
        "k_weight": bell_draw(streams_of[7], (D, HD), D ** -0.5, 0.1875, ((0, 8),)),
        "v_weight": bell_draw(streams_of[8], (D, HD), D ** -0.5, 0.1875, ((0, 8),)),
        "o_weight": bell_draw(streams_of[9], (HQ, D), (HQ // 32) ** -0.5, 1.0, ((0, 8),)),
        "q_down": bell_draw(streams_of[10], (D, R), D ** -0.5, 0.1875, ((0, 8),)),
        "q_up": bell_draw(streams_of[11], (R, HQ), (4 * R) ** -0.5, 0.1875, ((0, 8),)),
        "k_down": bell_draw(streams_of[12], (D, R), D ** -0.5, 0.1875, ((0, 8),)),
        "k_up": bell_draw(streams_of[13], (R, HD), (4 * R) ** -0.5, 0.1875, ((0, 8),)),
        "v_down": bell_draw(streams_of[14], (D, R), D ** -0.5, 0.1875, ((0, 8),)),
        "v_up": bell_draw(streams_of[15], (R, HD), (4 * R) ** -0.5, 0.1875, ((0, 8),)),
        "o_down": bell_draw(streams_of[16], (HQ, R), (HQ // 32) ** -0.5, 1.0, ((0, 8),)),
        "o_up": bell_draw(streams_of[17], (R, D), (4 * R) ** -0.5, 0.1875, ((0, 8),)),
        "mlp_gain": jnp.clip(1.0 + 0.18 * jax.random.normal(streams_of[18], (D,), jnp.float32), 0.099609375, 1.8984375).astype(jnp.bfloat16),
        "gate_weight": bell_draw(streams_of[19], (D, FF), D ** -0.5, 0.1875, ((0, 8),)),
        "up_weight": bell_draw(streams_of[20], (D, FF), D ** -0.5, 0.1875, ((0, 8),)),
        "down_weight": bell_draw(streams_of[21], (FF, D), FF ** -0.5, 0.078125, ((0, 8),)),
        "gate_down": bell_draw(streams_of[22], (D, R), D ** -0.5, 0.1875, ((0, 8),)),
        "gate_up": bell_draw(streams_of[23], (R, FF), (4 * R) ** -0.5, 0.1875, ((0, 8),)),
        "up_down": bell_draw(streams_of[24], (D, R), D ** -0.5, 0.1875, ((0, 8),)),
        "up_up": bell_draw(streams_of[25], (R, FF), (4 * R) ** -0.5, 0.1875, ((0, 8),)),
        "down_down": bell_draw(streams_of[26], (FF, R), FF ** -0.5, 0.078125, ((0, 8),)),
        "down_up": bell_draw(streams_of[27], (R, D), (4 * R) ** -0.5, 0.1875, ((0, 8),)),
    }


@jax.custom_vjp
def low(v):
    return lax.optimization_barrier(v.astype(jnp.bfloat16)).astype(jnp.float32)

@jax.custom_vjp
def low_back(v):
    return v

def low_keep(v):
    return (low(v), None)

def low_pass(kept, grad):
    return (grad,)

def back_keep(v):
    return (v, None)

def back_low(kept, grad):
    return (low(grad),)
low.defvjp(low_keep, low_pass)
low_back.defvjp(back_keep, back_low)
epsilon = 1e-06
rope_base = 10000.0
highest = lax.Precision.HIGHEST

def matmul(left, right):
    return jnp.dot(left, right, precision=highest)

def rms_norm(values, gain):
    return values * lax.rsqrt(lax.optimization_barrier(jnp.mean(values * values, axis=-1, keepdims=True)) + epsilon) * gain

def adapted_matrix(source, base_matrix, down_matrix, up_matrix):
    low_inner = low(low_back(matmul(source, down_matrix)))
    return matmul(source, base_matrix) + matmul(low_inner, up_matrix)

def rotate(values, positions, sign):
    half_width = values.shape[-1] // 2
    frequency = rope_base ** (-2.0 * jnp.arange(half_width, dtype=jnp.float32) / values.shape[-1])
    angles = sign * positions.astype(jnp.float32)[:, None] * frequency[None, :]
    cosine = jnp.cos(angles)[:, None, :]
    sine_part = jnp.sin(angles)[:, None, :]
    first_half = values[..., :half_width]
    second_half = values[..., half_width:]
    return jnp.concatenate([first_half * cosine - second_half * sine_part, second_half * cosine + first_half * sine_part], axis=-1)

def attend(queries, keys_rot, values, seg_row):
    length = queries.shape[0]
    places = jnp.arange(length, dtype=jnp.int32)
    scores = jnp.einsum('qhd,kd->hqk', queries, keys_rot, precision=highest) * HD ** (-0.5)
    scores = low_back(scores)
    allowed = (seg_row[:, None] == seg_row[None, :]) & (places[None, :] <= places[:, None])
    scores = jnp.where(allowed[None], scores, -1e+30)
    row_top = lax.optimization_barrier(jnp.max(scores, axis=-1, keepdims=True))
    weights = jnp.exp(scores - row_top)
    probs = low(weights / lax.optimization_barrier(jnp.sum(weights, axis=-1, keepdims=True)))
    return jnp.einsum('hqk,kd->qhd', probs, values, precision=highest)

def layer_row(resid, active, seg_row, params):
    attn_gain, q_weight, k_weight, v_weight, o_weight, q_down, q_up, k_down, k_up, v_down, v_up, o_down, o_up, mlp_gain, gate_weight, up_weight, down_weight, gate_down, gate_up, up_down, up_up, down_down, down_up = params
    length = resid.shape[0]
    places = jnp.arange(length, dtype=jnp.int32)
    normed = low(rms_norm(resid, attn_gain))
    q_lin = low_back(adapted_matrix(normed, q_weight, q_down, q_up)).reshape(length, H, HD)
    k_lin = low_back(adapted_matrix(normed, k_weight, k_down, k_up))
    values = low(low_back(adapted_matrix(normed, v_weight, v_down, v_up)))
    queries = low(rotate(q_lin, places, 1.0))
    keys_rot = low(rotate(k_lin[:, None, :], places, 1.0)[:, 0, :])
    attn = low(low_back(attend(queries, keys_rot, values, seg_row).reshape(length, H * HD)))
    branch_attn = low_back(adapted_matrix(attn, o_weight, o_down, o_up))
    middle = resid + active[:, None] * branch_attn
    normed2 = low(rms_norm(middle, mlp_gain))
    gate = low_back(adapted_matrix(normed2, gate_weight, gate_down, gate_up))
    up_linear_output = low_back(adapted_matrix(normed2, up_weight, up_down, up_up))
    hidden = low(jax.nn.gelu(gate, approximate=True) * up_linear_output)
    feedforward_branch = low_back(adapted_matrix(hidden, down_weight, down_down, down_up))
    return middle + active[:, None] * feedforward_branch

def reference(inputs, cotangent, segments, exits, confidence, attn_gain, q_weight, k_weight, v_weight, o_weight, q_down, q_up, k_down, k_up, v_down, v_up, o_down, o_up, mlp_gain, gate_weight, up_weight, down_weight, gate_down, gate_up, up_down, up_up, down_down, down_up):
    params = tuple((weight_item.astype(jnp.float32) for weight_item in (attn_gain, q_weight, k_weight, v_weight, o_weight, q_down, q_up, k_down, k_up, v_down, v_up, o_down, o_up, mlp_gain, gate_weight, up_weight, down_weight, gate_down, gate_up, up_down, up_up, down_down, down_up)))

    def one_row(totals, row_data):
        row_in, row_cot, row_seg, row_exit = row_data
        active = (row_exit >= LOOP).astype(jnp.float32)

        def forward(resid, par):
            return layer_row(resid, active, row_seg, par)
        result, pullback = jax.vjp(forward, row_in.astype(jnp.float32), params)
        grad_in, grad_par = pullback(row_cot.astype(jnp.float32))
        totals = jax.tree.map(jnp.add, totals, grad_par)
        return (totals, (result.astype(jnp.bfloat16), grad_in.astype(jnp.bfloat16)))
    zeros_all = tuple((jnp.zeros(weight_item.shape, jnp.float32) for weight_item in params))
    grads, (outputs, input_grad) = lax.scan(one_row, zeros_all, (inputs, cotangent, segments, exits))
    g_attn_gain, g_q_weight, g_k_weight, g_v_weight, g_o_weight, g_q_down, g_q_up, g_k_down, g_k_up, g_v_down, g_v_up, g_o_down, g_o_up, g_mlp_gain, g_gate_weight, g_up_weight, g_down_weight, g_gate_down, g_gate_up, g_up_down, g_up_up, g_down_down, g_down_up = grads
    depth_ids = jnp.arange(DEPTHS, dtype=jnp.int32)
    matches = (exits.reshape(-1)[:, None] == depth_ids[None, :]).astype(jnp.float32)
    count_sum = lax.optimization_barrier(jnp.sum(matches, axis=0))
    conf_sum = lax.optimization_barrier(jnp.sum(matches * confidence.reshape(-1)[:, None], axis=0))
    mean_confidence = conf_sum / count_sum
    return (outputs, input_grad, g_attn_gain, g_q_weight, g_k_weight, g_v_weight, g_o_weight, g_q_down, g_q_up, g_k_down, g_k_up, g_v_down, g_v_up, g_o_down, g_o_up, g_mlp_gain, g_gate_weight, g_up_weight, g_down_weight, g_gate_down, g_gate_up, g_up_down, g_up_up, g_down_down, g_down_up, count_sum.astype(jnp.int32), mean_confidence)
```

```python
import jax
import jax.numpy as jnp
from jax import lax
from jax.sharding import PartitionSpec as P

H = 4
HD = 256
DEPTHS = 3
LOOP = 1
CORES = 2

epsilon = 1e-06
rope_base = 10000.0
low = jnp.bfloat16
wide = jnp.float32


def mul(left, right):
    return jnp.dot(left, right, preferred_element_type=wide)


def mul_t(left, right):
    return lax.dot_general(left, right, (((1,), (1,)), ((), ())), preferred_element_type=wide)


def t_mul(left, right):
    return lax.dot_general(left, right, (((0,), (0,)), ((), ())), preferred_element_type=wide)


def ring_order(count, width):
    if width < 2 or count % width or (count // width) % 2:
        return list(range(count))
    depth = count // width
    walk = [0]
    for z in range(depth):
        columns = range(1, width) if z % 2 == 0 else range(width - 1, 0, -1)
        walk += [z * width + x for x in columns]
    walk += [z * width for z in range(depth - 1, 0, -1)]
    return walk


class Ring:
    def __init__(self, count, width):
        self.count = count
        walk = ring_order(count, width)
        self.walk = jnp.array(walk, jnp.int32)
        place = [0] * count
        for spot, device in enumerate(walk):
            place[device] = spot
        self.spot = jnp.array(place, jnp.int32)[lax.axis_index("fsdp")]
        self.up = [(walk[i], walk[(i + 1) % count]) for i in range(count)]
        self.down = [(b, a) for a, b in self.up]

    def at(self, offset):
        return self.walk[lax.rem(self.spot + offset + self.count, self.count)]

    def gather(self, block, flip=False):
        ahead, back, sign = (self.down, self.up, 1) if flip else (self.up, self.down, -1)
        pieces = [(self.at(0), block)]
        first = second = block
        for step in range(1, self.count // 2 + 1):
            first = lax.ppermute(first, "fsdp", ahead)
            pieces.append((self.at(sign * step), first))
            if step <= (self.count - 1) // 2:
                second = lax.ppermute(second, "fsdp", back)
                pieces.append((self.at(-sign * step), second))
        return pieces

    def scatter(self, part, flip=False):
        ahead, back, sign = (self.down, self.up, -1) if flip else (self.up, self.down, 1)
        total = part(self.at(0))
        for way, side, steps in (
            (ahead, sign, self.count // 2),
            (back, -sign, (self.count - 1) // 2),
        ):
            moving = None
            for step in range(steps, 0, -1):
                term = part(self.at(side * step))
                if moving is not None:
                    term = term + moving.astype(wide)
                moving = lax.ppermute(term.astype(low), "fsdp", way)
            if moving is not None:
                total = total + moving.astype(wide)
        return total


class Group:
    def __init__(self, count):
        self.count = count
        self.chips = count // CORES
        me = lax.axis_index("seq")
        self.y, self.core = me // CORES, lax.rem(me, CORES)
        self.sibling = [(i, i ^ 1) for i in range(count)]
        self.order = [(k, c) for k in range(self.chips) for c in range(CORES)]

    def shift(self, k):
        n = self.chips
        return [(i, ((i // CORES + k) % n) * CORES + i % CORES) for i in range(self.count)]

    def index(self, k, c):
        return lax.rem(self.y + k, self.chips) * CORES + (self.core + c) % CORES

    def pieces(self, block):
        mine = [block] + [
            lax.ppermute(block, "seq", self.shift(-k)) for k in range(1, self.chips)
        ]
        out = []
        for piece in mine:
            out += [piece, lax.ppermute(piece, "seq", self.sibling)]
        return out

    def scatter(self, part):
        near = [part(k, 0) for k in range(self.chips)]
        far = [
            lax.ppermute(part(k, 1).astype(low), "seq", self.sibling) for k in range(self.chips)
        ]
        sums = [a + b.astype(wide) for a, b in zip(near, far, strict=True)]
        total = sums[0]
        for k in range(1, self.chips):
            total = total + lax.ppermute(sums[k].astype(low), "seq", self.shift(k)).astype(wide)
        return total

    def laid(self, pieces, axis, dtype):
        width = pieces[0].shape[axis]
        shape = list(pieces[0].shape)
        shape[axis] = width * self.count
        out = jnp.zeros(shape, dtype)
        for (k, c), piece in zip(self.order, pieces, strict=True):
            out = lax.dynamic_update_slice_in_dim(
                out, piece.astype(dtype), self.index(k, c) * width, axis
            )
        return out


def stacked(pieces, count):
    out = jnp.zeros((count,) + pieces[0][1].shape, pieces[0][1].dtype)
    for index, block in pieces:
        out = lax.dynamic_update_index_in_dim(out, block, index, 0)
    return out


def spread_sum(values, axis):
    count = lax.axis_size(axis)
    if count & (count - 1):
        return lax.psum(values, axis)
    step = 1
    while step < count:
        values = values + lax.ppermute(values, axis, [(i, i ^ step) for i in range(count)])
        step *= 2
    return values


def rope(values, cosine, sine):
    half = values.shape[-1] // 2
    first, second = values[..., :half], values[..., half:]
    cosine, sine = cosine[:, None, :], sine[:, None, :]
    return jnp.concatenate([first * cosine - second * sine, second * cosine + first * sine], axis=-1)


def gelu_parts(gate):
    scale = (2.0 / jnp.pi) ** 0.5
    cube = 0.044715
    curve = jnp.tanh(scale * (gate + cube * gate * gate * gate))
    value = 0.5 * gate * (1.0 + curve)
    slope = 0.5 * (1.0 + curve) + 0.5 * gate * (1.0 - curve * curve) * scale * (
        1.0 + 3.0 * cube * gate * gate
    )
    return value, slope


def shards(
    inputs,
    cotangent,
    segments,
    exits,
    confidence,
    attn_gain,
    q_weight,
    k_weight,
    v_weight,
    o_weight,
    q_down,
    q_up,
    k_down,
    k_up,
    v_down,
    v_up,
    o_down,
    o_up,
    mlp_gain,
    gate_weight,
    up_weight,
    down_weight,
    gate_down,
    gate_up,
    up_down,
    up_up,
    down_down,
    down_up,
):
    n_seq, n_f = lax.axis_size("seq"), lax.axis_size("fsdp")
    me = lax.axis_index("seq")
    ring = Ring(n_f, n_seq // CORES)
    group = Group(n_seq)
    rows, length, width = inputs.shape
    tokens = rows * length
    rank = q_down.shape[1]
    hq = q_weight.shape[1]
    ff = gate_weight.shape[1]
    own_rows = q_weight.shape[0]
    rank_rows = q_up.shape[0]
    o_rows = o_weight.shape[0]
    cut = ff // (n_f * n_seq)
    slab = n_f * cut
    scale = HD ** (-0.5)

    gain1 = attn_gain.astype(wide)[:, None]
    gain2 = mlp_gain.astype(wide)[:, None]

    def columns_of(array):
        part = array.shape[1] // n_seq
        return lax.dynamic_slice_in_dim(array, me * part, part, 1)

    def rows_of(array):
        part = array.shape[0] // n_seq
        return lax.dynamic_slice_in_dim(array, me * part, part, 0)

    def whole_by_columns(array):
        part = columns_of(array)
        mine = stacked(ring.gather(part), n_f).reshape(-1, part.shape[1])
        return group.laid(group.pieces(mine), 1, low)

    def whole_by_rows(array, flip=False):
        part = rows_of(array)
        mine = stacked(ring.gather(part, flip), n_f)
        return group.laid(group.pieces(mine), 1, low).reshape(-1, part.shape[1])

    def cut_columns(array):
        view = array.reshape(array.shape[0], n_f, n_seq, cut)
        return lax.dynamic_index_in_dim(view, me, 2, keepdims=False).reshape(-1, slab)

    side1 = jnp.concatenate(
        [
            part.astype(wide) * gain1
            for part in (q_weight, k_weight, v_weight, q_down, k_down, v_down)
        ]
        + [gate_down.astype(wide) * gain2],
        axis=1,
    ).astype(low)
    side1 = whole_by_columns(side1)
    ups = whole_by_rows(jnp.concatenate([q_up, k_up, v_up, o_up, down_up], axis=1), True)
    side_o = whole_by_rows(jnp.concatenate([o_weight, o_down], axis=1))
    up_adapter = whole_by_columns((up_down.astype(wide) * gain2).astype(low))

    kv = HD
    lin = hq + 2 * kv
    qkv_side = side1[:, : lin + 3 * rank]
    gate_adapter = side1[:, lin + 3 * rank :]
    q_raise, k_raise, v_raise = ups[:, :hq], ups[:, hq : hq + kv], ups[:, hq + kv : lin]
    o_raise, d_raise = ups[:, lin : lin + width], ups[:, lin + width :]

    raises = jnp.concatenate([cut_columns(gate_up), cut_columns(up_up)], axis=0)
    raises = stacked(ring.gather(raises, True), n_f)
    g_raise = raises[:, :rank_rows].reshape(-1, slab)
    u_raise = raises[:, rank_rows:].reshape(-1, slab)
    gate_own = cut_columns(gate_weight).astype(wide) + mul(gate_down, g_raise)
    up_own = cut_columns(up_weight).astype(wide) + mul(up_down, u_raise)
    gate_full = stacked(ring.gather((gate_own * gain2).astype(low)), n_f).reshape(-1, slab)
    up_full = stacked(ring.gather((up_own * gain2).astype(low), True), n_f).reshape(-1, slab)
    gate_own, up_own = gate_own.astype(low), up_own.astype(low)
    d_lower = rows_of(down_down)
    down_own = (rows_of(down_weight).astype(wide) + mul(d_lower, d_raise)).astype(low)
    down_full = stacked(ring.gather(down_own), n_f).reshape(slab, width)

    resid = inputs.reshape(tokens, width).astype(wide)
    active = (exits.reshape(tokens) >= LOOP).astype(wide)[:, None]
    cot = cotangent.reshape(tokens, width).astype(wide)
    g_mlp = group.pieces((active * cot).astype(low))
    g_mlp = jnp.concatenate(g_mlp, axis=0)
    places = me * length + jnp.arange(length, dtype=jnp.int32)
    frequency = rope_base ** (-2.0 * jnp.arange(HD // 2, dtype=wide) / HD)
    angles = jnp.tile(places, rows).astype(wide)[:, None] * frequency[None, :]
    cosine, sine = jnp.cos(angles), jnp.sin(angles)
    r1 = lax.rsqrt(jnp.mean(resid * resid, axis=-1, keepdims=True) + epsilon)
    unit1 = (resid * r1).astype(low)
    projected = mul(unit1, qkv_side)
    inner = projected[:, lin:].astype(low)
    q_inner, k_inner, v_inner = inner[:, :rank], inner[:, rank : 2 * rank], inner[:, 2 * rank :]
    q_lin = projected[:, :hq] + mul(q_inner, q_raise)
    k_lin = projected[:, hq : hq + kv] + mul(k_inner, k_raise)
    v_lin = projected[:, hq + kv : lin] + mul(v_inner, v_raise)
    queries = rope(q_lin.reshape(tokens, H, HD), cosine, sine).astype(low)
    queries = queries.reshape(rows, length, H, HD).transpose(0, 2, 1, 3)
    queries = queries.reshape(rows, H * length, HD)
    keys = rope(k_lin.reshape(tokens, 1, HD), cosine, sine).astype(low).reshape(rows, length, HD)
    values = v_lin.astype(low).reshape(rows, length, HD)
    both = group.pieces(jnp.concatenate([keys, values], axis=-1))
    both = jnp.concatenate(both, axis=1)
    keys, values = both[..., :HD], both[..., HD:]
    key_seg = jnp.concatenate(group.pieces(segments.astype(low)), axis=1).astype(jnp.int32)
    key_place = jnp.concatenate(
        [
            group.index(k, c) * length + jnp.arange(length, dtype=jnp.int32)
            for k, c in group.order
        ]
    )
    query_seg, query_place = jnp.tile(segments, (1, H)), jnp.tile(places, H)
    allowed = (query_seg[:, :, None] == key_seg[:, None, :]) & (
        key_place[None, None, :] <= query_place[None, :, None]
    )
    scores = (
        jnp.einsum("sqd,skd->sqk", queries, keys, preferred_element_type=wide) * scale
    )
    scores = jnp.where(allowed, scores, -1e30)
    top = jnp.max(scores, axis=-1, keepdims=True)
    weights = jnp.exp(scores - top)
    totals = jnp.sum(weights, axis=-1, keepdims=True)
    attn = (
        jnp.einsum("sqk,skd->sqd", weights.astype(low), values, preferred_element_type=wide)
        / totals
    )
    log_total = top + jnp.log(totals)

    def to_tokens(rows_heads):
        view = rows_heads.reshape(rows, H, length, HD).transpose(0, 2, 1, 3)
        return view.reshape(tokens, hq)

    def to_heads(flat):
        view = flat.reshape(rows, length, H, HD).transpose(0, 2, 1, 3)
        return view.reshape(rows, H * length, HD)

    attn_low = to_tokens(attn.astype(low))
    projected = mul(attn_low, side_o)
    o_inner = projected[:, width:].astype(low)
    mid = resid + active * (projected[:, :width] + mul(o_inner, o_raise))

    r2 = lax.rsqrt(jnp.mean(mid * mid, axis=-1, keepdims=True) + epsilon)
    unit2 = jnp.concatenate(group.pieces((mid * r2).astype(low)), axis=0)
    gate = mul(unit2, gate_full).astype(low)
    up = mul(unit2, up_full).astype(low)
    value, slope = gelu_parts(gate.astype(wide))
    hidden = (value * up.astype(wide)).astype(low)
    g_down = t_mul(hidden, g_mlp).astype(low)
    branch = mul(hidden, down_full)

    def token_block(array):
        def part(k, c):
            at = group.order.index((k, c)) * tokens
            return array[at : at + tokens]

        return part

    outputs = mid + active * group.scatter(token_block(branch))
    outputs = outputs.astype(low).reshape(rows, length, width)

    def ring_block(array, size):
        return lambda owner: lax.dynamic_slice_in_dim(array, owner * size, size, 0).astype(wide)

    g_down = ring.scatter(ring_block(g_down, cut), True).astype(low)
    g_hidden = mul_t(g_mlp, down_full)
    g_gate = (g_hidden * up.astype(wide) * slope).astype(low)
    g_up = (g_hidden * value).astype(low)
    e2 = mul_t(g_gate, gate_full) + mul_t(g_up, up_full)
    e2 = group.scatter(token_block(e2))
    g_mid = cot + r2 * e2 - mid * (r2 * r2 * r2 * jnp.mean(e2 * mid, axis=-1, keepdims=True))
    gg = t_mul(unit2, g_gate).astype(low)
    gu = t_mul(unit2, g_up).astype(low)
    gg_raise = t_mul(gate_adapter, gg).astype(low)
    gu_raise = t_mul(up_adapter, gu).astype(low)
    gg = ring.scatter(ring_block(gg, own_rows))
    gu = ring.scatter(ring_block(gu, own_rows), True)

    def raise_block(owner):
        return jnp.concatenate(
            [
                lax.dynamic_slice_in_dim(part, owner * rank_rows, rank_rows, 0)
                for part in (gg_raise, gu_raise)
            ],
            axis=0,
        ).astype(wide)

    g_raises = ring.scatter(raise_block).astype(low)

    mlp_small = jnp.concatenate(
        [
            mul_t((gg * gain2).astype(low), g_raise),
            mul_t((gu * gain2).astype(low), u_raise),
            jnp.broadcast_to(
                jnp.sum(
                    gg * gate_own.astype(wide) + gu * up_own.astype(wide), axis=1, keepdims=True
                ),
                (own_rows, 128),
            ),
        ],
        axis=1,
    )
    mlp_small = spread_sum(mlp_small, "seq")
    grad_gate_down, grad_up_down = mlp_small[:, :rank], mlp_small[:, rank : 2 * rank]
    grad_mlp_gain = mlp_small[:, 2 * rank]

    def back_columns(array):
        view = array.reshape(array.shape[0], n_f, cut)
        return group.laid(
            [piece[:, :, None, :] for piece in group.pieces(view)], 2, wide
        ).reshape(array.shape[0], ff)

    grad_gate_weight = back_columns((gg * gain2).astype(low))
    grad_up_weight = back_columns((gu * gain2).astype(low))
    g_raises = back_columns(g_raises)
    grad_gate_up, grad_up_up = g_raises[:rank_rows], g_raises[rank_rows:]
    down_rows = jnp.concatenate([g_down, mul_t(g_down, d_raise).astype(low)], axis=1)
    down_rows = group.laid(group.pieces(down_rows), 0, wide)
    grad_down_weight, grad_down_down = down_rows[:, :width], down_rows[:, width:]
    gd_raise = t_mul(d_lower, g_down).astype(low)

    g_branch = (active * g_mid).astype(low)
    g_inner = mul_t(g_branch, o_raise).astype(low)
    g_attn = mul_t(jnp.concatenate([g_branch, g_inner], axis=1), side_o).astype(low)
    g_o = t_mul(attn_low, g_branch).astype(low)
    go_raise = t_mul(o_inner, g_branch).astype(low)
    o_pack = jnp.concatenate(
        [
            g_o.reshape(n_f, o_rows, width),
            go_raise.reshape(n_f, rank_rows, width),
            gd_raise.reshape(n_f, rank_rows, width),
        ],
        axis=1,
    )

    def whole_sum_rows(pack, flip=False):
        part = pack.shape[1] // n_seq
        mine = group.scatter(
            lambda k, c: lax.dynamic_slice_in_dim(
                pack, group.index(k, c) * part, part, 1
            ).astype(wide)
        ).astype(low)
        done = ring.scatter(
            lambda owner: lax.dynamic_index_in_dim(mine, owner, 0, keepdims=False).astype(wide), flip
        ).astype(low)
        return group.laid(group.pieces(done), 0, wide)

    def whole_sum_columns(pack, flip=False):
        part = pack.shape[2] // n_seq
        mine = group.scatter(
            lambda k, c: lax.dynamic_slice_in_dim(
                pack, group.index(k, c) * part, part, 2
            ).astype(wide)
        ).astype(low)
        done = ring.scatter(
            lambda owner: lax.dynamic_index_in_dim(mine, owner, 0, keepdims=False).astype(wide), flip
        ).astype(low)
        return group.laid(group.pieces(done), 1, wide)

    o_pack = whole_sum_rows(o_pack)
    grad_o_weight = o_pack[:o_rows]
    grad_o_up = o_pack[o_rows : o_rows + rank_rows]
    grad_down_up = o_pack[o_rows + rank_rows :]
    grad_o_down = mul_t(grad_o_weight.astype(low), o_raise)

    g_heads = to_heads(g_attn)
    dots = jnp.sum(g_heads.astype(wide) * attn, axis=-1, keepdims=True)
    scores = (
        jnp.einsum("sqd,skd->sqk", queries, keys, preferred_element_type=wide) * scale
    )
    probs = jnp.where(allowed, jnp.exp(scores - log_total), 0.0)
    d_probs = jnp.einsum("sqd,skd->sqk", g_heads, values, preferred_element_type=wide)
    d_scores = (probs * (d_probs - dots)).astype(low)
    d_query = jnp.einsum("sqk,skd->sqd", d_scores, keys, preferred_element_type=wide) * scale
    d_key = jnp.einsum("sqk,sqd->skd", d_scores, queries, preferred_element_type=wide) * scale
    d_value = jnp.einsum("sqk,sqd->skd", probs.astype(low), g_heads, preferred_element_type=wide)
    d_both = jnp.concatenate([d_key, d_value], axis=-1)

    def key_block(k, c):
        at = group.order.index((k, c)) * length
        return d_both[:, at : at + length]

    d_both = group.scatter(key_block).reshape(tokens, 2 * HD)
    g_q = rope(to_tokens(d_query).reshape(tokens, H, HD), cosine, -sine)
    g_q = g_q.reshape(tokens, hq).astype(low)
    g_k = rope(d_both[:, None, :HD], cosine, -sine).reshape(tokens, HD).astype(low)
    g_v = d_both[:, HD:].astype(low)
    gi_q = mul_t(g_q, q_raise).astype(low)
    gi_k = mul_t(g_k, k_raise).astype(low)
    gi_v = mul_t(g_v, v_raise).astype(low)
    g_lin = jnp.concatenate([g_q, g_k, g_v], axis=1)
    e1 = mul_t(jnp.concatenate([g_lin, gi_q, gi_k, gi_v], axis=1), qkv_side)
    input_grad = g_mid + r1 * e1 - resid * (
        r1 * r1 * r1 * jnp.mean(e1 * resid, axis=-1, keepdims=True)
    )
    input_grad = input_grad.astype(low).reshape(rows, length, width)
    g_qkv = t_mul(unit1, g_lin).astype(low)
    gr_qkv = jnp.concatenate(
        [t_mul(q_inner, g_q), t_mul(k_inner, g_k), t_mul(v_inner, g_v)], axis=1
    ).astype(low)
    qkv_pack = jnp.concatenate(
        [g_qkv.reshape(n_f, own_rows, lin), gr_qkv.reshape(n_f, rank_rows, lin)], axis=1
    )
    qkv_pack = whole_sum_columns(qkv_pack, True)
    unit_grad = qkv_pack[:own_rows]
    grad_lin = unit_grad * gain1
    grad_q_weight, grad_k_weight, grad_v_weight = (
        grad_lin[:, :hq],
        grad_lin[:, hq : hq + kv],
        grad_lin[:, hq + kv :],
    )
    grad_q_up, grad_k_up, grad_v_up = (
        qkv_pack[own_rows:, :hq],
        qkv_pack[own_rows:, hq : hq + kv],
        qkv_pack[own_rows:, hq + kv :],
    )
    grad_q_down = mul_t(grad_q_weight.astype(low), q_raise)
    grad_k_down = mul_t(grad_k_weight.astype(low), k_raise)
    grad_v_down = mul_t(grad_v_weight.astype(low), v_raise)
    own_lin = jnp.concatenate(
        [
            q_weight.astype(wide) + mul(q_down, q_raise),
            k_weight.astype(wide) + mul(k_down, k_raise),
            v_weight.astype(wide) + mul(v_down, v_raise),
        ],
        axis=1,
    )
    grad_attn_gain = jnp.sum(unit_grad * own_lin, axis=1)

    depth_ids = jnp.arange(DEPTHS, dtype=jnp.int32)
    matches = (exits.reshape(tokens)[:, None] == depth_ids[None, :]).astype(wide)
    counted = jnp.concatenate(
        [jnp.sum(matches, axis=0), jnp.sum(matches * confidence.reshape(tokens)[:, None], axis=0)]
    )
    counted = spread_sum(spread_sum(counted, "seq"), "fsdp")
    mean_confidence = counted[DEPTHS:] / counted[:DEPTHS]
    return (
        outputs,
        input_grad,
        grad_attn_gain,
        grad_q_weight,
        grad_k_weight,
        grad_v_weight,
        grad_o_weight,
        grad_q_down,
        grad_q_up,
        grad_k_down,
        grad_k_up,
        grad_v_down,
        grad_v_up,
        grad_o_down,
        grad_o_up,
        grad_mlp_gain,
        grad_gate_weight,
        grad_up_weight,
        grad_down_weight,
        grad_gate_down,
        grad_gate_up,
        grad_up_down,
        grad_up_up,
        grad_down_down,
        grad_down_up,
        counted[:DEPTHS].astype(jnp.int32),
        mean_confidence,
    )


def solution(mesh):
    tokens3 = P("fsdp", "seq", None)
    tokens2 = P("fsdp", "seq")
    vector, matrix = P("fsdp"), P("fsdp", None)
    in_specs = (tokens3,) * 2 + (tokens2,) * 3 + (vector,) + (matrix,) * 12 + (vector,) + (matrix,) * 9
    out_specs = (
        (tokens3,) * 2 + (vector,) + (matrix,) * 12 + (vector,) + (matrix,) * 9 + (P(), P())
    )
    return jax.shard_map(shards, mesh=mesh, in_specs=in_specs, out_specs=out_specs, check_vma=False)
```

```python
import jax
import jax.numpy as jnp
from jax import lax
from jax.experimental import pallas as pl
from jax.experimental.pallas import tpu as pltpu
from jax.sharding import PartitionSpec as P

H = 4
HD = 256
DEPTHS = 3
LOOP = 1
CORES = 2

epsilon = 1e-06
rope_base = 10000.0
low = jnp.bfloat16
wide = jnp.float32


def mul(left, right):
    return jnp.dot(left, right, preferred_element_type=wide)


def mul_t(left, right):
    return lax.dot_general(left, right, (((1,), (1,)), ((), ())), preferred_element_type=wide)


def t_mul(left, right):
    return lax.dot_general(left, right, (((0,), (0,)), ((), ())), preferred_element_type=wide)


def ring_order(count, width):
    if width < 2 or count % width or (count // width) % 2:
        return list(range(count))
    depth = count // width
    walk = [0]
    for z in range(depth):
        columns = range(1, width) if z % 2 == 0 else range(width - 1, 0, -1)
        walk += [z * width + x for x in columns]
    walk += [z * width for z in range(depth - 1, 0, -1)]
    return walk


MESH = pl.DeviceIdType.MESH
ANY = pl.BlockSpec(memory_space=pl.ANY)
VMEM = pl.BlockSpec(memory_space=pltpu.VMEM)


def pick(index, table):
    result = jnp.int32(table[0])
    for spot, value in enumerate(table):
        if spot:
            result = jnp.where(index == spot, jnp.int32(value), result)
    return result


class Places:
    def __init__(self, n_f, n_seq):
        self.n_f, self.n_seq, self.chips = n_f, n_seq, n_seq // CORES
        self.walk = ring_order(n_f, n_seq // CORES)
        spots = [0] * n_f
        for spot, device in enumerate(self.walk):
            spots[device] = spot
        self.f, self.me = lax.axis_index("fsdp"), lax.axis_index("seq")
        self.spot = pick(self.f, spots)
        self.y, self.core = self.me // CORES, lax.rem(self.me, CORES)

    def at(self, offset):
        return pick(lax.rem(self.spot + offset + self.n_f, self.n_f), self.walk)

    def seq(self, k, c):
        return lax.rem(self.y + k + self.chips, self.chips) * CORES + lax.rem(
            self.core + c, CORES
        )

    def greet(self, ring):
        barrier = pltpu.get_barrier_semaphore()
        friends = [{"seq": self.seq(0, 1)}]
        friends += [{"seq": self.seq(k, 0)} for k in range(1, self.chips)]
        if ring:
            friends += [{"fsdp": self.at(1)}, {"fsdp": self.at(-1)}]
        for friend in friends:
            pl.semaphore_signal(barrier, inc=1, device_id=friend, device_id_type=MESH)
        pl.semaphore_wait(barrier, len(friends))


def remote(source, target, send, receive, device):
    return pltpu.make_async_remote_copy(
        src_ref=source,
        dst_ref=target,
        send_sem=send,
        recv_sem=receive,
        device_id=device,
        device_id_type=MESH,
    )


def params(number):
    return pltpu.CompilerParams(
        collective_id=number, has_side_effects=True, vmem_limit_bytes=56 * 2**20
    )


def ring_steps(n_f):
    order = []
    for step in range(1, n_f // 2 + 1):
        order.append((step, 1))
        if step <= (n_f - 1) // 2:
            order.append((step, -1))
    return order


def gather_whole(blocks, number, n_f, n_seq):
    count = len(blocks)
    chips = n_seq // CORES
    steps = ring_steps(n_f)

    def body(*refs):
        ins, outs = refs[:count], refs[count : 2 * count]
        local, ring_s, ring_r, y_s, y_r, core_s, core_r = refs[2 * count :]
        here = Places(n_f, n_seq)
        started = []

        def share(ref, spot):
            width = ref.shape[-1] // n_seq
            return (slice(None), pl.ds(pl.multiple_of(spot * width, 128), width))

        copies = []
        for j in range(count):
            copy = pltpu.make_async_copy(ins[j], outs[j].at[here.f], local.at[j])
            copy.start()
            copies.append(copy)
        here.greet(True)

        def forward(j, step, way):
            owner = here.at(-way * (step - 1))
            mine = share(ins[j], here.me)
            source = ins[j].at[mine] if step == 1 else outs[j].at[(owner, *mine)]
            at = steps.index((step, way))
            copy = remote(
                source,
                outs[j].at[(owner, *mine)],
                ring_s.at[j, at],
                ring_r.at[j, at],
                {"fsdp": here.at(way)},
            )
            copy.start()
            started.append(copy)

        def landed(j, step, way):
            owner = here.at(-way * step)
            mine = share(ins[j], here.me)
            at = steps.index((step, way))
            block = outs[j].at[(owner, *mine)]
            remote(block, block, ring_s.at[j, at], ring_r.at[j, at], {"fsdp": here.at(way)}).wait_recv()
            return owner

        def to_core(j, at, k, owner):
            block = outs[j].at[(owner, *share(ins[j], here.seq(k, 0)))]
            copy = remote(
                block, block, core_s.at[j, at, k], core_r.at[j, at, k], {"seq": here.seq(0, 1)}
            )
            copy.start()
            started.append(copy)

        for j in range(count):
            for way in (1, -1):
                forward(j, 1, way)
        for at, (step, way) in enumerate(steps):
            for j in range(count):
                owner = landed(j, step, way)
                if (step + 1, way) in steps:
                    forward(j, step + 1, way)
                block = outs[j].at[(owner, *share(ins[j], here.me))]
                for k in range(1, chips):
                    copy = remote(
                        block, block, y_s.at[j, at, k], y_r.at[j, at, k], {"seq": here.seq(-k, 0)}
                    )
                    copy.start()
                    started.append(copy)
                to_core(j, at, 0, owner)
        for at, (step, way) in enumerate(steps):
            owner = here.at(-way * step)
            for j in range(count):
                for k in range(1, chips):
                    block = outs[j].at[(owner, *share(ins[j], here.seq(k, 0)))]
                    remote(
                        block, block, y_s.at[j, at, k], y_r.at[j, at, k], {"seq": here.seq(-k, 0)}
                    ).wait_recv()
                    to_core(j, at, k, owner)
        for at, (step, way) in enumerate(steps):
            owner = here.at(-way * step)
            for j in range(count):
                for k in range(chips):
                    block = outs[j].at[(owner, *share(ins[j], here.seq(k, 1)))]
                    remote(
                        block, block, core_s.at[j, at, k], core_r.at[j, at, k], {"seq": here.seq(0, 1)}
                    ).wait_recv()
        for copy in started:
            copy.wait_send()
        for copy in copies:
            copy.wait()

    sems = pltpu.SemaphoreType.DMA
    return pl.pallas_call(
        body,
        out_shape=tuple(jax.ShapeDtypeStruct((n_f,) + b.shape, b.dtype) for b in blocks),
        in_specs=[ANY] * count,
        out_specs=(ANY,) * count,
        scratch_shapes=[sems((count,))]
        + [sems((count, len(steps)))] * 2
        + [sems((count, len(steps), chips))] * 4,
        compiler_params=params(number),
    )(*blocks)


def gather_group(block, number, n_seq):
    rows = block.shape[0]
    chips = n_seq // CORES
    parts = 4 if rows % 64 == 0 else 1
    size = rows // parts

    def body(x, out, local, y_s, y_r, core_s, core_r):
        here = Places(1, n_seq)
        own = pltpu.make_async_copy(x, out.at[0], local)
        own.start()
        here.greet(False)
        started = []

        def to_core(source, k, part):
            cut = pl.ds(part * size, size)
            copy = remote(
                source.at[cut],
                out.at[k * CORES + 1, cut],
                core_s.at[k, part],
                core_r.at[k, part],
                {"seq": here.seq(0, 1)},
            )
            copy.start()
            started.append(copy)

        def over(k, part):
            cut = pl.ds(part * size, size)
            return remote(
                x.at[cut],
                out.at[k * CORES, cut],
                y_s.at[k, part],
                y_r.at[k, part],
                {"seq": here.seq(-k, 0)},
            )

        for part in range(parts):
            for k in range(1, chips):
                copy = over(k, part)
                copy.start()
                started.append(copy)
            to_core(x, 0, part)
        for part in range(parts):
            for k in range(1, chips):
                over(k, part).wait_recv()
                to_core(out.at[k * CORES], k, part)
        for part in range(parts):
            for k in range(chips):
                cut = pl.ds(part * size, size)
                block = out.at[k * CORES + 1, cut]
                remote(
                    block, block, core_s.at[k, part], core_r.at[k, part], {"seq": here.seq(0, 1)}
                ).wait_recv()
        for copy in started:
            copy.wait_send()
        own.wait()

    sems = pltpu.SemaphoreType.DMA
    return pl.pallas_call(
        body,
        out_shape=jax.ShapeDtypeStruct((n_seq,) + block.shape, block.dtype),
        in_specs=[ANY],
        out_specs=ANY,
        scratch_shapes=[sems(())] + [sems((chips, parts))] * 4,
        compiler_params=params(number),
    )(block)


def scatter_group(terms, number):
    n_seq, rows, columns = terms.shape
    chips = n_seq // CORES
    parts = 4 if rows % 64 == 0 else 1
    size = rows // parts

    def body(x, out, near, sums, far, y_s, y_r, core_s, core_r):
        here = Places(1, n_seq)
        here.greet(False)
        started = []

        def cross(k, part):
            cut = pl.ds(part * size, size)
            return remote(
                x.at[k * CORES + 1, cut],
                near.at[k, cut],
                core_s.at[k, part],
                core_r.at[k, part],
                {"seq": here.seq(0, 1)},
            )

        def over(k, part):
            cut = pl.ds(part * size, size)
            return remote(
                sums.at[k, cut],
                far.at[k, cut],
                y_s.at[k, part],
                y_r.at[k, part],
                {"seq": here.seq(k, 0)},
            )

        for k in [*range(1, chips), 0]:
            for part in range(parts):
                copy = cross(k, part)
                copy.start()
                started.append(copy)
        for k in range(1, chips):
            for part in range(parts):
                cut = pl.ds(part * size, size)
                cross(k, part).wait_recv()
                total = x[k * CORES, cut, :].astype(wide) + near[k, cut, :].astype(wide)
                sums[k, cut, :] = total.astype(low)
                copy = over(k, part)
                copy.start()
                started.append(copy)
        for part in range(parts):
            cut = pl.ds(part * size, size)
            cross(0, part).wait_recv()
            out[cut, :] = x[0, cut, :].astype(wide) + near[0, cut, :].astype(wide)
        for part in range(parts):
            cut = pl.ds(part * size, size)
            for k in range(1, chips):
                over(k, part).wait_recv()
                out[cut, :] = out[cut, :] + far[k, cut, :].astype(wide)
        for copy in started:
            copy.wait_send()

    sems = pltpu.SemaphoreType.DMA
    buffer = pltpu.VMEM((chips, rows, columns), low)
    return pl.pallas_call(
        body,
        out_shape=jax.ShapeDtypeStruct((rows, columns), wide),
        in_specs=[VMEM],
        out_specs=VMEM,
        scratch_shapes=[buffer] * 3 + [sems((chips, parts))] * 4,
        compiler_params=params(number),
    )(terms)


def scatter_whole(packs, number, n_seq):
    wanted = [pack.shape[2] for pack in packs]
    gaps = [-count % (128 * n_seq) for count in wanted]
    packs = [
        jnp.pad(pack, ((0, 0), (0, 0), (0, gap))) if gap else pack
        for pack, gap in zip(packs, gaps, strict=True)
    ]
    n_f, count = packs[0].shape[0], len(packs)
    chips = n_seq // CORES
    widths = [pack.shape[2] // n_seq for pack in packs]
    steps = ring_steps(n_f)
    offsets = [way * step for step, way in reversed(steps)] + [0]
    last = {way: max(step for step, w in steps if w == way) for way in (1, -1)}

    def body(*refs):
        xs, outs = refs[:count], refs[count : 2 * count]
        buffers, sem = refs[2 * count : 7 * count], refs[7 * count :]
        nears, sums, fars, terms, moves = (
            buffers[i * count : (i + 1) * count] for i in range(5)
        )
        core_s, core_r, y_s, y_r, ring_s, ring_r, over_s, over_r, side_s, side_r = sem
        here = Places(n_f, n_seq)
        here.greet(True)
        started = []

        def share(j, spot):
            return pl.ds(pl.multiple_of(spot * widths[j], 128), widths[j])

        def cross(j, i, k):
            owner = here.at(offsets[i])
            return remote(
                xs[j].at[owner, :, share(j, here.seq(k, 1))],
                nears[j].at[i, k],
                core_s.at[j, i, k],
                core_r.at[j, i, k],
                {"seq": here.seq(0, 1)},
            )

        def over(j, i, k):
            return remote(
                sums[j].at[i, k],
                fars[j].at[i, k],
                y_s.at[j, i, k],
                y_r.at[j, i, k],
                {"seq": here.seq(k, 0)},
            )

        def hop(j, step, way):
            at = steps.index((step, way))
            return remote(
                terms[j].at[at],
                moves[j].at[at],
                ring_s.at[j, at],
                ring_r.at[j, at],
                {"fsdp": here.at(way)},
            )

        def go(copy):
            copy.start()
            started.append(copy)

        for i in range(n_f):
            for j in range(count):
                for k in [*range(1, chips), 0]:
                    go(cross(j, i, k))
        for i in range(n_f):
            owner = here.at(offsets[i])
            for j in range(count):
                for k in range(1, chips):
                    cross(j, i, k).wait_recv()
                    mine = xs[j][owner, :, share(j, here.seq(k, 0))].astype(wide)
                    sums[j][i, k] = (mine + nears[j][i, k].astype(wide)).astype(low)
                    go(over(j, i, k))
        for i in range(n_f):
            owner = here.at(offsets[i])
            for j in range(count):
                cross(j, i, 0).wait_recv()
                total = xs[j][owner, :, share(j, here.me)].astype(wide)
                total = total + nears[j][i, 0].astype(wide)
                for k in range(1, chips):
                    over(j, i, k).wait_recv()
                    total = total + fars[j][i, k].astype(wide)
                if offsets[i]:
                    step, way = abs(offsets[i]), 1 if offsets[i] > 0 else -1
                    if step < last[way]:
                        hop(j, step + 1, way).wait_recv()
                        total = total + moves[j][steps.index((step + 1, way))].astype(wide)
                    terms[j][steps.index((step, way))] = total.astype(low)
                    go(hop(j, step, way))
                else:
                    for way in (1, -1):
                        if last[way] >= 1:
                            hop(j, 1, way).wait_recv()
                            total = total + moves[j][steps.index((1, way))].astype(wide)
                    outs[j][:, share(j, here.me)] = total.astype(low)

        def swap(j, k, spot):
            block = outs[j].at[:, share(j, spot)]
            return remote(block, block, over_s.at[j, k], over_r.at[j, k], {"seq": here.seq(-k, 0)})

        def side(j, k, spot):
            block = outs[j].at[:, share(j, spot)]
            return remote(block, block, side_s.at[j, k], side_r.at[j, k], {"seq": here.seq(0, 1)})

        for j in range(count):
            for k in range(1, chips):
                go(swap(j, k, here.me))
            go(side(j, 0, here.me))
        for j in range(count):
            for k in range(1, chips):
                swap(j, k, here.seq(k, 0)).wait_recv()
                go(side(j, k, here.seq(k, 0)))
        for j in range(count):
            for k in range(chips):
                side(j, k, here.seq(k, 1)).wait_recv()
        for copy in started:
            copy.wait_send()

    sems = pltpu.SemaphoreType.DMA
    shapes = [(pack.shape[1], width) for pack, width in zip(packs, widths, strict=True)]
    full = [pltpu.VMEM((n_f, chips, *shape), low) for shape in shapes]
    ring = [pltpu.VMEM((len(steps), *shape), low) for shape in shapes]
    results = pl.pallas_call(
        body,
        out_shape=tuple(jax.ShapeDtypeStruct(pack.shape[1:], low) for pack in packs),
        in_specs=[VMEM] * count,
        out_specs=(VMEM,) * count,
        scratch_shapes=full * 3
        + ring * 2
        + [sems((count, n_f, chips))] * 4
        + [sems((count, len(steps)))] * 2
        + [sems((count, chips))] * 4,
        compiler_params=params(number),
    )(*packs)
    return [result[:, :size] for result, size in zip(results, wanted, strict=True)]


class Ring:
    def __init__(self, count, width):
        self.count = count
        walk = ring_order(count, width)
        self.walk = jnp.array(walk, jnp.int32)
        place = [0] * count
        for spot, device in enumerate(walk):
            place[device] = spot
        self.spot = jnp.array(place, jnp.int32)[lax.axis_index("fsdp")]
        self.up = [(walk[i], walk[(i + 1) % count]) for i in range(count)]
        self.down = [(b, a) for a, b in self.up]

    def at(self, offset):
        return self.walk[lax.rem(self.spot + offset + self.count, self.count)]

    def hop(self, block, way):
        return lax.ppermute(block, "fsdp", self.up if way > 0 else self.down)


class Gathering:
    def __init__(self, ring, block, buffers, keep):
        self.ring, self.buffers, self.keep = ring, buffers, keep
        self.step, self.steps = 0, ring.count // 2
        self.moving = (block, block)
        self.new = [(0, block)]

    def advance(self):
        self.settle()
        if self.step == self.steps:
            return
        self.step += 1
        first, second = self.moving
        if self.step < self.steps:
            self.moving = (self.ring.hop(first, 1), self.ring.hop(second, -1))
            self.new = [(-self.step, self.moving[0]), (self.step, self.moving[1])]
        else:
            half = first.shape[1] // 256 * 128
            self.moving = (
                self.ring.hop(first[:, :half], 1),
                self.ring.hop(second[:, half:], -1),
            )
            self.new = [(self.step, jnp.concatenate(self.moving, axis=1))]

    def settle(self):
        for offset, block in self.new:
            self.buffers = self.keep(self.buffers, self.ring.at(offset), block)
        self.new = []

    def done(self):
        while self.step < self.steps:
            self.advance()
        self.settle()
        return self.buffers

    def live(self):
        return (self.moving, self.buffers, [block for _, block in self.new])

    def restore(self, live):
        self.moving, self.buffers, blocks = live
        self.new = [(offset, block) for (offset, _), block in zip(self.new, blocks, strict=True)]


class Scattering:
    def __init__(self, ring, part):
        self.ring, self.part = ring, part
        self.step, self.steps = 0, ring.count // 2
        self.moving = ()

    def advance(self):
        if self.step == self.steps:
            return
        self.step += 1
        offset = self.steps - self.step + 1
        if self.step == 1:
            term = self.part(self.ring.at(offset))
            self.half = term.shape[1] // 256 * 128
            ahead, back = term[:, : self.half], term[:, self.half :]
        else:
            ahead, back = self.joined(offset)
        self.moving = (
            self.ring.hop(ahead.astype(low), 1),
            self.ring.hop(back.astype(low), -1),
        )

    def joined(self, offset):
        ahead, back = self.part(self.ring.at(offset)), self.part(self.ring.at(-offset))
        first, second = (block.astype(wide) for block in self.moving)
        if self.step == 2:
            first = jnp.pad(first, ((0, 0), (0, ahead.shape[1] - self.half)))
            second = jnp.pad(second, ((0, 0), (self.half, 0)))
        return ahead + first, back + second

    def done(self):
        while self.step < self.steps:
            self.advance()
        total = self.part(self.ring.at(0))
        for block in self.moving:
            total = total + block.astype(wide)
        return total

    def live(self):
        return self.moving

    def restore(self, live):
        self.moving = live


def tie(movers, values):
    lives, values = lax.optimization_barrier(([mover.live() for mover in movers], values))
    for mover, live in zip(movers, lives, strict=True):
        mover.restore(live)
    return values


class Group:
    def __init__(self, count):
        self.count = count
        self.chips = count // CORES
        me = lax.axis_index("seq")
        self.y, self.core = me // CORES, lax.rem(me, CORES)
        self.sibling = [(i, i ^ 1) for i in range(count)]
        self.order = [(k, c) for k in range(self.chips) for c in range(CORES)]

    def shift(self, k):
        n = self.chips
        return [(i, ((i // CORES + k) % n) * CORES + i % CORES) for i in range(self.count)]

    def index(self, k, c):
        return lax.rem(self.y + k, self.chips) * CORES + (self.core + c) % CORES

    def over(self, block):
        return [block] + [
            lax.ppermute(block, "seq", self.shift(-k)) for k in range(1, self.chips)
        ]

    def across(self, blocks):
        out = []
        for block in blocks:
            out += [block, lax.ppermute(block, "seq", self.sibling)]
        return out

    def cross(self, terms):
        return [
            lax.ppermute(terms[k * CORES + 1], "seq", self.sibling) for k in range(self.chips)
        ]

    def send(self, sums):
        return [
            lax.ppermute(sums[k].astype(low), "seq", self.shift(k)) for k in range(1, self.chips)
        ]

    def laid(self, pieces, axis, dtype):
        width = pieces[0].shape[axis]
        shape = list(pieces[0].shape)
        shape[axis] = width * self.count
        out = jnp.zeros(shape, dtype)
        for (k, c), piece in zip(self.order, pieces, strict=True):
            out = lax.dynamic_update_slice_in_dim(
                out, piece.astype(dtype), self.index(k, c) * width, axis
            )
        return out


class Summing:
    def __init__(self, values, axes):
        self.values = values
        self.steps = [
            (axis, 1 << bit)
            for axis in axes
            for bit in range((lax.axis_size(axis) - 1).bit_length())
        ]
        assert all(lax.axis_size(axis) & (lax.axis_size(axis) - 1) == 0 for axis in axes)

    def advance(self):
        if self.steps:
            axis, step = self.steps.pop(0)
            pairs = [(i, i ^ step) for i in range(lax.axis_size(axis))]
            self.values = self.values + lax.ppermute(self.values, axis, pairs)

    def done(self):
        while self.steps:
            self.advance()
        return self.values

    def live(self):
        return self.values

    def restore(self, live):
        self.values = live


def cut_columns(weights, raises, gains, n_f, n_seq, slab):
    rows, ff = weights[0].shape
    rank_rows = raises[0].shape[0]
    block, cut = ff // n_f, ff // (n_f * n_seq)

    def body(gain_ref, w0, w1, r0, r1, out):
        me = lax.axis_index("seq")

        def run(ref, spot):
            runs = [
                ref[:, f * block + spot * cut : f * block + (spot + 1) * cut] for f in range(n_f)
            ]
            gap = slab - n_f * cut
            if gap:
                runs.append(jnp.zeros((ref.shape[0], gap), ref.dtype))
            return jnp.concatenate(runs, axis=1)

        for spot in range(n_seq):

            @pl.when(me == spot)
            def _():
                for side, (weight, raised) in enumerate(((w0, r0), (w1, r1))):
                    at = side * slab
                    out[:rank_rows, at : at + slab] = run(raised, spot)
                    scaled = run(weight, spot).astype(wide) * gain_ref[...]
                    out[rank_rows:, at : at + slab] = scaled.astype(low)

    return pl.pallas_call(
        body,
        out_shape=jax.ShapeDtypeStruct((rank_rows + rows, 2 * slab), low),
        compiler_params=pltpu.CompilerParams(vmem_limit_bytes=48 * 2**20),
    )(gains, *weights, *raises)


def place_columns(pieces, gains, n_f, n_seq, rank_rows, ff, slab):
    rows = pieces.shape[1] - rank_rows
    cut = ff // (n_f * n_seq)
    chips = n_seq // CORES

    def body(gain_ref, x, w0, w1, r0, r1):
        me = lax.axis_index("seq")
        y, core = me // CORES, lax.rem(me, CORES)

        def spot_of(spot):
            ahead = lax.rem(spot // CORES - y + chips, chips)
            return ahead * CORES + lax.rem(spot % CORES + core, CORES)

        def fill(out, first, count, at, gain):
            whole = [x[spot_of(spot), first : first + count, at : at + slab] for spot in range(n_seq)]
            runs = [
                whole[spot][:, f * cut : (f + 1) * cut] for f in range(n_f) for spot in range(n_seq)
            ]
            result = jnp.concatenate(runs, axis=1).astype(wide)
            out[...] = result if gain is None else result * gain

        for side, (weight, raised) in enumerate(((w0, r0), (w1, r1))):
            fill(raised, 0, rank_rows, side * slab, None)
            fill(weight, rank_rows, rows, side * slab, gain_ref[...])

    return pl.pallas_call(
        body,
        out_shape=(jax.ShapeDtypeStruct((rows, ff), wide),) * 2
        + (jax.ShapeDtypeStruct((rank_rows, ff), wide),) * 2,
        compiler_params=pltpu.CompilerParams(vmem_limit_bytes=56 * 2**20),
    )(gains, pieces)


def rope(values, cosine, sine):
    half = values.shape[-1] // 2
    first, second = values[..., :half], values[..., half:]
    cosine, sine = cosine[:, None, :], sine[:, None, :]
    return jnp.concatenate([first * cosine - second * sine, second * cosine + first * sine], axis=-1)


def gelu_parts(gate):
    scale = (2.0 / jnp.pi) ** 0.5
    cube = 0.044715
    curve = jnp.tanh(scale * (gate + cube * gate * gate * gate))
    value = 0.5 * gate * (1.0 + curve)
    slope = 0.5 * (1.0 + curve) + 0.5 * gate * (1.0 - curve * curve) * scale * (
        1.0 + 3.0 * cube * gate * gate
    )
    return value, slope


def shards(
    inputs,
    cotangent,
    segments,
    exits,
    confidence,
    attn_gain,
    q_weight,
    k_weight,
    v_weight,
    o_weight,
    q_down,
    q_up,
    k_down,
    k_up,
    v_down,
    v_up,
    o_down,
    o_up,
    mlp_gain,
    gate_weight,
    up_weight,
    down_weight,
    gate_down,
    gate_up,
    up_down,
    up_up,
    down_down,
    down_up,
):
    n_seq, n_f = lax.axis_size("seq"), lax.axis_size("fsdp")
    me = lax.axis_index("seq")
    ring = Ring(n_f, n_seq // CORES)
    group = Group(n_seq)
    rows, length, width = inputs.shape
    tokens = rows * length
    rank = q_down.shape[1]
    hq = q_weight.shape[1]
    ff = gate_weight.shape[1]
    own_rows = q_weight.shape[0]
    rank_rows = q_up.shape[0]
    o_rows = o_weight.shape[0]
    cut = ff // (n_f * n_seq)
    slab = -(-n_f * cut // 128) * 128
    scale = HD ** (-0.5)

    gain1 = attn_gain.astype(wide)[:, None]
    gain2 = mlp_gain.astype(wide)[:, None]

    def rows_of(array):
        part = array.shape[0] // n_seq
        return lax.dynamic_slice_in_dim(array, me * part, part, 0)

    def side_by_side(parts):
        total = sum(part.shape[1] for part in parts)
        gap = -total % (128 * n_seq)
        if gap:
            parts = [*parts, jnp.zeros((parts[0].shape[0], gap), low)]
        return jnp.concatenate(parts, axis=1)

    side1 = side_by_side(
        [
            (part.astype(wide) * gain1).astype(low)
            for part in (q_weight, k_weight, v_weight, q_down, k_down, v_down)
        ]
        + [(part.astype(wide) * gain2).astype(low) for part in (gate_down, up_down)]
    )
    ups = side_by_side([q_up, k_up, v_up, o_up, down_up])
    side_o = side_by_side([o_weight, o_down])

    def keep_slab(buffers, owner, block):
        raised, gates, raises = buffers
        put = lax.dynamic_update_index_in_dim
        return (
            put(raised, block[:rank_rows], owner, 0),
            put(gates, block[rank_rows:, :slab], owner, 0),
            put(raises, block[rank_rows:, slab:], owner, 0),
        )

    def keep_down(buffers, owner, block):
        return (lax.dynamic_update_index_in_dim(buffers[0], block, owner, 0),)

    slabs = Gathering(
        ring,
        cut_columns((gate_weight, up_weight), (gate_up, up_up), gain2, n_f, n_seq, slab),
        (
            jnp.zeros((n_f, rank_rows, 2 * slab), low),
            jnp.zeros((n_f, own_rows, slab), low),
            jnp.zeros((n_f, own_rows, slab), low),
        ),
        keep_slab,
    )
    d_lower = rows_of(down_down)
    downs = Gathering(
        ring,
        jnp.concatenate([rows_of(down_weight), d_lower], axis=1),
        (jnp.zeros((n_f, cut, width + rank), low),),
        keep_down,
    )

    depth_ids = jnp.arange(DEPTHS, dtype=jnp.int32)
    matches = (exits.reshape(tokens)[:, None] == depth_ids[None, :]).astype(wide)
    counted = Summing(
        jnp.concatenate(
            [jnp.sum(matches, axis=0), jnp.sum(matches * confidence.reshape(tokens)[:, None], axis=0)]
        ),
        ("seq", "fsdp"),
    )
    resid = inputs.reshape(tokens, width).astype(wide)
    active = (exits.reshape(tokens) >= LOOP).astype(wide)[:, None]
    cot = cotangent.reshape(tokens, width).astype(wide)
    g_mlp = (active * cot).astype(low)
    places = me * length + jnp.arange(length, dtype=jnp.int32)
    frequency = rope_base ** (-2.0 * jnp.arange(HD // 2, dtype=wide) / HD)
    angles = jnp.tile(places, rows).astype(wide)[:, None] * frequency[None, :]
    cosine, sine = jnp.cos(angles), jnp.sin(angles)
    r1 = lax.rsqrt(jnp.mean(resid * resid, axis=-1, keepdims=True) + epsilon)
    unit1 = (resid * r1).astype(low)

    slabs.advance()
    downs.advance()
    seg_pieces = group.over(segments.astype(low))
    whole = gather_whole((side1, ups, side_o), 0, n_f, n_seq)
    whole, seg_pieces, unit1, cosine, sine = tie(
        (slabs, downs), (whole, seg_pieces, unit1, cosine, sine)
    )
    side1, ups, side_o = (part.reshape(-1, part.shape[2]) for part in whole)
    kv = HD
    lin = hq + 2 * kv
    qkv_side = side1[:, : lin + 3 * rank]
    gate_adapter = side1[:, lin + 3 * rank : lin + 4 * rank]
    up_adapter = side1[:, lin + 4 * rank : lin + 5 * rank]
    side_o = side_o[:, : width + rank]
    q_raise, k_raise, v_raise = ups[:, :hq], ups[:, hq : hq + kv], ups[:, hq + kv : lin]
    o_raise, d_raise = ups[:, lin : lin + width], ups[:, lin + width : lin + 2 * width]

    slabs.advance()
    seg_pieces = group.across(seg_pieces)
    projected = mul(unit1, qkv_side)
    inner = projected[:, lin:].astype(low)
    q_inner, k_inner, v_inner = inner[:, :rank], inner[:, rank : 2 * rank], inner[:, 2 * rank :]
    q_lin = projected[:, :hq] + mul(q_inner, q_raise)
    k_lin = projected[:, hq : hq + kv] + mul(k_inner, k_raise)
    v_lin = projected[:, hq + kv : lin] + mul(v_inner, v_raise)
    queries = rope(q_lin.reshape(tokens, H, HD), cosine, sine).astype(low)
    queries = queries.reshape(rows, length, H, HD).transpose(0, 2, 1, 3)
    queries = queries.reshape(rows, H * length, HD)
    keys = rope(k_lin.reshape(tokens, 1, HD), cosine, sine).astype(low).reshape(tokens, HD)
    values = v_lin.astype(low)
    both = gather_group(jnp.concatenate([keys, values], axis=-1), 2, n_seq)
    both, queries, seg_pieces, inner = tie((slabs,), (both, queries, seg_pieces, inner))
    q_inner, k_inner, v_inner = inner[:, :rank], inner[:, rank : 2 * rank], inner[:, 2 * rank :]

    slabs.advance()
    g_mlp = group.over(g_mlp)
    both = both.reshape(n_seq, rows, length, 2 * HD)
    both = both.transpose(1, 0, 2, 3).reshape(rows, n_seq * length, 2 * HD)
    keys, values = both[..., :HD], both[..., HD:]
    key_seg = jnp.concatenate(seg_pieces, axis=1).astype(jnp.int32)
    key_place = jnp.concatenate(
        [
            group.index(k, c) * length + jnp.arange(length, dtype=jnp.int32)
            for k, c in group.order
        ]
    )
    query_seg, query_place = jnp.tile(segments, (1, H)), jnp.tile(places, H)
    allowed = (query_seg[:, :, None] == key_seg[:, None, :]) & (
        key_place[None, None, :] <= query_place[None, :, None]
    )
    scores = (
        jnp.einsum("sqd,skd->sqk", queries, keys, preferred_element_type=wide) * scale
    )
    scores = jnp.where(allowed, scores, -1e30)
    top = jnp.max(scores, axis=-1, keepdims=True)
    weights = jnp.exp(scores - top)
    totals = jnp.sum(weights, axis=-1, keepdims=True)
    attn = (
        jnp.einsum("sqk,skd->sqd", weights.astype(low), values, preferred_element_type=wide)
        / totals
    )
    log_total = top + jnp.log(totals)

    def to_tokens(rows_heads):
        view = rows_heads.reshape(rows, H, length, HD).transpose(0, 2, 1, 3)
        return view.reshape(tokens, hq)

    def to_heads(flat):
        view = flat.reshape(rows, length, H, HD).transpose(0, 2, 1, 3)
        return view.reshape(rows, H * length, HD)

    attn_low = to_tokens(attn.astype(low))
    projected = mul(attn_low, side_o)
    o_inner = projected[:, width:].astype(low)
    mid = resid + active * (projected[:, :width] + mul(o_inner, o_raise))
    r2 = lax.rsqrt(jnp.mean(mid * mid, axis=-1, keepdims=True) + epsilon)
    unit2 = (mid * r2).astype(low)
    unit2, mid, r2, g_mlp, attn, attn_low, o_inner, log_total = tie(
        (slabs, counted), (unit2, mid, r2, g_mlp, attn, attn_low, o_inner, log_total)
    )

    slabs.advance()
    downs.advance()
    counted.advance()
    g_mlp = group.across(g_mlp)
    unit2 = gather_group(unit2, 3, n_seq).reshape(-1, width)
    unit2, g_mlp = tie((slabs, downs, counted), (unit2, g_mlp))
    g_mlp = jnp.concatenate(g_mlp, axis=0)

    downs.advance()
    counted.advance()
    raised, gate_full, up_full = slabs.done()
    raised = raised.reshape(rank, 2 * slab)
    g_raise, u_raise = raised[:, :slab], raised[:, slab:]
    gate_full = (gate_full.reshape(width, slab).astype(wide) + mul(gate_adapter, g_raise)).astype(low)
    up_full = (up_full.reshape(width, slab).astype(wide) + mul(up_adapter, u_raise)).astype(low)
    gate = mul(unit2, gate_full).astype(low)
    up = mul(unit2, up_full).astype(low)
    value, slope = gelu_parts(gate.astype(wide))
    hidden = (value * up.astype(wide)).astype(low)[:, : n_f * cut]
    hidden, gate, up = tie((downs, counted), (hidden, gate, up))

    downs.advance()
    counted.advance()
    g_down = t_mul(hidden, g_mlp).astype(low)
    g_down, g_mlp = tie((downs, counted), (g_down, g_mlp))

    def ring_block(array, size):
        return lambda owner: lax.dynamic_slice_in_dim(array, owner * size, size, 0).astype(wide)

    down_sums = Scattering(ring, ring_block(g_down, cut))
    down_sums.advance()
    counted.advance()
    (down_raw,) = downs.done()
    down_raw = down_raw.reshape(n_f * cut, width + rank)
    down_full = (down_raw[:, :width].astype(wide) + mul(down_raw[:, width:], d_raise)).astype(low)
    padded = jnp.pad(down_full, ((0, slab - n_f * cut), (0, 0)))
    g_hidden = mul_t(g_mlp, padded)
    value, slope = gelu_parts(gate.astype(wide))
    g_gate = (g_hidden * up.astype(wide) * slope).astype(low)
    g_up = (g_hidden * value).astype(low)
    g_gate, g_up, down_full = tie((down_sums, counted), (g_gate, g_up, down_full))

    down_sums.advance()
    counted.advance()
    branch = mul(hidden, down_full).astype(low)
    branch, g_gate, g_up = tie((down_sums, counted), (branch, g_gate, g_up))

    down_sums.advance()
    terms = [branch[i * tokens : (i + 1) * tokens] for i in range(n_seq)]
    near = group.cross(terms)
    gg = t_mul(unit2, g_gate).astype(low)
    gu = t_mul(unit2, g_up).astype(low)
    gg_raise = t_mul(gate_adapter, gg).astype(low)
    gu_raise = t_mul(up_adapter, gu).astype(low)
    near, gg, gu, gg_raise, gu_raise, g_gate, g_up = tie(
        (down_sums,), (near, gg, gu, gg_raise, gu_raise, g_gate, g_up)
    )

    def slab_block(owner):
        return jnp.concatenate(
            [
                jnp.concatenate(
                    [
                        lax.dynamic_slice_in_dim(part, owner * size, size, 0)
                        for part in (raised, weight)
                        for size in (part.shape[0] // n_f,)
                    ],
                    axis=0,
                )
                for raised, weight in ((gg_raise, gg), (gu_raise, gu))
            ],
            axis=1,
        ).astype(wide)

    slab_sums = Scattering(ring, slab_block)
    slab_sums.advance()
    down_sums.advance()
    sums = [
        terms[k * CORES].astype(wide) + near[k].astype(wide) for k in range(n_seq // CORES)
    ]
    far = group.send(sums)
    e2 = (mul_t(g_gate, gate_full) + mul_t(g_up, up_full)).astype(low)
    e2, far, own_branch = tie((slab_sums, down_sums), (e2, far, sums[0]))
    for block in far:
        own_branch = own_branch + block.astype(wide)
    outputs = (mid + active * own_branch).astype(low).reshape(rows, length, width)

    slab_sums.advance()
    e2 = scatter_group(e2.reshape(n_seq, tokens, width), 5)
    g_down = down_sums.done().astype(low)
    down_rows = jnp.concatenate([g_down, mul_t(g_down, d_raise).astype(low)], axis=1)
    gd_raise = t_mul(d_lower, g_down).astype(low)
    e2, down_rows, gd_raise = tie((slab_sums,), (e2, down_rows, gd_raise))

    slab_sums.advance()
    down_rows = group.over(down_rows)
    g_mid = cot + r2 * e2 - mid * (r2 * r2 * r2 * jnp.mean(e2 * mid, axis=-1, keepdims=True))
    g_branch = (active * g_mid).astype(low)
    g_inner = mul_t(g_branch, o_raise).astype(low)
    g_attn = mul_t(jnp.concatenate([g_branch, g_inner], axis=1), side_o).astype(low)
    g_o = t_mul(attn_low, g_branch).astype(low)
    go_raise = t_mul(o_inner, g_branch).astype(low)
    o_pack = jnp.concatenate(
        [
            g_o.reshape(n_f, o_rows, width),
            go_raise.reshape(n_f, rank_rows, width),
            gd_raise.reshape(n_f, rank_rows, width),
        ],
        axis=1,
    )
    g_heads = to_heads(g_attn)
    dots = jnp.sum(g_heads.astype(wide) * attn, axis=-1, keepdims=True)
    scores = (
        jnp.einsum("sqd,skd->sqk", queries, keys, preferred_element_type=wide) * scale
    )
    probs = jnp.where(allowed, jnp.exp(scores - log_total), 0.0)
    d_probs = jnp.einsum("sqd,skd->sqk", g_heads, values, preferred_element_type=wide)
    d_scores = (probs * (d_probs - dots)).astype(low)
    d_query = jnp.einsum("sqk,skd->sqd", d_scores, keys, preferred_element_type=wide) * scale
    d_key = jnp.einsum("sqk,sqd->skd", d_scores, queries, preferred_element_type=wide) * scale
    d_value = jnp.einsum("sqk,sqd->skd", probs.astype(low), g_heads, preferred_element_type=wide)
    d_both = jnp.concatenate([d_key, d_value], axis=-1)
    d_both = d_both.astype(low).reshape(rows, n_seq, length, 2 * HD)
    d_both = scatter_group(d_both.transpose(1, 0, 2, 3).reshape(n_seq, tokens, 2 * HD), 8)
    d_both, d_query, o_pack, g_mid, down_rows = tie(
        (slab_sums,), (d_both, d_query, o_pack, g_mid, down_rows)
    )

    slab_sums.advance()
    down_rows = group.across(down_rows)
    g_q = rope(to_tokens(d_query).reshape(tokens, H, HD), cosine, -sine)
    g_q = g_q.reshape(tokens, hq).astype(low)
    g_k = rope(d_both[:, None, :HD], cosine, -sine).reshape(tokens, HD).astype(low)
    g_v = d_both[:, HD:].astype(low)
    gi_q = mul_t(g_q, q_raise).astype(low)
    gi_k = mul_t(g_k, k_raise).astype(low)
    gi_v = mul_t(g_v, v_raise).astype(low)
    g_lin = jnp.concatenate([g_q, g_k, g_v], axis=1)
    e1 = mul_t(jnp.concatenate([g_lin, gi_q, gi_k, gi_v], axis=1), qkv_side)
    input_grad = g_mid + r1 * e1 - resid * (
        r1 * r1 * r1 * jnp.mean(e1 * resid, axis=-1, keepdims=True)
    )
    input_grad = input_grad.astype(low).reshape(rows, length, width)
    g_qkv = t_mul(unit1, g_lin).astype(low)
    gr_qkv = jnp.concatenate(
        [t_mul(q_inner, g_q), t_mul(k_inner, g_k), t_mul(v_inner, g_v)], axis=1
    ).astype(low)
    qkv_pack = jnp.concatenate(
        [g_qkv.reshape(n_f, own_rows, lin), gr_qkv.reshape(n_f, rank_rows, lin)], axis=1
    )
    packs = scatter_whole((qkv_pack, o_pack), 6, n_seq)
    packs, down_rows = tie((slab_sums,), (packs, down_rows))
    qkv_pack, o_pack = (pack.astype(wide) for pack in packs)
    down_rows = group.laid(down_rows, 0, wide)
    grad_down_weight, grad_down_down = down_rows[:, :width], down_rows[:, width:]

    grad_o_weight = o_pack[:o_rows]
    grad_o_up = o_pack[o_rows : o_rows + rank_rows]
    grad_down_up = o_pack[o_rows + rank_rows :]
    grad_o_down = mul_t(packs[1][:o_rows], o_raise)
    unit_grad = qkv_pack[:own_rows]
    grad_lin = unit_grad * gain1
    grad_q_weight, grad_k_weight, grad_v_weight = (
        grad_lin[:, :hq],
        grad_lin[:, hq : hq + kv],
        grad_lin[:, hq + kv :],
    )
    grad_q_up, grad_k_up, grad_v_up = (
        qkv_pack[own_rows:, :hq],
        qkv_pack[own_rows:, hq : hq + kv],
        qkv_pack[own_rows:, hq + kv :],
    )
    grad_q_down = mul_t(grad_q_weight.astype(low), q_raise)
    grad_k_down = mul_t(grad_k_weight.astype(low), k_raise)
    grad_v_down = mul_t(grad_v_weight.astype(low), v_raise)
    own_lin = jnp.concatenate(
        [
            q_weight.astype(wide) + mul(q_down, q_raise),
            k_weight.astype(wide) + mul(k_down, k_raise),
            v_weight.astype(wide) + mul(v_down, v_raise),
        ],
        axis=1,
    )
    grad_attn_gain = jnp.sum(unit_grad * own_lin, axis=1)

    g_slab = slab_sums.done()
    unit_grad = g_slab[rank_rows:]
    own_full = [
        lax.dynamic_slice_in_dim(full, lax.axis_index("fsdp") * own_rows, own_rows, 0)
        for full in (gate_full, up_full)
    ]
    merged = jnp.concatenate(own_full, axis=1).astype(wide)
    weight_grad = (unit_grad * gain2).astype(low)
    mlp_small = Summing(
        jnp.concatenate(
            [
                mul_t(weight_grad[:, :slab], g_raise),
                mul_t(weight_grad[:, slab:], u_raise),
                jnp.broadcast_to(
                    jnp.sum(unit_grad * merged, axis=1, keepdims=True) / gain2, (own_rows, 128)
                ),
            ],
            axis=1,
        ),
        ("seq",),
    )
    slab_pieces = gather_group(g_slab.astype(low), 7, n_seq)
    mlp_small = mlp_small.done()
    grad_gate_down, grad_up_down = mlp_small[:, :rank], mlp_small[:, rank : 2 * rank]
    grad_mlp_gain = mlp_small[:, 2 * rank]
    grad_gate_weight, grad_up_weight, grad_gate_up, grad_up_up = place_columns(
        slab_pieces, gain2, n_f, n_seq, rank_rows, ff, slab
    )

    counted = counted.done()
    mean_confidence = counted[DEPTHS:] / counted[:DEPTHS]
    return (
        outputs,
        input_grad,
        grad_attn_gain,
        grad_q_weight,
        grad_k_weight,
        grad_v_weight,
        grad_o_weight,
        grad_q_down,
        grad_q_up,
        grad_k_down,
        grad_k_up,
        grad_v_down,
        grad_v_up,
        grad_o_down,
        grad_o_up,
        grad_mlp_gain,
        grad_gate_weight,
        grad_up_weight,
        grad_down_weight,
        grad_gate_down,
        grad_gate_up,
        grad_up_down,
        grad_up_up,
        grad_down_down,
        grad_down_up,
        counted[:DEPTHS].astype(jnp.int32),
        mean_confidence,
    )


def solution(mesh):
    tokens3 = P("fsdp", "seq", None)
    tokens2 = P("fsdp", "seq")
    vector, matrix = P("fsdp"), P("fsdp", None)
    in_specs = (tokens3,) * 2 + (tokens2,) * 3 + (vector,) + (matrix,) * 12 + (vector,) + (matrix,) * 9
    out_specs = (
        (tokens3,) * 2 + (vector,) + (matrix,) * 12 + (vector,) + (matrix,) * 9 + (P(), P())
    )
    return jax.shard_map(shards, mesh=mesh, in_specs=in_specs, out_specs=out_specs, check_vma=False)
```

```python
import jax
import jax.numpy as jnp
from jax import lax
from jax.experimental import pallas as pl
from jax.experimental.pallas import tpu as pltpu
from jax.sharding import PartitionSpec as P

H = 4
HD = 256
DEPTHS = 3
LOOP = 1
CORES = 2

epsilon = 1e-06
rope_base = 10000.0
low = jnp.bfloat16
wide = jnp.float32


def mul(left, right):
    return jnp.dot(left, right, preferred_element_type=wide)


def mul_t(left, right):
    return lax.dot_general(left, right, (((1,), (1,)), ((), ())), preferred_element_type=wide)


def t_mul(left, right):
    return lax.dot_general(left, right, (((0,), (0,)), ((), ())), preferred_element_type=wide)


def ring_order(count, width):
    if width < 2 or count % width or (count // width) % 2:
        return list(range(count))
    depth = count // width
    walk = [0]
    for z in range(depth):
        columns = range(1, width) if z % 2 == 0 else range(width - 1, 0, -1)
        walk += [z * width + x for x in columns]
    walk += [z * width for z in range(depth - 1, 0, -1)]
    return walk


MESH = pl.DeviceIdType.MESH
ANY = pl.BlockSpec(memory_space=pl.ANY)
VMEM = pl.BlockSpec(memory_space=pltpu.VMEM)


def pick(index, table):
    result = jnp.int32(table[0])
    for spot, value in enumerate(table):
        if spot:
            result = jnp.where(index == spot, jnp.int32(value), result)
    return result


class Places:
    def __init__(self, n_f, n_seq):
        self.n_f, self.n_seq, self.chips = n_f, n_seq, n_seq // CORES
        self.walk = ring_order(n_f, n_seq // CORES)
        spots = [0] * n_f
        for spot, device in enumerate(self.walk):
            spots[device] = spot
        self.f, self.me = lax.axis_index("fsdp"), lax.axis_index("seq")
        self.spot = pick(self.f, spots)
        self.y, self.core = self.me // CORES, lax.rem(self.me, CORES)

    def at(self, offset):
        return pick(lax.rem(self.spot + offset + self.n_f, self.n_f), self.walk)

    def seq(self, k, c):
        return lax.rem(self.y + k + self.chips, self.chips) * CORES + lax.rem(
            self.core + c, CORES
        )

    def greet(self, ring):
        barrier = pltpu.get_barrier_semaphore()
        friends = [{"seq": self.seq(0, 1)}]
        friends += [{"seq": self.seq(k, 0)} for k in range(1, self.chips)]
        if ring:
            friends += [{"fsdp": self.at(1)}, {"fsdp": self.at(-1)}]
        for friend in friends:
            pl.semaphore_signal(barrier, inc=1, device_id=friend, device_id_type=MESH)
        pl.semaphore_wait(barrier, len(friends))


def remote(source, target, send, receive, device):
    return pltpu.make_async_remote_copy(
        src_ref=source,
        dst_ref=target,
        send_sem=send,
        recv_sem=receive,
        device_id=device,
        device_id_type=MESH,
    )


def brief(us):
    return pl.CostEstimate(
        flops=int(us * 1.0e9), bytes_accessed=int(us * 1.0e6), transcendentals=0
    )


def params(number):
    return pltpu.CompilerParams(
        collective_id=number, has_side_effects=True, vmem_limit_bytes=56 * 2**20
    )


def ring_steps(n_f):
    order = []
    for step in range(1, n_f // 2 + 1):
        order.append((step, 1))
        if step <= (n_f - 1) // 2:
            order.append((step, -1))
    return order


def pack_small(gain1, gain2, attention, lower, raises, raises2, outward, n_seq):
    groups = [(attention, gain1), (raises, None), (outward, None), (raises2, None), (lower, gain2)]
    shares = (CORES, CORES, n_seq, n_seq, n_seq)

    def body(*refs):
        refs = list(refs)
        for (parts, gain), out in zip(groups, refs[-len(groups) :], strict=True):
            factor = None if gain is None else refs.pop(0)[...]
            at = 0
            for part in parts:
                block = refs.pop(0)[...]
                if factor is not None:
                    block = (block.astype(wide) * factor).astype(low)
                out[:, at : at + part.shape[1]] = block
                at += part.shape[1]
            if at < out.shape[1]:
                out[:, at:] = jnp.zeros((out.shape[0], out.shape[1] - at), low)

    sizes = []
    for (parts, _), ways in zip(groups, shares, strict=True):
        total = sum(part.shape[1] for part in parts)
        sizes.append((parts[0].shape[0], total + -total % (128 * ways)))
    operands = []
    for parts, gain in groups:
        operands += ([] if gain is None else [gain]) + list(parts)
    return pl.pallas_call(
        body,
        out_shape=tuple(jax.ShapeDtypeStruct(size, low) for size in sizes),
        compiler_params=pltpu.CompilerParams(vmem_limit_bytes=48 * 2**20),
    )(*operands)


def gather_whole(blocks, spread, number, n_f, n_seq):
    count = len(blocks)
    chips = n_seq // CORES
    steps = ring_steps(n_f)
    order = [j for j in range(count) if spread[j]] + [j for j in range(count) if not spread[j]]

    def body(*refs):
        ins, outs = refs[:count], refs[count : 2 * count]
        local, ring_s, ring_r, y_s, y_r, core_s, core_r = refs[2 * count :]
        here = Places(n_f, n_seq)
        started = []

        def share(j, k, c):
            spot = here.seq(k, c) if spread[j] else lax.rem(here.core + c, CORES)
            width = ins[j].shape[-1] // (n_seq if spread[j] else CORES)
            return (slice(None), pl.ds(pl.multiple_of(spot * width, 128), width))

        def far(j):
            return range(1, chips if spread[j] else 1)

        copies = []
        for j in range(count):
            copy = pltpu.make_async_copy(ins[j], outs[j].at[here.f], local.at[j])
            copy.start()
            copies.append(copy)
        here.greet(True)

        def flip(j):
            return 1 if j == 0 else -1

        def forward(j, step, way):
            owner = here.at(-flip(j) * way * (step - 1))
            mine = share(j, 0, 0)
            source = ins[j].at[mine] if step == 1 else outs[j].at[(owner, *mine)]
            at = steps.index((step, way))
            copy = remote(
                source,
                outs[j].at[(owner, *mine)],
                ring_s.at[j, at],
                ring_r.at[j, at],
                {"fsdp": here.at(flip(j) * way)},
            )
            copy.start()
            started.append(copy)

        def landed(j, step, way):
            owner = here.at(-flip(j) * way * step)
            at = steps.index((step, way))
            block = outs[j].at[(owner, *share(j, 0, 0))]
            remote(block, block, ring_s.at[j, at], ring_r.at[j, at], {"fsdp": here.at(flip(j) * way)}).wait_recv()
            return owner

        def to_core(j, at, k, owner):
            block = outs[j].at[(owner, *share(j, k, 0))]
            copy = remote(
                block, block, core_s.at[j, at, k], core_r.at[j, at, k], {"seq": here.seq(0, 1)}
            )
            copy.start()
            started.append(copy)

        for j in order:
            for way in (1, -1):
                forward(j, 1, way)
        for at, (step, way) in enumerate(steps):
            for j in order:
                owner = landed(j, step, way)
                if (step + 1, way) in steps:
                    forward(j, step + 1, way)
                block = outs[j].at[(owner, *share(j, 0, 0))]
                for k in far(j):
                    copy = remote(
                        block, block, y_s.at[j, at, k], y_r.at[j, at, k], {"seq": here.seq(-k, 0)}
                    )
                    copy.start()
                    started.append(copy)
                to_core(j, at, 0, owner)
        for at, (step, way) in enumerate(steps):
            for j in order:
                owner = here.at(-flip(j) * way * step)
                for k in far(j):
                    block = outs[j].at[(owner, *share(j, k, 0))]
                    remote(
                        block, block, y_s.at[j, at, k], y_r.at[j, at, k], {"seq": here.seq(-k, 0)}
                    ).wait_recv()
                    to_core(j, at, k, owner)
        for at, (step, way) in enumerate(steps):
            for j in order:
                owner = here.at(-flip(j) * way * step)
                for k in [0, *far(j)]:
                    block = outs[j].at[(owner, *share(j, k, 1))]
                    remote(
                        block, block, core_s.at[j, at, k], core_r.at[j, at, k], {"seq": here.seq(0, 1)}
                    ).wait_recv()
        for copy in started:
            copy.wait_send()
        for copy in copies:
            copy.wait()

    sems = pltpu.SemaphoreType.DMA
    return pl.pallas_call(
        body,
        out_shape=tuple(jax.ShapeDtypeStruct((n_f,) + b.shape, b.dtype) for b in blocks),
        in_specs=[ANY] * count,
        out_specs=(ANY,) * count,
        scratch_shapes=[sems((count,))]
        + [sems((count, len(steps)))] * 2
        + [sems((count, len(steps), chips))] * 4,
        compiler_params=params(number),
    )(*blocks)


def gather_group(block, number, n_seq):
    rows = block.shape[0]
    chips = n_seq // CORES
    parts = 4 if rows % 64 == 0 else 1
    size = rows // parts

    def body(x, out, local, y_s, y_r, core_s, core_r):
        here = Places(1, n_seq)
        own = pltpu.make_async_copy(x, out.at[0], local)
        own.start()
        here.greet(False)
        started = []

        def to_core(source, k, part):
            cut = pl.ds(part * size, size)
            copy = remote(
                source.at[cut],
                out.at[k * CORES + 1, cut],
                core_s.at[k, part],
                core_r.at[k, part],
                {"seq": here.seq(0, 1)},
            )
            copy.start()
            started.append(copy)

        def over(k, part):
            cut = pl.ds(part * size, size)
            return remote(
                x.at[cut],
                out.at[k * CORES, cut],
                y_s.at[k, part],
                y_r.at[k, part],
                {"seq": here.seq(-k, 0)},
            )

        for part in range(parts):
            for k in range(1, chips):
                copy = over(k, part)
                copy.start()
                started.append(copy)
            to_core(x, 0, part)
        for part in range(parts):
            for k in range(1, chips):
                over(k, part).wait_recv()
                to_core(out.at[k * CORES], k, part)
        for part in range(parts):
            for k in range(chips):
                cut = pl.ds(part * size, size)
                block = out.at[k * CORES + 1, cut]
                remote(
                    block, block, core_s.at[k, part], core_r.at[k, part], {"seq": here.seq(0, 1)}
                ).wait_recv()
        for copy in started:
            copy.wait_send()
        own.wait()

    sems = pltpu.SemaphoreType.DMA
    return pl.pallas_call(
        body,
        out_shape=jax.ShapeDtypeStruct((n_seq,) + block.shape, block.dtype),
        in_specs=[ANY],
        out_specs=ANY,
        scratch_shapes=[sems(())] + [sems((chips, parts))] * 4,
        compiler_params=params(number),
    )(block)


def scatter_group(terms, number):
    n_seq, rows, columns = terms.shape
    chips = n_seq // CORES
    parts = 4 if rows % 64 == 0 else 1
    size = rows // parts

    def body(x, out, near, sums, far, y_s, y_r, core_s, core_r):
        here = Places(1, n_seq)
        here.greet(False)
        started = []

        def cross(k, part):
            cut = pl.ds(part * size, size)
            return remote(
                x.at[k * CORES + 1, cut],
                near.at[k, cut],
                core_s.at[k, part],
                core_r.at[k, part],
                {"seq": here.seq(0, 1)},
            )

        def over(k, part):
            cut = pl.ds(part * size, size)
            return remote(
                sums.at[k, cut],
                far.at[k, cut],
                y_s.at[k, part],
                y_r.at[k, part],
                {"seq": here.seq(k, 0)},
            )

        for k in [*range(1, chips), 0]:
            for part in range(parts):
                copy = cross(k, part)
                copy.start()
                started.append(copy)
        for k in range(1, chips):
            for part in range(parts):
                cut = pl.ds(part * size, size)
                cross(k, part).wait_recv()
                total = x[k * CORES, cut, :].astype(wide) + near[k, cut, :].astype(wide)
                sums[k, cut, :] = total.astype(low)
                copy = over(k, part)
                copy.start()
                started.append(copy)
        for part in range(parts):
            cut = pl.ds(part * size, size)
            cross(0, part).wait_recv()
            out[cut, :] = x[0, cut, :].astype(wide) + near[0, cut, :].astype(wide)
        for part in range(parts):
            cut = pl.ds(part * size, size)
            for k in range(1, chips):
                over(k, part).wait_recv()
                out[cut, :] = out[cut, :] + far[k, cut, :].astype(wide)
        for copy in started:
            copy.wait_send()

    sems = pltpu.SemaphoreType.DMA
    buffer = pltpu.VMEM((chips, rows, columns), low)
    return pl.pallas_call(
        body,
        out_shape=jax.ShapeDtypeStruct((rows, columns), wide),
        in_specs=[VMEM],
        out_specs=VMEM,
        scratch_shapes=[buffer] * 3 + [sems((chips, parts))] * 4,
        compiler_params=params(number),
    )(terms)


def scatter_whole(packs, block, small, number, n_seq):
    wanted = [pack.shape[2] for pack in packs]
    gaps = [-count % (128 * CORES) for count in wanted]
    packs = [
        jnp.pad(pack, ((0, 0), (0, 0), (0, gap))) if gap else pack
        for pack, gap in zip(packs, gaps, strict=True)
    ]
    n_f, count = packs[0].shape[0], len(packs)
    chips = n_seq // CORES
    widths = [pack.shape[2] // CORES for pack in packs]
    steps = ring_steps(n_f)
    offsets = [way * step for step, way in reversed(steps)] + [0]
    last = {way: max(step for step, w in steps if w == way) for way in (1, -1)}

    def body(*refs):
        refs = list(refs)

        def take(n):
            taken, refs[:] = refs[:n], refs[n:]
            return taken

        xs = take(count)
        block_in, small_in = take(2)
        outs = take(count)
        block_out, small_out = take(2)
        nears, terms, moves, parts = (take(count) for _ in range(4))
        (smalls,) = take(1)
        core_s, core_r, ring_s, ring_r, y_s, y_r, side_s, side_r = take(8)
        local, far_s, far_r, near_s, near_r = take(5)
        here = Places(n_f, n_seq)
        own = pltpu.make_async_copy(block_in, block_out.at[0], local)
        own.start()
        smalls[here.me] = small_in[...]
        here.greet(True)
        started = []

        def flip(j):
            return 1 if j == 0 else -1

        def go(copy):
            copy.start()
            started.append(copy)

        def share(j, spot):
            return pl.ds(pl.multiple_of(spot * widths[j], 128), widths[j])

        other = lax.rem(here.core + 1, CORES)

        def cross(j, i):
            return remote(
                xs[j].at[here.at(flip(j) * offsets[i]), :, share(j, other)],
                nears[j].at[i],
                core_s.at[j, i],
                core_r.at[j, i],
                {"seq": here.seq(0, 1)},
            )

        def hop(j, step, way):
            at = steps.index((step, way))
            return remote(
                terms[j].at[at],
                moves[j].at[at],
                ring_s.at[j, at],
                ring_r.at[j, at],
                {"fsdp": here.at(flip(j) * way)},
            )

        def far_block(k):
            return remote(
                block_in, block_out.at[k * CORES], far_s.at[k], far_r.at[k], {"seq": here.seq(-k, 0)}
            )

        def near_block(k):
            source = block_in if k == 0 else block_out.at[k * CORES]
            return remote(
                source,
                block_out.at[k * CORES + 1],
                near_s.at[k],
                near_r.at[k],
                {"seq": here.seq(0, 1)},
            )

        def far_small(k, spot):
            slot = smalls.at[spot]
            return remote(
                slot, slot, far_s.at[chips + k], far_r.at[chips + k], {"seq": here.seq(-k, 0)}
            )

        def near_small(k, spot):
            slot = smalls.at[spot]
            return remote(
                slot, slot, near_s.at[chips + k], near_r.at[chips + k], {"seq": here.seq(0, 1)}
            )

        for k in range(1, chips):
            go(far_small(k, here.me))
            go(far_block(k))
        for i in range(n_f):
            for j in range(count):
                go(cross(j, i))
        go(near_small(0, here.me))
        go(near_block(0))
        for i in range(n_f):
            for j in range(count):
                cross(j, i).wait_recv()
                total = xs[j][here.at(flip(j) * offsets[i]), :, share(j, here.core)].astype(wide)
                total = total + nears[j][i].astype(wide)
                if offsets[i]:
                    step, way = abs(offsets[i]), 1 if offsets[i] > 0 else -1
                    if step < last[way]:
                        hop(j, step + 1, way).wait_recv()
                        total = total + moves[j][steps.index((step + 1, way))].astype(wide)
                    terms[j][steps.index((step, way))] = total.astype(low)
                    go(hop(j, step, way))
                else:
                    for way in (1, -1):
                        if last[way] >= 1:
                            hop(j, 1, way).wait_recv()
                            total = total + moves[j][steps.index((1, way))].astype(wide)
                    parts[j][here.y] = total.astype(low)

        def swap(j, k, spot):
            slot = parts[j].at[spot]
            return remote(slot, slot, y_s.at[j, k], y_r.at[j, k], {"seq": here.seq(-k, 0)})

        def side(j, core):
            columns = outs[j].at[:, share(j, core)]
            return remote(columns, columns, side_s.at[j], side_r.at[j], {"seq": here.seq(0, 1)})

        for j in range(count):
            for k in range(1, chips):
                go(swap(j, k, here.y))
        for k in range(1, chips):
            far_small(k, here.seq(k, 0)).wait_recv()
            go(near_small(k, here.seq(k, 0)))
            far_block(k).wait_recv()
            go(near_block(k))
        for j in range(count):
            for k in range(1, chips):
                swap(j, k, lax.rem(here.y + k, chips)).wait_recv()
            total = parts[j][0].astype(wide)
            for y in range(1, chips):
                total = total + parts[j][y].astype(wide)
            outs[j][:, share(j, here.core)] = total.astype(low)
            go(side(j, here.core))
        for k in range(chips):
            near_small(k, here.seq(k, 1)).wait_recv()
        total = smalls[0].astype(wide)
        for spot in range(1, n_seq):
            total = total + smalls[spot].astype(wide)
        small_out[...] = total
        for k in range(chips):
            near_block(k).wait_recv()
        for j in range(count):
            side(j, other).wait_recv()
        for copy in started:
            copy.wait_send()
        own.wait()

    sems = pltpu.SemaphoreType.DMA
    shapes = [(pack.shape[1], width) for pack, width in zip(packs, widths, strict=True)]
    near = [pltpu.VMEM((n_f, *shape), low) for shape in shapes]
    ring = [pltpu.VMEM((len(steps), *shape), low) for shape in shapes]
    part = [pltpu.VMEM((chips, *shape), low) for shape in shapes]
    results = pl.pallas_call(
        body,
        out_shape=tuple(jax.ShapeDtypeStruct(pack.shape[1:], low) for pack in packs)
        + (
            jax.ShapeDtypeStruct((n_seq, *block.shape), low),
            jax.ShapeDtypeStruct(small.shape, wide),
        ),
        in_specs=[VMEM] * count + [ANY, VMEM],
        out_specs=(VMEM,) * count + (ANY, VMEM),
        scratch_shapes=near
        + ring * 2
        + part
        + [pltpu.VMEM((n_seq, *small.shape), low)]
        + [sems((count, n_f))] * 2
        + [sems((count, len(steps)))] * 2
        + [sems((count, chips))] * 2
        + [sems((count,))] * 2
        + [sems(())]
        + [sems((2 * chips,))] * 4,
        compiler_params=params(number),
    )(*packs, block, small)
    sums = [result[:, :size] for result, size in zip(results[:count], wanted, strict=True)]
    return sums, results[count], results[count + 1]


def ring_terms(sides, outs, n_f, n_seq, dtype):
    flat, spots = [], []
    left = 0
    for side in sides:
        top = 0
        for part in side:
            flat.append(part)
            spots.append((top, left))
            top += part.shape[1]
        left += side[0].shape[2]
    moved = [block for _, _, _, came in outs for block, _ in came]

    def body(*refs):
        parts, moves = refs[: len(flat)], list(refs[len(flat) : len(flat) + len(moved)])
        results = refs[len(flat) + len(moved) : len(flat) + len(moved) + len(outs)]
        scratch, sem = refs[len(flat) + len(moved) + len(outs) : -1], refs[-1]
        here = Places(n_f, n_seq)
        copies = []
        for i, (offset, first, stop, _) in enumerate(outs):
            owner = here.at(offset)
            for at, (part, (above, before)) in enumerate(zip(parts, spots, strict=True)):
                start, end = max(first, before), min(stop, before + part.shape[2])
                if start < end:
                    copies.append(
                        pltpu.make_async_copy(
                            part.at[owner, :, start - before : end - before],
                            scratch[i].at[
                                above : above + part.shape[1], start - first : end - first
                            ],
                            sem.at[i, at],
                        )
                    )
        for copy in copies:
            copy.start()
        for copy in copies:
            copy.wait()
        for i, (_, first, stop, came) in enumerate(outs):
            edges = sorted(
                {first, stop}
                | {c for _, c in came}
                | {c + block.shape[1] for block, c in came}
            )
            here_moves = [(moves.pop(0), c) for _, c in came]
            for start, end in zip(edges, edges[1:]):
                total = scratch[i][:, start - first : end - first].astype(wide)
                for ref, c in here_moves:
                    if c <= start and end <= c + ref.shape[1]:
                        total = total + ref[:, start - c : end - c].astype(wide)
                results[i][:, start - first : end - first] = total.astype(dtype)

    rows = sum(part.shape[1] for part in sides[0])
    shapes = [(rows, stop - first) for _, first, stop, _ in outs]
    return pl.pallas_call(
        body,
        out_shape=tuple(jax.ShapeDtypeStruct(shape, dtype) for shape in shapes),
        in_specs=[ANY] * len(flat) + [VMEM] * len(moved),
        out_specs=(VMEM,) * len(outs),
        scratch_shapes=[pltpu.VMEM(shape, low) for shape in shapes]
        + [pltpu.SemaphoreType.DMA((len(outs), len(flat)))],
        cost_estimate=brief(1),
        compiler_params=pltpu.CompilerParams(vmem_limit_bytes=32 * 2**20),
    )(*flat, *moved)


class Ring:
    def __init__(self, count, width):
        self.count = count
        walk = ring_order(count, width)
        self.up = [(walk[i], walk[(i + 1) % count]) for i in range(count)]
        self.down = [(b, a) for a, b in self.up]

    def hop(self, block, way):
        return lax.ppermute(block, "fsdp", self.up if way > 0 else self.down)


class Gathering:
    def __init__(self, ring, block):
        self.ring = ring
        self.step, self.steps = 0, ring.count // 2
        self.moving = (block, block)
        self.places = [(0, 0)]
        self.blocks = [block]

    def advance(self):
        if self.step == self.steps:
            return
        self.step += 1
        first, second = self.moving
        if self.step < self.steps:
            self.moving = (self.ring.hop(first, 1), self.ring.hop(second, -1))
            self.places += [(-self.step, 0), (self.step, 0)]
        else:
            half = first.shape[1] // 256 * 128
            self.moving = (
                self.ring.hop(first[:, :half], 1),
                self.ring.hop(second[:, half:], -1),
            )
            self.places += [(self.step, 0), (self.step, half)]
        self.blocks += list(self.moving)

    def done(self):
        while self.step < self.steps:
            self.advance()
        return [
            (offset, block, column)
            for (offset, column), block in zip(self.places, self.blocks, strict=True)
        ]

    def live(self):
        return (self.moving, self.blocks)

    def restore(self, live):
        self.moving, self.blocks = live


class Scattering:
    def __init__(self, ring, sides, n_seq):
        self.ring, self.sides, self.n_seq = ring, sides, n_seq
        self.width = sum(side[0].shape[2] for side in sides)
        self.half = self.width // 256 * 128
        self.step, self.steps = 0, ring.count // 2
        self.moving = ()

    def terms(self, outs, dtype):
        return ring_terms(self.sides, outs, self.ring.count, self.n_seq, dtype)

    def advance(self):
        if self.step == self.steps:
            return
        self.step += 1
        offset = self.steps - self.step + 1
        if self.step == 1:
            outs = [(offset, 0, self.half, []), (offset, self.half, self.width, [])]
        else:
            ahead, back = self.moving
            right = self.half if self.step == 2 else 0
            outs = [
                (offset, 0, self.width, [(ahead, 0)]),
                (-offset, 0, self.width, [(back, right)]),
            ]
        ahead, back = self.terms(outs, low)
        self.moving = (self.ring.hop(ahead, 1), self.ring.hop(back, -1))

    def done(self, dtype):
        while self.step < self.steps:
            self.advance()
        right = self.half if self.steps == 1 else 0
        ahead, back = self.moving
        (total,) = self.terms([(0, 0, self.width, [(ahead, 0), (back, right)])], dtype)
        return total

    def live(self):
        return self.moving

    def restore(self, live):
        self.moving = live


def tie(movers, values):
    lives, values = lax.optimization_barrier(([mover.live() for mover in movers], values))
    for mover, live in zip(movers, lives, strict=True):
        mover.restore(live)
    return values


class Group:
    def __init__(self, count):
        self.count = count
        self.chips = count // CORES
        me = lax.axis_index("seq")
        self.y, self.core = me // CORES, lax.rem(me, CORES)
        self.sibling = [(i, i ^ 1) for i in range(count)]
        self.order = [(k, c) for k in range(self.chips) for c in range(CORES)]

    def shift(self, k):
        n = self.chips
        return [(i, ((i // CORES + k) % n) * CORES + i % CORES) for i in range(self.count)]

    def index(self, k, c):
        return lax.rem(self.y + k, self.chips) * CORES + (self.core + c) % CORES

    def over(self, block):
        return [block] + [
            lax.ppermute(block, "seq", self.shift(-k)) for k in range(1, self.chips)
        ]

    def across(self, blocks):
        out = []
        for block in blocks:
            out += [block, lax.ppermute(block, "seq", self.sibling)]
        return out

    def swap(self, block):
        return lax.ppermute(block, "seq", self.sibling)

    def cross(self, terms):
        return [
            lax.ppermute(terms[k * CORES + 1], "seq", self.sibling) for k in range(self.chips)
        ]

    def send(self, sums):
        return [
            lax.ppermute(sums[k].astype(low), "seq", self.shift(k)) for k in range(1, self.chips)
        ]

    def laid(self, pieces, axis, dtype):
        width = pieces[0].shape[axis]
        shape = list(pieces[0].shape)
        shape[axis] = width * self.count
        out = jnp.zeros(shape, dtype)
        for (k, c), piece in zip(self.order, pieces, strict=True):
            out = lax.dynamic_update_slice_in_dim(
                out, piece.astype(dtype), self.index(k, c) * width, axis
            )
        return out


class Summing:
    def __init__(self, values, axes):
        self.values = values
        self.steps = [
            (axis, 1 << bit)
            for axis in axes
            for bit in range((lax.axis_size(axis) - 1).bit_length())
        ]
        assert all(lax.axis_size(axis) & (lax.axis_size(axis) - 1) == 0 for axis in axes)

    def advance(self):
        if self.steps:
            axis, step = self.steps.pop(0)
            pairs = [(i, i ^ step) for i in range(lax.axis_size(axis))]
            self.values = self.values + lax.ppermute(self.values, axis, pairs)

    def done(self):
        while self.steps:
            self.advance()
        return self.values

    def live(self):
        return self.values

    def restore(self, live):
        self.values = live


def cut_columns(weights, raises, gains, n_f, n_seq, slab):
    rows, ff = weights[0].shape
    rank_rows = raises[0].shape[0]
    block, cut = ff // n_f, ff // (n_f * n_seq)

    def body(gain_ref, w0, w1, r0, r1, out):
        me = lax.axis_index("seq")

        def run(ref, spot):
            runs = [
                ref[:, f * block + spot * cut : f * block + (spot + 1) * cut] for f in range(n_f)
            ]
            gap = slab - n_f * cut
            if gap:
                runs.append(jnp.zeros((ref.shape[0], gap), ref.dtype))
            return jnp.concatenate(runs, axis=1)

        for spot in range(n_seq):

            @pl.when(me == spot)
            def _():
                for side, (weight, raised) in enumerate(((w0, r0), (w1, r1))):
                    at = side * slab
                    out[:rank_rows, at : at + slab] = run(raised, spot)
                    scaled = run(weight, spot).astype(wide) * gain_ref[...]
                    out[rank_rows:, at : at + slab] = scaled.astype(low)

    return pl.pallas_call(
        body,
        out_shape=jax.ShapeDtypeStruct((rank_rows + rows, 2 * slab), low),
        compiler_params=pltpu.CompilerParams(vmem_limit_bytes=48 * 2**20),
    )(gains, *weights, *raises)


def place_columns(pieces, gains, n_f, n_seq, rank_rows, ff, slab):
    rows = pieces.shape[1] - rank_rows
    cut = ff // (n_f * n_seq)
    chips = n_seq // CORES

    def body(gain_ref, x, w0, w1, r0, r1):
        me = lax.axis_index("seq")
        y, core = me // CORES, lax.rem(me, CORES)

        def spot_of(spot):
            ahead = lax.rem(spot // CORES - y + chips, chips)
            return ahead * CORES + lax.rem(spot % CORES + core, CORES)

        def fill(out, first, count, at, gain):
            whole = [x[spot_of(spot), first : first + count, at : at + slab] for spot in range(n_seq)]
            runs = [
                whole[spot][:, f * cut : (f + 1) * cut] for f in range(n_f) for spot in range(n_seq)
            ]
            result = jnp.concatenate(runs, axis=1).astype(wide)
            out[...] = result if gain is None else result * gain

        for side, (weight, raised) in enumerate(((w0, r0), (w1, r1))):
            fill(raised, 0, rank_rows, side * slab, None)
            fill(weight, rank_rows, rows, side * slab, gain_ref[...])

    return pl.pallas_call(
        body,
        out_shape=(jax.ShapeDtypeStruct((rows, ff), wide),) * 2
        + (jax.ShapeDtypeStruct((rank_rows, ff), wide),) * 2,
        compiler_params=pltpu.CompilerParams(vmem_limit_bytes=56 * 2**20),
    )(gains, pieces)


def gelu_parts(gate):
    scale = (2.0 / jnp.pi) ** 0.5
    cube = 0.044715
    square = gate * gate
    half = 0.5 * jnp.tanh(gate * (scale + scale * cube * square)) + 0.5
    value = gate * half
    slope = half + value * (1.0 - half) * (2.0 * scale + 6.0 * scale * cube * square)
    return value, slope


def attention(queries, both, mask, rows):
    n_seq, tokens, _ = both.shape
    length = tokens // rows
    scale = HD ** (-0.5)

    def body(q, kv, hidden, out, log_total):
        for r in range(rows):
            at = slice(r * length, (r + 1) * length)
            keys = kv[:, at, :HD].reshape(n_seq * length, HD)
            values = kv[:, at, HD:].reshape(n_seq * length, HD)
            for h in range(H):
                head = slice(h * HD, (h + 1) * HD)
                scores = mul_t(q[at, head], keys) * scale + hidden[r]
                top = jnp.max(scores, axis=-1, keepdims=True)
                weights = jnp.exp(scores - top)
                total = jnp.sum(weights, axis=-1, keepdims=True)
                out[at, head] = (mul(weights.astype(low), values) / total).astype(low)
                log_total[r, h] = top + jnp.log(total)

    return pl.pallas_call(
        body,
        out_shape=(
            jax.ShapeDtypeStruct(queries.shape, low),
            jax.ShapeDtypeStruct((rows, H, length, 1), wide),
        ),
        cost_estimate=brief(2),
        compiler_params=pltpu.CompilerParams(vmem_limit_bytes=48 * 2**20),
    )(queries, both, mask)


def attention_back(queries, both, mask, log_total, out, g_out, cosine, sine, rows):
    n_seq, tokens, _ = both.shape
    length = tokens // rows
    scale = HD ** (-0.5)
    half = HD // 2

    def body(q, kv, hidden, logs, o, g, cos, sin, g_q, g_both):
        for r in range(rows):
            at = slice(r * length, (r + 1) * length)
            keys = kv[:, at, :HD].reshape(n_seq * length, HD)
            values = kv[:, at, HD:].reshape(n_seq * length, HD)
            d_keys = d_values = None
            for h in range(H):
                head = slice(h * HD, (h + 1) * HD)
                scores = mul_t(q[at, head], keys) * scale + hidden[r]
                probs = jnp.exp(scores - logs[r, h])
                grad = g[at, head]
                dots = jnp.sum(
                    grad.astype(wide) * o[at, head].astype(wide), axis=-1, keepdims=True
                )
                d_scores = (probs * (mul_t(grad, values) - dots)).astype(low)
                d_query = mul(d_scores, keys) * scale
                first, second = d_query[:, :half], d_query[:, half:]
                c, s = cos[at, :], sin[at, :]
                turned = jnp.concatenate([first * c + second * s, second * c - first * s], axis=1)
                g_q[at, head] = turned.astype(low)
                d_key = t_mul(d_scores, q[at, head])
                d_value = t_mul(probs.astype(low), grad)
                d_keys = d_key if d_keys is None else d_keys + d_key
                d_values = d_value if d_values is None else d_values + d_value
            g_both[:, at, :HD] = (d_keys * scale).astype(low).reshape(n_seq, length, HD)
            g_both[:, at, HD:] = d_values.astype(low).reshape(n_seq, length, HD)

    return pl.pallas_call(
        body,
        out_shape=(
            jax.ShapeDtypeStruct(queries.shape, low),
            jax.ShapeDtypeStruct(both.shape, low),
        ),
        cost_estimate=brief(3),
        compiler_params=pltpu.CompilerParams(vmem_limit_bytes=56 * 2**20),
    )(queries, both, mask, log_total, out, g_out, cosine, sine)


def landing(items, buffers, rows_first, sem, here):
    copies = []
    for at, (offset, ref, column) in enumerate(items):
        owner = here.at(offset)
        first = 0
        for part, buffer in enumerate(buffers):
            count = rows_first[part]
            copies.append(
                pltpu.make_async_copy(
                    ref.at[first : first + count],
                    buffer.at[owner, :, column : column + ref.shape[1]],
                    sem.at[at, part],
                )
            )
            first += count
    for copy in copies:
        copy.start()
    for copy in copies:
        copy.wait()


def mlp_forward(
    items, tokens2, adapters, before, part, n_f, n_seq, rank_rows, own_rows, slab
):
    count, width = tokens2.shape
    rank = rank_rows * n_f
    tile = 256 if slab % 256 == 0 else 128
    chunk = 512
    first, stop = part
    wanted = []
    for side in range(2):
        start, end = side * slab + first * tile, side * slab + stop * tile
        for at, (offset, block, column) in enumerate(items):
            low_end, high_end = max(start, column), min(end, column + block.shape[1])
            if low_end < high_end:
                wanted.append((at, offset, low_end - column, high_end - column, side, low_end - start))
    adapters = [a.reshape(n_f, own_rows, rank) for a in adapters]

    def body(x, lower_g, lower_u, *refs):
        blocks, refs = refs[: len(items)], refs[len(items) + len(before) :]
        hidden, back_g, back_u, full_g, full_u, raised_g, raised_u = refs[:7]
        raises, weights, merged, sem = refs[7:]
        here = Places(n_f, n_seq)
        step = pl.program_id(0)

        @pl.when(step == 0)
        def _():
            copies = []
            for number, (at, offset, start, end, side, column) in enumerate(wanted):
                owner = here.at(offset)
                for which, (buffer, rows) in enumerate(
                    (
                        (raises, slice(0, rank_rows)),
                        (weights, slice(rank_rows, rank_rows + own_rows)),
                    )
                ):
                    copies.append(
                        pltpu.make_async_copy(
                            blocks[at].at[rows, start:end],
                            buffer.at[side, owner, :, column : column + end - start],
                            sem.at[number, which],
                        )
                    )
            for copy in copies:
                copy.start()
            for copy in copies:
                copy.wait()

        for side, (lower, full, raised) in enumerate(
            ((lower_g, full_g, raised_g), (lower_u, full_u, raised_u))
        ):
            columns = pl.ds(pl.multiple_of(step * tile, 128), tile)
            up_matrix = raises[side, :, :, columns].reshape(rank, tile)
            raised[...] = up_matrix
            for f in range(n_f):
                total = weights[side, f, :, columns].astype(wide) + mul(lower[f], up_matrix)
                total = total.astype(low)
                full[f] = total
                merged[side, f * own_rows : (f + 1) * own_rows, :] = total

        def some(i, carry):
            at = pl.ds(pl.multiple_of(i * chunk, chunk), chunk)
            gate = mul(x[at, :], merged[0])
            up = mul(x[at, :], merged[1])
            value, slope = gelu_parts(gate)
            hidden[at, :] = (value * up).astype(low)
            back_g[at, :] = (up * slope).astype(low)
            back_u[at, :] = value.astype(low)
            return carry

        lax.fori_loop(0, count // chunk, some, 0, unroll=True)

    by_column = pl.BlockSpec((count, tile), lambda j: (0, j + first))
    by_weight = pl.BlockSpec((n_f, own_rows, tile), lambda j: (0, 0, j + first))
    by_raise = pl.BlockSpec((rank, tile), lambda j: (0, j + first))
    return pl.pallas_call(
        body,
        grid=(stop - first,),
        out_shape=(jax.ShapeDtypeStruct((count, slab), low),) * 3
        + (jax.ShapeDtypeStruct((n_f, own_rows, slab), low),) * 2
        + (jax.ShapeDtypeStruct((rank, slab), low),) * 2,
        in_specs=[VMEM] * 3 + [ANY] * (len(items) + len(before)),
        input_output_aliases={3 + len(items) + i: i for i in range(len(before))},
        out_specs=(by_column,) * 3 + (by_weight,) * 2 + (by_raise,) * 2,
        scratch_shapes=[
            pltpu.VMEM((2, n_f, rank_rows, (stop - first) * tile), low),
            pltpu.VMEM((2, n_f, own_rows, (stop - first) * tile), low),
            pltpu.VMEM((2, width, tile), low),
            pltpu.SemaphoreType.DMA((len(wanted), 2)),
        ],
        cost_estimate=brief(3),
        compiler_params=pltpu.CompilerParams(vmem_limit_bytes=56 * 2**20),
    )(tokens2, *adapters, *(block for _, block, _ in items), *before)


def mlp_backward(items, d_raise, g_tokens, back_g, back_u, n_f, n_seq, cut, slab):
    count, width = g_tokens.shape
    rank = d_raise.shape[0]
    tile = 256 if slab % 256 == 0 else 128
    chunk = 512
    offsets = [(offset, column) for offset, _, column in items]

    def body(g, raised, mul_g, mul_u, *refs):
        blocks = refs[: len(items)]
        grad_g, grad_u, full, raw, merged, sem = refs[len(items) :]
        here = Places(n_f, n_seq)
        step = pl.program_id(0)

        @pl.when(step == 0)
        def _():
            landing(
                [(o, ref, c) for (o, c), ref in zip(offsets, blocks, strict=True)],
                (raw,),
                (cut,),
                sem,
                here,
            )
            for f in range(n_f):
                merged[f * cut : (f + 1) * cut, :] = raw[f, :, :width].astype(wide) + mul(
                    raw[f, :, width:], raised[...]
                )
            if slab > n_f * cut:
                merged[n_f * cut :, :] = jnp.zeros((slab - n_f * cut, width), wide)

        weight = merged[pl.ds(pl.multiple_of(step * tile, tile), tile), :].astype(low)
        full[...] = weight

        def some(i, carry):
            at = pl.ds(pl.multiple_of(i * chunk, chunk), chunk)
            g_hidden = mul_t(g[at, :], weight)
            grad_g[at, :] = (g_hidden * mul_g[at, :].astype(wide)).astype(low)
            grad_u[at, :] = (g_hidden * mul_u[at, :].astype(wide)).astype(low)
            return carry

        lax.fori_loop(0, count // chunk, some, 0, unroll=True)

    by_column = pl.BlockSpec((count, tile), lambda j: (0, j))
    return pl.pallas_call(
        body,
        grid=(slab // tile,),
        out_shape=(jax.ShapeDtypeStruct((count, slab), low),) * 2
        + (jax.ShapeDtypeStruct((slab, width), low),),
        in_specs=[VMEM] * 2 + [by_column] * 2 + [ANY] * len(items),
        out_specs=(by_column,) * 2 + (pl.BlockSpec((tile, width), lambda j: (j, 0)),),
        scratch_shapes=[
            pltpu.VMEM((n_f, cut, width + rank), low),
            pltpu.VMEM((slab, width), wide),
            pltpu.SemaphoreType.DMA((len(items), 1)),
        ],
        cost_estimate=brief(3),
        compiler_params=pltpu.CompilerParams(vmem_limit_bytes=56 * 2**20),
    )(g_tokens, d_raise, back_g, back_u, *(block for _, block, _ in items))


def shards(
    inputs,
    cotangent,
    segments,
    exits,
    confidence,
    attn_gain,
    q_weight,
    k_weight,
    v_weight,
    o_weight,
    q_down,
    q_up,
    k_down,
    k_up,
    v_down,
    v_up,
    o_down,
    o_up,
    mlp_gain,
    gate_weight,
    up_weight,
    down_weight,
    gate_down,
    gate_up,
    up_down,
    up_up,
    down_down,
    down_up,
):
    n_seq, n_f = lax.axis_size("seq"), lax.axis_size("fsdp")
    me = lax.axis_index("seq")
    ring = Ring(n_f, n_seq // CORES)
    group = Group(n_seq)
    rows, length, width = inputs.shape
    tokens = rows * length
    rank = q_down.shape[1]
    hq = q_weight.shape[1]
    ff = gate_weight.shape[1]
    own_rows = q_weight.shape[0]
    rank_rows = q_up.shape[0]
    o_rows = o_weight.shape[0]
    cut = ff // (n_f * n_seq)
    slab = -(-n_f * cut // 128) * 128
    scale = HD ** (-0.5)

    gain1 = attn_gain.astype(wide)[:, None]
    gain2 = mlp_gain.astype(wide)[:, None]

    def rows_of(array):
        part = array.shape[0] // n_seq
        return lax.dynamic_slice_in_dim(array, me * part, part, 0)

    small_blocks = pack_small(
        gain1,
        gain2,
        (q_weight, k_weight, v_weight, q_down, k_down, v_down),
        (gate_down, up_down),
        (q_up, k_up, v_up),
        (o_up, down_up),
        (o_weight, o_down),
        n_seq,
    )

    slabs = Gathering(
        ring, cut_columns((gate_weight, up_weight), (gate_up, up_up), gain2, n_f, n_seq, slab)
    )
    d_lower = rows_of(down_down)
    downs = Gathering(ring, jnp.concatenate([rows_of(down_weight), d_lower], axis=1))

    depth_ids = jnp.arange(DEPTHS, dtype=jnp.int32)
    matches = (exits.reshape(tokens)[:, None] == depth_ids[None, :]).astype(wide)
    counted = Summing(
        jnp.concatenate(
            [jnp.sum(matches, axis=0), jnp.sum(matches * confidence.reshape(tokens)[:, None], axis=0)]
        ),
        ("seq", "fsdp"),
    )
    resid = inputs.reshape(tokens, width).astype(wide)
    active = (exits.reshape(tokens) >= LOOP).astype(wide)[:, None]
    cot = cotangent.reshape(tokens, width).astype(wide)
    g_mlp = (active * cot).astype(low)
    places = me * length + jnp.arange(length, dtype=jnp.int32)
    frequency = rope_base ** (-2.0 * jnp.arange(HD // 2, dtype=wide) / HD)
    angles = jnp.tile(places, rows).astype(wide)[:, None] * frequency[None, :]
    cosine, sine = jnp.cos(angles), jnp.sin(angles)
    r1 = lax.rsqrt(jnp.mean(resid * resid, axis=-1, keepdims=True) + epsilon)
    unit1 = (resid * r1).astype(low)

    slabs.advance()
    seg_pieces = group.over(segments.astype(low))
    whole = gather_whole(small_blocks, (False, False, True, True, True), 0, n_f, n_seq)
    whole, seg_pieces, unit1, cosine, sine, g_mlp = tie(
        (slabs, downs), (whole, seg_pieces, unit1, cosine, sine, g_mlp)
    )
    qkv_side, ups, side_o, ups2, adapters = (part.reshape(-1, part.shape[2]) for part in whole)
    kv = HD
    lin = hq + 2 * kv
    gate_adapter, up_adapter = adapters[:, :rank], adapters[:, rank : 2 * rank]
    side_o = side_o[:, : width + rank]
    q_raise, k_raise, v_raise = ups[:, :hq], ups[:, hq : hq + kv], ups[:, hq + kv : lin]
    o_raise, d_raise = ups2[:, :width], ups2[:, width : 2 * width]

    slabs.advance()
    seg_pieces = group.across(seg_pieces)
    projected = mul(unit1, qkv_side)
    inner = projected[:, lin:].astype(low)
    q_inner, k_inner, v_inner = inner[:, :rank], inner[:, rank : 2 * rank], inner[:, 2 * rank :]
    q_lin = projected[:, :hq] + mul(q_inner, q_raise)
    k_lin = projected[:, hq : hq + kv] + mul(k_inner, k_raise)
    v_lin = projected[:, hq + kv : lin] + mul(v_inner, v_raise)
    half = HD // 2

    def rope(values):
        parts = []
        for at in range(0, values.shape[1], HD):
            first, second = values[:, at : at + half], values[:, at + half : at + HD]
            parts += [first * cosine - second * sine, second * cosine + first * sine]
        return jnp.concatenate(parts, axis=1)

    queries = rope(q_lin).astype(low)
    keys = rope(k_lin).astype(low)
    values = v_lin.astype(low)
    both = jnp.concatenate([keys, values], axis=-1)
    both = gather_group(both, 2, n_seq)
    key_seg = jnp.concatenate(seg_pieces, axis=1).astype(jnp.int32)
    key_place = jnp.concatenate(
        [
            group.index(k, c) * length + jnp.arange(length, dtype=jnp.int32)
            for k, c in group.order
        ]
    )
    allowed = (segments[:, :, None] == key_seg[:, None, :]) & (
        key_place[None, None, :] <= places[None, :, None]
    )
    mask = jnp.where(allowed, 0.0, -1e30).astype(wide)
    both, queries, mask, inner, g_mlp = tie((slabs,), (both, queries, mask, inner, g_mlp))
    q_inner, k_inner, v_inner = inner[:, :rank], inner[:, rank : 2 * rank], inner[:, 2 * rank :]

    slabs.advance()
    g_mlp = group.over(g_mlp)
    attn_low, log_total = attention(queries, both, mask, rows)
    projected = mul(attn_low, side_o)
    o_inner = projected[:, width:].astype(low)
    mid = resid + active * (projected[:, :width] + mul(o_inner, o_raise))
    r2 = lax.rsqrt(jnp.mean(mid * mid, axis=-1, keepdims=True) + epsilon)
    unit2 = (mid * r2).astype(low)
    unit2, mid, r2, g_mlp, attn_low, o_inner, log_total = tie(
        (slabs,), (unit2, mid, r2, g_mlp, attn_low, o_inner, log_total)
    )

    slabs.advance()
    downs.advance()
    unit2 = gather_group(unit2, 3, n_seq).reshape(-1, width)
    unit2, g_mlp = tie((slabs, downs), (unit2, g_mlp))

    downs.advance()
    g_mlp = group.across(g_mlp)
    tiles = slab // (256 if slab % 256 == 0 else 128)
    arrived = slabs.done()

    def forward(first, stop, before):
        return mlp_forward(
            arrived,
            unit2,
            (gate_adapter, up_adapter),
            before,
            (first, stop),
            n_f,
            n_seq,
            rank_rows,
            own_rows,
            slab,
        )

    half_way = forward(0, (tiles + 1) // 2, ())
    half_way, g_mlp = tie((downs,), (half_way, g_mlp))
    downs.advance()
    counted.advance()
    hidden, back_g, back_u, gate_full, up_full, g_raise, u_raise = forward(
        (tiles + 1) // 2, tiles, half_way
    )
    hidden, back_g, back_u, g_mlp = tie((downs, counted), (hidden, back_g, back_u, g_mlp))
    g_mlp = jnp.concatenate(g_mlp, axis=0)

    downs.advance()
    counted.advance()
    g_down = t_mul(hidden, g_mlp).astype(low)
    g_down, g_mlp, back_g, back_u = tie((downs, counted), (g_down, g_mlp, back_g, back_u))

    down_sums = Scattering(ring, [[g_down[: n_f * cut].reshape(n_f, cut, width)]], n_seq)

    down_sums.advance()
    counted.advance()
    g_gate, g_up, down_full = mlp_backward(
        downs.done(), d_raise, g_mlp, back_g, back_u, n_f, n_seq, cut, slab
    )
    g_gate, g_up, down_full = tie((down_sums, counted), (g_gate, g_up, down_full))

    down_sums.advance()
    counted.advance()
    gg = t_mul(unit2, g_gate).astype(low)
    gg_raise = t_mul(gate_adapter, gg).astype(low)
    gg, gg_raise, g_gate, g_up, unit2 = tie(
        (down_sums, counted), (gg, gg_raise, g_gate, g_up, unit2)
    )
    down_sums.advance()
    gu = t_mul(unit2, g_up).astype(low)
    gu_raise = t_mul(up_adapter, gu).astype(low)
    gg, gu, gg_raise, gu_raise, g_gate, g_up = tie(
        (down_sums,), (gg, gu, gg_raise, gu_raise, g_gate, g_up)
    )
    slab_sums = Scattering(
        ring,
        [
            [part.reshape(n_f, -1, slab) for part in side]
            for side in ((gg_raise, gg), (gu_raise, gu))
        ],
        n_seq,
    )
    chips = range(n_seq // CORES)
    here_tokens = CORES * tokens

    def token_gradient(at):
        result = mul_t(g_gate[at], gate_full.reshape(width, slab))
        return (result + mul_t(g_up[at], up_full.reshape(width, slab))).astype(low)

    slab_sums.advance()
    e2_there = token_gradient(slice(here_tokens, None))
    g_down = down_sums.done(low)
    down_rows = jnp.concatenate([g_down, mul_t(g_down, d_raise).astype(low)], axis=1)
    gd_raise = t_mul(d_lower, g_down).astype(low)
    e2_there, g_gate, g_up, down_rows, gd_raise = tie(
        (slab_sums,), (e2_there, g_gate, g_up, down_rows, gd_raise)
    )

    slab_sums.advance()
    there = [e2_there[i * tokens : (i + 1) * tokens] for i in range(n_seq - CORES)]
    e2_near = [group.swap(there[(k - 1) * CORES + 1]) for k in chips[1:]]
    down_rows = group.over(down_rows)
    e2_here = token_gradient(slice(0, here_tokens))
    e2_here, e2_near, hidden, down_rows = tie((slab_sums,), (e2_here, e2_near, hidden, down_rows))

    slab_sums.advance()
    e2_sums = [
        there[(k - 1) * CORES].astype(wide) + e2_near[k - 1].astype(wide) for k in chips[1:]
    ]
    e2_far = group.send([None, *e2_sums])
    e2_own = group.swap(e2_here[tokens:])
    branch = mul(hidden, down_full).astype(low)
    branch, e2_far, e2_own, e2_here = tie((slab_sums,), (branch, e2_far, e2_own, e2_here))
    terms = [branch[i * tokens : (i + 1) * tokens] for i in range(n_seq)]
    e2 = e2_here[:tokens].astype(wide) + e2_own.astype(wide)
    for block in e2_far:
        e2 = e2 + block.astype(wide)

    slab_sums.advance()
    near = group.cross(terms)
    g_mid = cot + r2 * e2 - mid * (r2 * r2 * r2 * jnp.mean(e2 * mid, axis=-1, keepdims=True))
    g_branch = (active * g_mid).astype(low)
    g_inner = mul_t(g_branch, o_raise).astype(low)
    g_attn = mul_t(jnp.concatenate([g_branch, g_inner], axis=1), side_o).astype(low)
    sums = [terms[k * CORES].astype(wide) + near[k].astype(wide) for k in chips]
    g_attn, sums, g_mid, g_branch, down_rows = tie(
        (slab_sums,), (g_attn, sums, g_mid, g_branch, down_rows)
    )

    middle = tokens // 2
    down_rows = group.across(down_rows)
    far_first = group.send([block[:middle] for block in sums])
    g_q, d_terms = attention_back(
        queries, both, mask, log_total, attn_low, g_attn, cosine, sine, rows
    )
    d_terms, g_q, g_mid, g_branch, down_rows, sums, far_first = tie(
        (), (d_terms, g_q, g_mid, g_branch, down_rows, sums, far_first)
    )

    d_near = group.cross([d_terms[i] for i in range(n_seq)])
    g_o = t_mul(attn_low, g_branch).astype(low)
    go_raise = t_mul(o_inner, g_branch).astype(low)
    o_pack = jnp.concatenate(
        [
            g_o.reshape(n_f, o_rows, width),
            go_raise.reshape(n_f, rank_rows, width),
            gd_raise.reshape(n_f, rank_rows, width),
        ],
        axis=1,
    )
    d_sums = [d_terms[k * CORES].astype(wide) + d_near[k].astype(wide) for k in chips]
    d_far = group.send(d_sums)
    d_far, g_q, d_both, o_pack, down_rows, sums = tie(
        (), (d_far, g_q, d_sums[0], o_pack, down_rows, sums)
    )

    far = group.send([block[middle:] for block in sums])
    down_rows = group.laid(down_rows, 0, wide)
    grad_down_weight, grad_down_down = down_rows[:, :width], down_rows[:, width:]
    for block in d_far:
        d_both = d_both + block.astype(wide)
    first, second = d_both[:, :half], d_both[:, half:HD]
    g_k = jnp.concatenate(
        [first * cosine + second * sine, second * cosine - first * sine], axis=1
    ).astype(low)
    g_v = d_both[:, HD:].astype(low)
    gi_q = mul_t(g_q, q_raise).astype(low)
    gi_k = mul_t(g_k, k_raise).astype(low)
    gi_v = mul_t(g_v, v_raise).astype(low)
    g_lin = jnp.concatenate([g_q, g_k, g_v], axis=1)
    e1 = mul_t(jnp.concatenate([g_lin, gi_q, gi_k, gi_v], axis=1), qkv_side)
    input_grad = g_mid + r1 * e1 - resid * (
        r1 * r1 * r1 * jnp.mean(e1 * resid, axis=-1, keepdims=True)
    )
    input_grad = input_grad.astype(low).reshape(rows, length, width)
    g_qkv = t_mul(unit1, g_lin).astype(low)
    gr_qkv = jnp.concatenate(
        [t_mul(q_inner, g_q), t_mul(k_inner, g_k), t_mul(v_inner, g_v)], axis=1
    ).astype(low)
    qkv_pack = jnp.concatenate(
        [g_qkv.reshape(n_f, own_rows, lin), gr_qkv.reshape(n_f, rank_rows, lin)], axis=1
    )
    qkv_pack, o_pack, grad_down_weight, grad_down_down, input_grad, far, own_branch = tie(
        (), (qkv_pack, o_pack, grad_down_weight, grad_down_down, input_grad, far, sums[0])
    )
    for first, second in zip(far_first, far, strict=True):
        own_branch = own_branch + jnp.concatenate([first, second], axis=0).astype(wide)
    outputs = (mid + active * own_branch).astype(low).reshape(rows, length, width)

    g_slab = slab_sums.done(wide)
    unit_grad = g_slab[rank_rows:]
    own_full = [
        lax.dynamic_index_in_dim(full, lax.axis_index("fsdp"), 0, False)
        for full in (gate_full, up_full)
    ]
    merged = jnp.concatenate(own_full, axis=1).astype(wide)
    weight_grad = (unit_grad * gain2).astype(low)
    mlp_small = jnp.concatenate(
        [
            mul_t(weight_grad[:, :slab], g_raise),
            mul_t(weight_grad[:, slab:], u_raise),
            jnp.broadcast_to(
                jnp.sum(unit_grad * merged, axis=1, keepdims=True) / gain2, (own_rows, 128)
            ),
        ],
        axis=1,
    ).astype(low)
    packs, slab_pieces, mlp_small = scatter_whole(
        (qkv_pack, o_pack), g_slab.astype(low), mlp_small, 6, n_seq
    )
    qkv_pack, o_pack = (pack.astype(wide) for pack in packs)

    grad_o_weight = o_pack[:o_rows]
    grad_o_up = o_pack[o_rows : o_rows + rank_rows]
    grad_down_up = o_pack[o_rows + rank_rows :]
    grad_o_down = mul_t(packs[1][:o_rows], o_raise)
    unit_grad = qkv_pack[:own_rows]
    grad_lin = unit_grad * gain1
    grad_q_weight, grad_k_weight, grad_v_weight = (
        grad_lin[:, :hq],
        grad_lin[:, hq : hq + kv],
        grad_lin[:, hq + kv :],
    )
    grad_q_up, grad_k_up, grad_v_up = (
        qkv_pack[own_rows:, :hq],
        qkv_pack[own_rows:, hq : hq + kv],
        qkv_pack[own_rows:, hq + kv :],
    )
    grad_q_down = mul_t(grad_q_weight.astype(low), q_raise)
    grad_k_down = mul_t(grad_k_weight.astype(low), k_raise)
    grad_v_down = mul_t(grad_v_weight.astype(low), v_raise)
    own_lin = jnp.concatenate(
        [
            q_weight.astype(wide) + mul(q_down, q_raise),
            k_weight.astype(wide) + mul(k_down, k_raise),
            v_weight.astype(wide) + mul(v_down, v_raise),
        ],
        axis=1,
    )
    grad_attn_gain = jnp.sum(unit_grad * own_lin, axis=1)

    grad_gate_down, grad_up_down = mlp_small[:, :rank], mlp_small[:, rank : 2 * rank]
    grad_mlp_gain = mlp_small[:, 2 * rank]
    grad_gate_weight, grad_up_weight, grad_gate_up, grad_up_up = place_columns(
        slab_pieces, gain2, n_f, n_seq, rank_rows, ff, slab
    )

    counted = counted.done()
    mean_confidence = counted[DEPTHS:] / counted[:DEPTHS]
    return (
        outputs,
        input_grad,
        grad_attn_gain,
        grad_q_weight,
        grad_k_weight,
        grad_v_weight,
        grad_o_weight,
        grad_q_down,
        grad_q_up,
        grad_k_down,
        grad_k_up,
        grad_v_down,
        grad_v_up,
        grad_o_down,
        grad_o_up,
        grad_mlp_gain,
        grad_gate_weight,
        grad_up_weight,
        grad_down_weight,
        grad_gate_down,
        grad_gate_up,
        grad_up_down,
        grad_up_up,
        grad_down_down,
        grad_down_up,
        counted[:DEPTHS].astype(jnp.int32),
        mean_confidence,
    )


def solution(mesh):
    tokens3 = P("fsdp", "seq", None)
    tokens2 = P("fsdp", "seq")
    vector, matrix = P("fsdp"), P("fsdp", None)
    in_specs = (tokens3,) * 2 + (tokens2,) * 3 + (vector,) + (matrix,) * 12 + (vector,) + (matrix,) * 9
    out_specs = (
        (tokens3,) * 2 + (vector,) + (matrix,) * 12 + (vector,) + (matrix,) * 9 + (P(), P())
    )
    return jax.shard_map(shards, mesh=mesh, in_specs=in_specs, out_specs=out_specs, check_vma=False)
```

```python
import jax
import jax.numpy as jnp
from jax import lax
from jax.experimental import pallas as pl
from jax.experimental.pallas import tpu as pltpu
from jax.sharding import PartitionSpec as P

H = 4
HD = 256
DEPTHS = 3
LOOP = 1
CORES = 2

epsilon = 1e-06
rope_base = 10000.0
low = jnp.bfloat16
wide = jnp.float32


def mul(left, right):
    return jnp.dot(left, right, preferred_element_type=wide)


def mul_t(left, right):
    return lax.dot_general(left, right, (((1,), (1,)), ((), ())), preferred_element_type=wide)


def t_mul(left, right):
    return lax.dot_general(left, right, (((0,), (0,)), ((), ())), preferred_element_type=wide)


def ring_order(count, width):
    if width < 2 or count % width or (count // width) % 2:
        return list(range(count))
    depth = count // width
    walk = [0]
    for z in range(depth):
        columns = range(1, width) if z % 2 == 0 else range(width - 1, 0, -1)
        walk += [z * width + x for x in columns]
    walk += [z * width for z in range(depth - 1, 0, -1)]
    return walk


MESH = pl.DeviceIdType.MESH
ANY = pl.BlockSpec(memory_space=pl.ANY)
VMEM = pl.BlockSpec(memory_space=pltpu.VMEM)


def pick(index, table):
    result = jnp.int32(table[0])
    for spot, value in enumerate(table):
        if spot:
            result = jnp.where(index == spot, jnp.int32(value), result)
    return result


class Places:
    def __init__(self, n_f, n_seq):
        self.n_f, self.n_seq, self.chips = n_f, n_seq, n_seq // CORES
        self.walk = ring_order(n_f, n_seq // CORES)
        spots = [0] * n_f
        for spot, device in enumerate(self.walk):
            spots[device] = spot
        self.f, self.me = lax.axis_index("fsdp"), lax.axis_index("seq")
        self.spot = pick(self.f, spots)
        self.y, self.core = self.me // CORES, lax.rem(self.me, CORES)

    def at(self, offset):
        return pick(lax.rem(self.spot + offset + self.n_f, self.n_f), self.walk)

    def seq(self, k, c):
        return lax.rem(self.y + k + self.chips, self.chips) * CORES + lax.rem(
            self.core + c, CORES
        )

    def greet(self, ring):
        barrier = pltpu.get_barrier_semaphore()
        friends = [{"seq": self.seq(0, 1)}]
        friends += [{"seq": self.seq(k, 0)} for k in range(1, self.chips)]
        if ring:
            friends += [{"fsdp": self.at(1)}, {"fsdp": self.at(-1)}]
        for friend in friends:
            pl.semaphore_signal(barrier, inc=1, device_id=friend, device_id_type=MESH)
        pl.semaphore_wait(barrier, len(friends))


def remote(source, target, send, receive, device):
    return pltpu.make_async_remote_copy(
        src_ref=source,
        dst_ref=target,
        send_sem=send,
        recv_sem=receive,
        device_id=device,
        device_id_type=MESH,
    )


def brief(us):
    return pl.CostEstimate(
        flops=int(us * 1.0e9), bytes_accessed=int(us * 1.0e6), transcendentals=0
    )


def params(number):
    return pltpu.CompilerParams(
        collective_id=number, has_side_effects=True, vmem_limit_bytes=56 * 2**20
    )


def ring_steps(n_f):
    order = []
    for step in range(1, n_f // 2 + 1):
        order.append((step, 1))
        if step <= (n_f - 1) // 2:
            order.append((step, -1))
    return order


def pack_small(gain1, gain2, attention, lower, raises, raises2, outward, n_seq):
    groups = [(attention, gain1), (raises, None), (outward, None), (raises2, None), (lower, gain2)]
    shares = (CORES, CORES, n_seq, n_seq, n_seq)

    def body(*refs):
        refs = list(refs)
        for (parts, gain), out in zip(groups, refs[-len(groups) :], strict=True):
            factor = None if gain is None else refs.pop(0)[...]
            at = 0
            for part in parts:
                block = refs.pop(0)[...]
                if factor is not None:
                    block = (block.astype(wide) * factor).astype(low)
                out[:, at : at + part.shape[1]] = block
                at += part.shape[1]
            if at < out.shape[1]:
                out[:, at:] = jnp.zeros((out.shape[0], out.shape[1] - at), low)

    sizes = []
    for (parts, _), ways in zip(groups, shares, strict=True):
        total = sum(part.shape[1] for part in parts)
        sizes.append((parts[0].shape[0], total + -total % (128 * ways)))
    operands = []
    for parts, gain in groups:
        operands += ([] if gain is None else [gain]) + list(parts)
    return pl.pallas_call(
        body,
        out_shape=tuple(jax.ShapeDtypeStruct(size, low) for size in sizes),
        compiler_params=pltpu.CompilerParams(vmem_limit_bytes=48 * 2**20),
    )(*operands)


def gather_whole(blocks, spread, number, n_f, n_seq):
    count = len(blocks)
    chips = n_seq // CORES
    steps = ring_steps(n_f)
    order = [j for j in range(count) if spread[j]] + [j for j in range(count) if not spread[j]]

    def body(*refs):
        ins, outs = refs[:count], refs[count : 2 * count]
        local, ring_s, ring_r, y_s, y_r, core_s, core_r = refs[2 * count :]
        here = Places(n_f, n_seq)
        started = []

        def share(j, k, c):
            spot = here.seq(k, c) if spread[j] else lax.rem(here.core + c, CORES)
            width = ins[j].shape[-1] // (n_seq if spread[j] else CORES)
            return (slice(None), pl.ds(pl.multiple_of(spot * width, 128), width))

        def far(j):
            return range(1, chips if spread[j] else 1)

        copies = []
        for j in range(count):
            copy = pltpu.make_async_copy(ins[j], outs[j].at[here.f], local.at[j])
            copy.start()
            copies.append(copy)
        here.greet(True)

        def flip(j):
            return 1 if j == 0 else -1

        def forward(j, step, way):
            owner = here.at(-flip(j) * way * (step - 1))
            mine = share(j, 0, 0)
            source = ins[j].at[mine] if step == 1 else outs[j].at[(owner, *mine)]
            at = steps.index((step, way))
            copy = remote(
                source,
                outs[j].at[(owner, *mine)],
                ring_s.at[j, at],
                ring_r.at[j, at],
                {"fsdp": here.at(flip(j) * way)},
            )
            copy.start()
            started.append(copy)

        def landed(j, step, way):
            owner = here.at(-flip(j) * way * step)
            at = steps.index((step, way))
            block = outs[j].at[(owner, *share(j, 0, 0))]
            remote(block, block, ring_s.at[j, at], ring_r.at[j, at], {"fsdp": here.at(flip(j) * way)}).wait_recv()
            return owner

        def to_core(j, at, k, owner):
            block = outs[j].at[(owner, *share(j, k, 0))]
            copy = remote(
                block, block, core_s.at[j, at, k], core_r.at[j, at, k], {"seq": here.seq(0, 1)}
            )
            copy.start()
            started.append(copy)

        for j in order:
            for way in (1, -1):
                forward(j, 1, way)
        for at, (step, way) in enumerate(steps):
            for j in order:
                owner = landed(j, step, way)
                if (step + 1, way) in steps:
                    forward(j, step + 1, way)
                block = outs[j].at[(owner, *share(j, 0, 0))]
                for k in far(j):
                    copy = remote(
                        block, block, y_s.at[j, at, k], y_r.at[j, at, k], {"seq": here.seq(-k, 0)}
                    )
                    copy.start()
                    started.append(copy)
                to_core(j, at, 0, owner)
        for at, (step, way) in enumerate(steps):
            for j in order:
                owner = here.at(-flip(j) * way * step)
                for k in far(j):
                    block = outs[j].at[(owner, *share(j, k, 0))]
                    remote(
                        block, block, y_s.at[j, at, k], y_r.at[j, at, k], {"seq": here.seq(-k, 0)}
                    ).wait_recv()
                    to_core(j, at, k, owner)
        for at, (step, way) in enumerate(steps):
            for j in order:
                owner = here.at(-flip(j) * way * step)
                for k in [0, *far(j)]:
                    block = outs[j].at[(owner, *share(j, k, 1))]
                    remote(
                        block, block, core_s.at[j, at, k], core_r.at[j, at, k], {"seq": here.seq(0, 1)}
                    ).wait_recv()
        for copy in started:
            copy.wait_send()
        for copy in copies:
            copy.wait()

    sems = pltpu.SemaphoreType.DMA
    return pl.pallas_call(
        body,
        out_shape=tuple(jax.ShapeDtypeStruct((n_f,) + b.shape, b.dtype) for b in blocks),
        in_specs=[ANY] * count,
        out_specs=(ANY,) * count,
        scratch_shapes=[sems((count,))]
        + [sems((count, len(steps)))] * 2
        + [sems((count, len(steps), chips))] * 4,
        compiler_params=params(number),
    )(*blocks)


def gather_group(block, number, n_seq):
    rows = block.shape[0]
    chips = n_seq // CORES
    parts = 4 if rows % 64 == 0 else 1
    size = rows // parts

    def body(x, out, local, y_s, y_r, core_s, core_r):
        here = Places(1, n_seq)
        own = pltpu.make_async_copy(x, out.at[0], local)
        own.start()
        here.greet(False)
        started = []

        def to_core(source, k, part):
            cut = pl.ds(part * size, size)
            copy = remote(
                source.at[cut],
                out.at[k * CORES + 1, cut],
                core_s.at[k, part],
                core_r.at[k, part],
                {"seq": here.seq(0, 1)},
            )
            copy.start()
            started.append(copy)

        def over(k, part):
            cut = pl.ds(part * size, size)
            return remote(
                x.at[cut],
                out.at[k * CORES, cut],
                y_s.at[k, part],
                y_r.at[k, part],
                {"seq": here.seq(-k, 0)},
            )

        for part in range(parts):
            for k in range(1, chips):
                copy = over(k, part)
                copy.start()
                started.append(copy)
            to_core(x, 0, part)
        for part in range(parts):
            for k in range(1, chips):
                over(k, part).wait_recv()
                to_core(out.at[k * CORES], k, part)
        for part in range(parts):
            for k in range(chips):
                cut = pl.ds(part * size, size)
                block = out.at[k * CORES + 1, cut]
                remote(
                    block, block, core_s.at[k, part], core_r.at[k, part], {"seq": here.seq(0, 1)}
                ).wait_recv()
        for copy in started:
            copy.wait_send()
        own.wait()

    sems = pltpu.SemaphoreType.DMA
    return pl.pallas_call(
        body,
        out_shape=jax.ShapeDtypeStruct((n_seq,) + block.shape, block.dtype),
        in_specs=[ANY],
        out_specs=ANY,
        scratch_shapes=[sems(())] + [sems((chips, parts))] * 4,
        compiler_params=params(number),
    )(block)


def scatter_group(terms, number):
    n_seq, rows, columns = terms.shape
    chips = n_seq // CORES
    parts = 4 if rows % 64 == 0 else 1
    size = rows // parts

    def body(x, out, near, sums, far, y_s, y_r, core_s, core_r):
        here = Places(1, n_seq)
        here.greet(False)
        started = []

        def cross(k, part):
            cut = pl.ds(part * size, size)
            return remote(
                x.at[k * CORES + 1, cut],
                near.at[k, cut],
                core_s.at[k, part],
                core_r.at[k, part],
                {"seq": here.seq(0, 1)},
            )

        def over(k, part):
            cut = pl.ds(part * size, size)
            return remote(
                sums.at[k, cut],
                far.at[k, cut],
                y_s.at[k, part],
                y_r.at[k, part],
                {"seq": here.seq(k, 0)},
            )

        for k in [*range(1, chips), 0]:
            for part in range(parts):
                copy = cross(k, part)
                copy.start()
                started.append(copy)
        for k in range(1, chips):
            for part in range(parts):
                cut = pl.ds(part * size, size)
                cross(k, part).wait_recv()
                total = x[k * CORES, cut, :].astype(wide) + near[k, cut, :].astype(wide)
                sums[k, cut, :] = total.astype(low)
                copy = over(k, part)
                copy.start()
                started.append(copy)
        for part in range(parts):
            cut = pl.ds(part * size, size)
            cross(0, part).wait_recv()
            out[cut, :] = x[0, cut, :].astype(wide) + near[0, cut, :].astype(wide)
        for part in range(parts):
            cut = pl.ds(part * size, size)
            for k in range(1, chips):
                over(k, part).wait_recv()
                out[cut, :] = out[cut, :] + far[k, cut, :].astype(wide)
        for copy in started:
            copy.wait_send()

    sems = pltpu.SemaphoreType.DMA
    buffer = pltpu.VMEM((chips, rows, columns), low)
    return pl.pallas_call(
        body,
        out_shape=jax.ShapeDtypeStruct((rows, columns), wide),
        in_specs=[VMEM],
        out_specs=VMEM,
        scratch_shapes=[buffer] * 3 + [sems((chips, parts))] * 4,
        compiler_params=params(number),
    )(terms)


def scatter_whole(packs, block, small, number, n_seq):
    wanted = [pack.shape[2] for pack in packs]
    gaps = [-count % (128 * CORES) for count in wanted]
    packs = [
        jnp.pad(pack, ((0, 0), (0, 0), (0, gap))) if gap else pack
        for pack, gap in zip(packs, gaps, strict=True)
    ]
    n_f, count = packs[0].shape[0], len(packs)
    chips = n_seq // CORES
    widths = [pack.shape[2] // CORES for pack in packs]
    steps = ring_steps(n_f)
    offsets = [way * step for step, way in reversed(steps)] + [0]
    last = {way: max(step for step, w in steps if w == way) for way in (1, -1)}

    def body(*refs):
        refs = list(refs)

        def take(n):
            taken, refs[:] = refs[:n], refs[n:]
            return taken

        xs = take(count)
        block_in, small_in = take(2)
        outs = take(count)
        block_out, small_out = take(2)
        nears, terms, moves, parts = (take(count) for _ in range(4))
        (smalls,) = take(1)
        core_s, core_r, ring_s, ring_r, y_s, y_r, side_s, side_r = take(8)
        local, far_s, far_r, near_s, near_r = take(5)
        here = Places(n_f, n_seq)
        own = pltpu.make_async_copy(block_in, block_out.at[0], local)
        own.start()
        smalls[here.me] = small_in[...]
        here.greet(True)
        started = []

        def flip(j):
            return 1 if j == 0 else -1

        def go(copy):
            copy.start()
            started.append(copy)

        def share(j, spot):
            return pl.ds(pl.multiple_of(spot * widths[j], 128), widths[j])

        other = lax.rem(here.core + 1, CORES)

        def cross(j, i):
            return remote(
                xs[j].at[here.at(flip(j) * offsets[i]), :, share(j, other)],
                nears[j].at[i],
                core_s.at[j, i],
                core_r.at[j, i],
                {"seq": here.seq(0, 1)},
            )

        def hop(j, step, way):
            at = steps.index((step, way))
            return remote(
                terms[j].at[at],
                moves[j].at[at],
                ring_s.at[j, at],
                ring_r.at[j, at],
                {"fsdp": here.at(flip(j) * way)},
            )

        def swap(j, k, spot):
            slot = parts[j].at[spot]
            return remote(slot, slot, y_s.at[j, k], y_r.at[j, k], {"seq": here.seq(-k, 0)})

        def far_block(k):
            return remote(
                block_in, block_out.at[k * CORES], far_s.at[k], far_r.at[k], {"seq": here.seq(-k, 0)}
            )

        def near_block(k):
            source = block_in if k == 0 else block_out.at[k * CORES]
            return remote(
                source,
                block_out.at[k * CORES + 1],
                near_s.at[k],
                near_r.at[k],
                {"seq": here.seq(0, 1)},
            )

        def far_small(k, spot):
            slot = smalls.at[spot]
            return remote(
                slot, slot, far_s.at[chips + k], far_r.at[chips + k], {"seq": here.seq(-k, 0)}
            )

        def near_small(k, spot):
            slot = smalls.at[spot]
            return remote(
                slot, slot, near_s.at[chips + k], near_r.at[chips + k], {"seq": here.seq(0, 1)}
            )

        for k in range(1, chips):
            go(far_small(k, here.me))
            go(far_block(k))
        for i in range(n_f):
            for j in range(count):
                go(cross(j, i))
        go(near_small(0, here.me))
        go(near_block(0))
        for i in range(n_f):
            for j in range(count):
                cross(j, i).wait_recv()
                total = xs[j][here.at(flip(j) * offsets[i]), :, share(j, here.core)].astype(wide)
                total = total + nears[j][i].astype(wide)
                if offsets[i]:
                    step, way = abs(offsets[i]), 1 if offsets[i] > 0 else -1
                    if step < last[way]:
                        hop(j, step + 1, way).wait_recv()
                        total = total + moves[j][steps.index((step + 1, way))].astype(wide)
                    terms[j][steps.index((step, way))] = total.astype(low)
                    go(hop(j, step, way))
                else:
                    for way in (1, -1):
                        if last[way] >= 1:
                            hop(j, 1, way).wait_recv()
                            total = total + moves[j][steps.index((1, way))].astype(wide)
                    parts[j][here.y] = total.astype(low)
                    for k in range(1, chips):
                        go(swap(j, k, here.y))

        def side(j, core):
            columns = outs[j].at[:, share(j, core)]
            return remote(columns, columns, side_s.at[j], side_r.at[j], {"seq": here.seq(0, 1)})

        for k in range(1, chips):
            far_small(k, here.seq(k, 0)).wait_recv()
            go(near_small(k, here.seq(k, 0)))
            far_block(k).wait_recv()
            go(near_block(k))
        for j in range(count):
            for k in range(1, chips):
                swap(j, k, lax.rem(here.y + k, chips)).wait_recv()
            total = parts[j][0].astype(wide)
            for y in range(1, chips):
                total = total + parts[j][y].astype(wide)
            outs[j][:, share(j, here.core)] = total.astype(low)
            go(side(j, here.core))
        for k in range(chips):
            near_small(k, here.seq(k, 1)).wait_recv()
        total = smalls[0].astype(wide)
        for spot in range(1, n_seq):
            total = total + smalls[spot].astype(wide)
        small_out[...] = total
        for k in range(chips):
            near_block(k).wait_recv()
        for j in range(count):
            side(j, other).wait_recv()
        for copy in started:
            copy.wait_send()
        own.wait()

    sems = pltpu.SemaphoreType.DMA
    shapes = [(pack.shape[1], width) for pack, width in zip(packs, widths, strict=True)]
    near = [pltpu.VMEM((n_f, *shape), low) for shape in shapes]
    ring = [pltpu.VMEM((len(steps), *shape), low) for shape in shapes]
    part = [pltpu.VMEM((chips, *shape), low) for shape in shapes]
    results = pl.pallas_call(
        body,
        out_shape=tuple(jax.ShapeDtypeStruct(pack.shape[1:], low) for pack in packs)
        + (
            jax.ShapeDtypeStruct((n_seq, *block.shape), low),
            jax.ShapeDtypeStruct(small.shape, wide),
        ),
        in_specs=[VMEM] * count + [ANY, VMEM],
        out_specs=(VMEM,) * count + (ANY, VMEM),
        scratch_shapes=near
        + ring * 2
        + part
        + [pltpu.VMEM((n_seq, *small.shape), low)]
        + [sems((count, n_f))] * 2
        + [sems((count, len(steps)))] * 2
        + [sems((count, chips))] * 2
        + [sems((count,))] * 2
        + [sems(())]
        + [sems((2 * chips,))] * 4,
        compiler_params=params(number),
    )(*packs, block, small)
    sums = [result[:, :size] for result, size in zip(results[:count], wanted, strict=True)]
    return sums, results[count], results[count + 1]


def ring_terms(sides, outs, n_f, n_seq, dtype):
    flat, spots = [], []
    left = 0
    for side in sides:
        top = 0
        for part in side:
            flat.append(part)
            spots.append((top, left))
            top += part.shape[1]
        left += side[0].shape[2]
    moved = [block for _, _, _, came in outs for block, _ in came]

    def body(*refs):
        parts, moves = refs[: len(flat)], list(refs[len(flat) : len(flat) + len(moved)])
        results = refs[len(flat) + len(moved) : len(flat) + len(moved) + len(outs)]
        scratch, sem = refs[len(flat) + len(moved) + len(outs) : -1], refs[-1]
        here = Places(n_f, n_seq)
        copies = []
        for i, (offset, first, stop, _) in enumerate(outs):
            owner = here.at(offset)
            for at, (part, (above, before)) in enumerate(zip(parts, spots, strict=True)):
                start, end = max(first, before), min(stop, before + part.shape[2])
                if start < end:
                    copies.append(
                        pltpu.make_async_copy(
                            part.at[owner, :, start - before : end - before],
                            scratch[i].at[
                                above : above + part.shape[1], start - first : end - first
                            ],
                            sem.at[i, at],
                        )
                    )
        for copy in copies:
            copy.start()
        for copy in copies:
            copy.wait()
        for i, (_, first, stop, came) in enumerate(outs):
            edges = sorted(
                {first, stop}
                | {c for _, c in came}
                | {c + block.shape[1] for block, c in came}
            )
            here_moves = [(moves.pop(0), c) for _, c in came]
            for start, end in zip(edges, edges[1:]):
                total = scratch[i][:, start - first : end - first].astype(wide)
                for ref, c in here_moves:
                    if c <= start and end <= c + ref.shape[1]:
                        total = total + ref[:, start - c : end - c].astype(wide)
                results[i][:, start - first : end - first] = total.astype(dtype)

    rows = sum(part.shape[1] for part in sides[0])
    shapes = [(rows, stop - first) for _, first, stop, _ in outs]
    return pl.pallas_call(
        body,
        out_shape=tuple(jax.ShapeDtypeStruct(shape, dtype) for shape in shapes),
        in_specs=[ANY] * len(flat) + [VMEM] * len(moved),
        out_specs=(VMEM,) * len(outs),
        scratch_shapes=[pltpu.VMEM(shape, low) for shape in shapes]
        + [pltpu.SemaphoreType.DMA((len(outs), len(flat)))],
        cost_estimate=brief(1),
        compiler_params=pltpu.CompilerParams(vmem_limit_bytes=32 * 2**20),
    )(*flat, *moved)


class Ring:
    def __init__(self, count, width):
        self.count = count
        walk = ring_order(count, width)
        self.up = [(walk[i], walk[(i + 1) % count]) for i in range(count)]
        self.down = [(b, a) for a, b in self.up]

    def hop(self, block, way):
        return lax.ppermute(block, "fsdp", self.up if way > 0 else self.down)


class Gathering:
    def __init__(self, ring, block):
        self.ring = ring
        self.step, self.steps = 0, ring.count // 2
        self.moving = (block, block)
        self.places = [(0, 0)]
        self.blocks = [block]

    def advance(self):
        if self.step == self.steps:
            return
        self.step += 1
        first, second = self.moving
        if self.step < self.steps:
            self.moving = (self.ring.hop(first, 1), self.ring.hop(second, -1))
            self.places += [(-self.step, 0), (self.step, 0)]
        else:
            half = first.shape[1] // 256 * 128
            self.moving = (
                self.ring.hop(first[:, :half], 1),
                self.ring.hop(second[:, half:], -1),
            )
            self.places += [(self.step, 0), (self.step, half)]
        self.blocks += list(self.moving)

    def done(self):
        while self.step < self.steps:
            self.advance()
        return [
            (offset, block, column)
            for (offset, column), block in zip(self.places, self.blocks, strict=True)
        ]

    def live(self):
        return (self.moving, self.blocks)

    def restore(self, live):
        self.moving, self.blocks = live


class Scattering:
    def __init__(self, ring, sides, n_seq):
        self.ring, self.sides, self.n_seq = ring, sides, n_seq
        self.width = sum(side[0].shape[2] for side in sides)
        self.half = self.width // 256 * 128
        self.step, self.steps = 0, ring.count // 2
        self.moving = ()

    def terms(self, outs, dtype):
        return ring_terms(self.sides, outs, self.ring.count, self.n_seq, dtype)

    def advance(self):
        if self.step == self.steps:
            return
        self.step += 1
        offset = self.steps - self.step + 1
        if self.step == 1:
            outs = [(offset, 0, self.half, []), (offset, self.half, self.width, [])]
        else:
            ahead, back = self.moving
            right = self.half if self.step == 2 else 0
            outs = [
                (offset, 0, self.width, [(ahead, 0)]),
                (-offset, 0, self.width, [(back, right)]),
            ]
        ahead, back = self.terms(outs, low)
        self.moving = (self.ring.hop(ahead, 1), self.ring.hop(back, -1))

    def done(self, dtype):
        while self.step < self.steps:
            self.advance()
        right = self.half if self.steps == 1 else 0
        ahead, back = self.moving
        (total,) = self.terms([(0, 0, self.width, [(ahead, 0), (back, right)])], dtype)
        return total

    def live(self):
        return self.moving

    def restore(self, live):
        self.moving = live


def tie(movers, values):
    lives, values = lax.optimization_barrier(([mover.live() for mover in movers], values))
    for mover, live in zip(movers, lives, strict=True):
        mover.restore(live)
    return values


class Group:
    def __init__(self, count):
        self.count = count
        self.chips = count // CORES
        me = lax.axis_index("seq")
        self.y, self.core = me // CORES, lax.rem(me, CORES)
        self.sibling = [(i, i ^ 1) for i in range(count)]
        self.order = [(k, c) for k in range(self.chips) for c in range(CORES)]

    def shift(self, k):
        n = self.chips
        return [(i, ((i // CORES + k) % n) * CORES + i % CORES) for i in range(self.count)]

    def index(self, k, c):
        return lax.rem(self.y + k, self.chips) * CORES + (self.core + c) % CORES

    def over(self, block):
        return [block] + [
            lax.ppermute(block, "seq", self.shift(-k)) for k in range(1, self.chips)
        ]

    def across(self, blocks):
        out = []
        for block in blocks:
            out += [block, lax.ppermute(block, "seq", self.sibling)]
        return out

    def swap(self, block):
        return lax.ppermute(block, "seq", self.sibling)

    def cross(self, terms):
        return [
            lax.ppermute(terms[k * CORES + 1], "seq", self.sibling) for k in range(self.chips)
        ]

    def send(self, sums):
        return [
            lax.ppermute(sums[k].astype(low), "seq", self.shift(k)) for k in range(1, self.chips)
        ]

    def laid(self, pieces, axis, dtype):
        width = pieces[0].shape[axis]
        shape = list(pieces[0].shape)
        shape[axis] = width * self.count
        out = jnp.zeros(shape, dtype)
        for (k, c), piece in zip(self.order, pieces, strict=True):
            out = lax.dynamic_update_slice_in_dim(
                out, piece.astype(dtype), self.index(k, c) * width, axis
            )
        return out


class Summing:
    def __init__(self, values, axes):
        self.values = values
        self.steps = [
            (axis, 1 << bit)
            for axis in axes
            for bit in range((lax.axis_size(axis) - 1).bit_length())
        ]
        assert all(lax.axis_size(axis) & (lax.axis_size(axis) - 1) == 0 for axis in axes)

    def advance(self):
        if self.steps:
            axis, step = self.steps.pop(0)
            pairs = [(i, i ^ step) for i in range(lax.axis_size(axis))]
            self.values = self.values + lax.ppermute(self.values, axis, pairs)

    def done(self):
        while self.steps:
            self.advance()
        return self.values

    def live(self):
        return self.values

    def restore(self, live):
        self.values = live


def cut_columns(weights, raises, gains, n_f, n_seq, slab):
    rows, ff = weights[0].shape
    rank_rows = raises[0].shape[0]
    block, cut = ff // n_f, ff // (n_f * n_seq)

    def body(gain_ref, w0, w1, r0, r1, out):
        me = lax.axis_index("seq")

        def run(ref, spot):
            runs = [
                ref[:, f * block + spot * cut : f * block + (spot + 1) * cut] for f in range(n_f)
            ]
            gap = slab - n_f * cut
            if gap:
                runs.append(jnp.zeros((ref.shape[0], gap), ref.dtype))
            return jnp.concatenate(runs, axis=1)

        for spot in range(n_seq):

            @pl.when(me == spot)
            def _():
                for side, (weight, raised) in enumerate(((w0, r0), (w1, r1))):
                    at = side * slab
                    out[:rank_rows, at : at + slab] = run(raised, spot)
                    scaled = run(weight, spot).astype(wide) * gain_ref[...]
                    out[rank_rows:, at : at + slab] = scaled.astype(low)

    return pl.pallas_call(
        body,
        out_shape=jax.ShapeDtypeStruct((rank_rows + rows, 2 * slab), low),
        compiler_params=pltpu.CompilerParams(vmem_limit_bytes=48 * 2**20),
    )(gains, *weights, *raises)


def place_columns(pieces, gains, n_f, n_seq, rank_rows, ff, slab):
    rows = pieces.shape[1] - rank_rows
    cut = ff // (n_f * n_seq)
    chips = n_seq // CORES

    def body(gain_ref, x, w0, w1, r0, r1):
        me = lax.axis_index("seq")
        y, core = me // CORES, lax.rem(me, CORES)

        def spot_of(spot):
            ahead = lax.rem(spot // CORES - y + chips, chips)
            return ahead * CORES + lax.rem(spot % CORES + core, CORES)

        def fill(out, first, count, at, gain):
            whole = [x[spot_of(spot), first : first + count, at : at + slab] for spot in range(n_seq)]
            runs = [
                whole[spot][:, f * cut : (f + 1) * cut] for f in range(n_f) for spot in range(n_seq)
            ]
            result = jnp.concatenate(runs, axis=1).astype(wide)
            out[...] = result if gain is None else result * gain

        for side, (weight, raised) in enumerate(((w0, r0), (w1, r1))):
            fill(raised, 0, rank_rows, side * slab, None)
            fill(weight, rank_rows, rows, side * slab, gain_ref[...])

    return pl.pallas_call(
        body,
        out_shape=(jax.ShapeDtypeStruct((rows, ff), wide),) * 2
        + (jax.ShapeDtypeStruct((rank_rows, ff), wide),) * 2,
        compiler_params=pltpu.CompilerParams(vmem_limit_bytes=56 * 2**20),
    )(gains, pieces)


def gelu_parts(gate):
    scale = (2.0 / jnp.pi) ** 0.5
    cube = 0.044715
    square = gate * gate
    half = 0.5 * jnp.tanh(gate * (scale + scale * cube * square)) + 0.5
    value = gate * half
    slope = half + value * (1.0 - half) * (2.0 * scale + 6.0 * scale * cube * square)
    return value, slope


def project(unit, side, ups, cosine, sine, hq, rank):
    tokens = unit.shape[0]
    lin = hq + 2 * HD
    half = HD // 2

    def body(x, weights, raises, cos, sin, queries, both, inner):
        low_inner = mul(x[...], weights[:, lin:]).astype(low)
        inner[...] = low_inner

        def head(at, own):
            columns = slice(at, at + HD)
            return mul(x[...], weights[:, columns]) + mul(
                low_inner[:, own * rank : (own + 1) * rank], raises[:, columns]
            )

        def turned(values):
            first, second = values[:, :half], values[:, half:]
            c, s = cos[...], sin[...]
            return jnp.concatenate(
                [first * c - second * s, second * c + first * s], axis=1
            ).astype(low)

        for at in range(0, hq, HD):
            queries[:, at : at + HD] = turned(head(at, 0))
        both[:, :HD] = turned(head(hq, 1))
        both[:, HD:] = head(hq + HD, 2).astype(low)

    return pl.pallas_call(
        body,
        out_shape=(
            jax.ShapeDtypeStruct((tokens, hq), low),
            jax.ShapeDtypeStruct((tokens, 2 * HD), low),
            jax.ShapeDtypeStruct((tokens, 3 * rank), low),
        ),
        cost_estimate=brief(2),
        compiler_params=pltpu.CompilerParams(vmem_limit_bytes=48 * 2**20),
    )(unit, side, ups, cosine, sine)


def attention(queries, both, mask, rows):
    n_seq, tokens, _ = both.shape
    length = tokens // rows
    scale = HD ** (-0.5)

    def body(q, kv, hidden, out, log_total):
        for r in range(rows):
            at = slice(r * length, (r + 1) * length)
            keys = kv[:, at, :HD].reshape(n_seq * length, HD)
            values = kv[:, at, HD:].reshape(n_seq * length, HD)
            for h in range(H):
                head = slice(h * HD, (h + 1) * HD)
                scores = mul_t(q[at, head], keys) * scale + hidden[r]
                top = jnp.max(scores, axis=-1, keepdims=True)
                weights = jnp.exp(scores - top)
                total = jnp.sum(weights, axis=-1, keepdims=True)
                out[at, head] = (mul(weights.astype(low), values) / total).astype(low)
                log_total[r, h] = top + jnp.log(total)

    return pl.pallas_call(
        body,
        out_shape=(
            jax.ShapeDtypeStruct(queries.shape, low),
            jax.ShapeDtypeStruct((rows, H, length, 1), wide),
        ),
        cost_estimate=brief(2),
        compiler_params=pltpu.CompilerParams(vmem_limit_bytes=48 * 2**20),
    )(queries, both, mask)


def attention_back(queries, both, mask, log_total, out, g_out, cosine, sine, rows):
    n_seq, tokens, _ = both.shape
    length = tokens // rows
    scale = HD ** (-0.5)
    half = HD // 2

    def body(q, kv, hidden, logs, o, g, cos, sin, g_q, g_both):
        for r in range(rows):
            at = slice(r * length, (r + 1) * length)
            keys = kv[:, at, :HD].reshape(n_seq * length, HD)
            values = kv[:, at, HD:].reshape(n_seq * length, HD)
            d_keys = d_values = None
            for h in range(H):
                head = slice(h * HD, (h + 1) * HD)
                scores = mul_t(q[at, head], keys) * scale + hidden[r]
                probs = jnp.exp(scores - logs[r, h])
                grad = g[at, head]
                dots = jnp.sum(
                    grad.astype(wide) * o[at, head].astype(wide), axis=-1, keepdims=True
                )
                d_scores = (probs * (mul_t(grad, values) - dots)).astype(low)
                d_query = mul(d_scores, keys) * scale
                first, second = d_query[:, :half], d_query[:, half:]
                c, s = cos[at, :], sin[at, :]
                turned = jnp.concatenate([first * c + second * s, second * c - first * s], axis=1)
                g_q[at, head] = turned.astype(low)
                d_key = t_mul(d_scores, q[at, head])
                d_value = t_mul(probs.astype(low), grad)
                d_keys = d_key if d_keys is None else d_keys + d_key
                d_values = d_value if d_values is None else d_values + d_value
            g_both[:, at, :HD] = (d_keys * scale).astype(low).reshape(n_seq, length, HD)
            g_both[:, at, HD:] = d_values.astype(low).reshape(n_seq, length, HD)

    return pl.pallas_call(
        body,
        out_shape=(
            jax.ShapeDtypeStruct(queries.shape, low),
            jax.ShapeDtypeStruct(both.shape, low),
        ),
        cost_estimate=brief(3),
        compiler_params=pltpu.CompilerParams(vmem_limit_bytes=56 * 2**20),
    )(queries, both, mask, log_total, out, g_out, cosine, sine)


def by_owner(out, first, product, n_f):
    rows = product.shape[0] // n_f
    for f in range(n_f):
        out[f, first : first + rows, :] = product[f * rows : (f + 1) * rows].astype(low)
    return first + rows


def output_gradients(attn, inner, g_branch, ready, n_f):
    columns = g_branch.shape[1]
    sizes = [part.shape[-2] if part.ndim == 3 else part.shape[1] // n_f for part in (attn, inner, ready)]

    def body(a, b, g, done, out):
        first = by_owner(out, 0, t_mul(a[...], g[...]), n_f)
        first = by_owner(out, first, t_mul(b[...], g[...]), n_f)
        out[:, first:, :] = done[...]

    return pl.pallas_call(
        body,
        out_shape=jax.ShapeDtypeStruct((n_f, sum(sizes), columns), low),
        cost_estimate=brief(2),
        compiler_params=pltpu.CompilerParams(vmem_limit_bytes=40 * 2**20),
    )(attn, inner, g_branch, ready)


def query_gradients(unit, inner, g_q, raises, side, hq, rank, n_f):
    tokens, width = unit.shape
    lin = hq + 2 * HD
    rows = width // n_f + rank // n_f

    def body(x, low_inner, g, ups, weights, e1, out):
        g_inner = mul_t(g[...], ups[:, :hq]).astype(low)
        e1[...] = mul_t(g[...], weights[:, :hq]) + mul_t(g_inner, weights[:, lin : lin + rank])
        first = by_owner(out, 0, t_mul(x[...], g[...]), n_f)
        by_owner(out, first, t_mul(low_inner[...], g[...]), n_f)

    return pl.pallas_call(
        body,
        out_shape=(
            jax.ShapeDtypeStruct((tokens, width), wide),
            jax.ShapeDtypeStruct((n_f, rows, hq), low),
        ),
        cost_estimate=brief(2),
        compiler_params=pltpu.CompilerParams(vmem_limit_bytes=48 * 2**20),
    )(unit, inner, g_q, raises, side)


def lay_rows(pieces, cut_at, n_seq):
    rows, columns = pieces[0].shape
    chips = n_seq // CORES

    def body(*refs):
        me = lax.axis_index("seq")
        y, core = me // CORES, lax.rem(me, CORES)
        for at, ref in enumerate(refs[:n_seq]):
            spot = lax.rem(y + at // CORES, chips) * CORES + lax.rem(core + at % CORES, CORES)
            refs[n_seq][spot] = ref[:, :cut_at].astype(wide)
            refs[n_seq + 1][spot] = ref[:, cut_at:].astype(wide)

    results = pl.pallas_call(
        body,
        out_shape=(
            jax.ShapeDtypeStruct((n_seq, rows, cut_at), wide),
            jax.ShapeDtypeStruct((n_seq, rows, columns - cut_at), wide),
        ),
        cost_estimate=brief(1),
        compiler_params=pltpu.CompilerParams(vmem_limit_bytes=32 * 2**20),
    )(*pieces)
    return [result.reshape(n_seq * rows, -1) for result in results]


def landing(items, buffers, rows_first, sem, here):
    copies = []
    for at, (offset, ref, column) in enumerate(items):
        owner = here.at(offset)
        first = 0
        for part, buffer in enumerate(buffers):
            count = rows_first[part]
            copies.append(
                pltpu.make_async_copy(
                    ref.at[first : first + count],
                    buffer.at[owner, :, column : column + ref.shape[1]],
                    sem.at[at, part],
                )
            )
            first += count
    for copy in copies:
        copy.start()
    for copy in copies:
        copy.wait()


def mlp_forward(
    items, tokens2, adapters, before, part, n_f, n_seq, rank_rows, own_rows, slab
):
    count, width = tokens2.shape
    rank = rank_rows * n_f
    tile = 256 if slab % 256 == 0 else 128
    chunk = 512
    first, stop = part
    wanted = []
    for side in range(2):
        start, end = side * slab + first * tile, side * slab + stop * tile
        for at, (offset, block, column) in enumerate(items):
            low_end, high_end = max(start, column), min(end, column + block.shape[1])
            if low_end < high_end:
                wanted.append((at, offset, low_end - column, high_end - column, side, low_end - start))
    adapters = [a.reshape(n_f, own_rows, rank) for a in adapters]

    def body(x, lower_g, lower_u, *refs):
        blocks, refs = refs[: len(items)], refs[len(items) + len(before) :]
        hidden, back_g, back_u, full_g, full_u, raised_g, raised_u = refs[:7]
        raises, weights, merged, sem = refs[7:]
        here = Places(n_f, n_seq)
        step = pl.program_id(0)

        @pl.when(step == 0)
        def _():
            copies = []
            for number, (at, offset, start, end, side, column) in enumerate(wanted):
                owner = here.at(offset)
                for which, (buffer, rows) in enumerate(
                    (
                        (raises, slice(0, rank_rows)),
                        (weights, slice(rank_rows, rank_rows + own_rows)),
                    )
                ):
                    copies.append(
                        pltpu.make_async_copy(
                            blocks[at].at[rows, start:end],
                            buffer.at[side, owner, :, column : column + end - start],
                            sem.at[number, which],
                        )
                    )
            for copy in copies:
                copy.start()
            for copy in copies:
                copy.wait()

        for side, (lower, full, raised) in enumerate(
            ((lower_g, full_g, raised_g), (lower_u, full_u, raised_u))
        ):
            columns = pl.ds(pl.multiple_of(step * tile, 128), tile)
            up_matrix = raises[side, :, :, columns].reshape(rank, tile)
            raised[...] = up_matrix
            for f in range(n_f):
                total = weights[side, f, :, columns].astype(wide) + mul(lower[f], up_matrix)
                total = total.astype(low)
                full[f] = total
                merged[side, f * own_rows : (f + 1) * own_rows, :] = total

        def some(i, carry):
            at = pl.ds(pl.multiple_of(i * chunk, chunk), chunk)
            gate = mul(x[at, :], merged[0])
            up = mul(x[at, :], merged[1])
            value, slope = gelu_parts(gate)
            hidden[at, :] = (value * up).astype(low)
            back_g[at, :] = (up * slope).astype(low)
            back_u[at, :] = value.astype(low)
            return carry

        lax.fori_loop(0, count // chunk, some, 0, unroll=True)

    by_column = pl.BlockSpec((count, tile), lambda j: (0, j + first))
    by_weight = pl.BlockSpec((n_f, own_rows, tile), lambda j: (0, 0, j + first))
    by_raise = pl.BlockSpec((rank, tile), lambda j: (0, j + first))
    return pl.pallas_call(
        body,
        grid=(stop - first,),
        out_shape=(jax.ShapeDtypeStruct((count, slab), low),) * 3
        + (jax.ShapeDtypeStruct((n_f, own_rows, slab), low),) * 2
        + (jax.ShapeDtypeStruct((rank, slab), low),) * 2,
        in_specs=[VMEM] * 3 + [ANY] * (len(items) + len(before)),
        input_output_aliases={3 + len(items) + i: i for i in range(len(before))},
        out_specs=(by_column,) * 3 + (by_weight,) * 2 + (by_raise,) * 2,
        scratch_shapes=[
            pltpu.VMEM((2, n_f, rank_rows, (stop - first) * tile), low),
            pltpu.VMEM((2, n_f, own_rows, (stop - first) * tile), low),
            pltpu.VMEM((2, width, tile), low),
            pltpu.SemaphoreType.DMA((len(wanted), 2)),
        ],
        cost_estimate=brief(3),
        compiler_params=pltpu.CompilerParams(vmem_limit_bytes=56 * 2**20),
    )(tokens2, *adapters, *(block for _, block, _ in items), *before)


def mlp_backward(items, d_raise, g_tokens, back_g, back_u, n_f, n_seq, cut, slab):
    count, width = g_tokens.shape
    rank = d_raise.shape[0]
    tile = 256 if slab % 256 == 0 else 128
    chunk = 512
    offsets = [(offset, column) for offset, _, column in items]

    def body(g, raised, mul_g, mul_u, *refs):
        blocks = refs[: len(items)]
        grad_g, grad_u, full, raw, merged, sem = refs[len(items) :]
        here = Places(n_f, n_seq)
        step = pl.program_id(0)

        @pl.when(step == 0)
        def _():
            landing(
                [(o, ref, c) for (o, c), ref in zip(offsets, blocks, strict=True)],
                (raw,),
                (cut,),
                sem,
                here,
            )
            for f in range(n_f):
                merged[f * cut : (f + 1) * cut, :] = raw[f, :, :width].astype(wide) + mul(
                    raw[f, :, width:], raised[...]
                )
            if slab > n_f * cut:
                merged[n_f * cut :, :] = jnp.zeros((slab - n_f * cut, width), wide)

        weight = merged[pl.ds(pl.multiple_of(step * tile, tile), tile), :].astype(low)
        full[...] = weight

        def some(i, carry):
            at = pl.ds(pl.multiple_of(i * chunk, chunk), chunk)
            g_hidden = mul_t(g[at, :], weight)
            grad_g[at, :] = (g_hidden * mul_g[at, :].astype(wide)).astype(low)
            grad_u[at, :] = (g_hidden * mul_u[at, :].astype(wide)).astype(low)
            return carry

        lax.fori_loop(0, count // chunk, some, 0, unroll=True)

    by_column = pl.BlockSpec((count, tile), lambda j: (0, j))
    return pl.pallas_call(
        body,
        grid=(slab // tile,),
        out_shape=(jax.ShapeDtypeStruct((count, slab), low),) * 2
        + (jax.ShapeDtypeStruct((slab, width), low),),
        in_specs=[VMEM] * 2 + [by_column] * 2 + [ANY] * len(items),
        out_specs=(by_column,) * 2 + (pl.BlockSpec((tile, width), lambda j: (j, 0)),),
        scratch_shapes=[
            pltpu.VMEM((n_f, cut, width + rank), low),
            pltpu.VMEM((slab, width), wide),
            pltpu.SemaphoreType.DMA((len(items), 1)),
        ],
        cost_estimate=brief(3),
        compiler_params=pltpu.CompilerParams(vmem_limit_bytes=56 * 2**20),
    )(g_tokens, d_raise, back_g, back_u, *(block for _, block, _ in items))


def shards(
    inputs,
    cotangent,
    segments,
    exits,
    confidence,
    attn_gain,
    q_weight,
    k_weight,
    v_weight,
    o_weight,
    q_down,
    q_up,
    k_down,
    k_up,
    v_down,
    v_up,
    o_down,
    o_up,
    mlp_gain,
    gate_weight,
    up_weight,
    down_weight,
    gate_down,
    gate_up,
    up_down,
    up_up,
    down_down,
    down_up,
):
    n_seq, n_f = lax.axis_size("seq"), lax.axis_size("fsdp")
    me = lax.axis_index("seq")
    ring = Ring(n_f, n_seq // CORES)
    group = Group(n_seq)
    rows, length, width = inputs.shape
    tokens = rows * length
    rank = q_down.shape[1]
    hq = q_weight.shape[1]
    ff = gate_weight.shape[1]
    own_rows = q_weight.shape[0]
    rank_rows = q_up.shape[0]
    o_rows = o_weight.shape[0]
    cut = ff // (n_f * n_seq)
    slab = -(-n_f * cut // 128) * 128
    scale = HD ** (-0.5)

    gain1 = attn_gain.astype(wide)[:, None]
    gain2 = mlp_gain.astype(wide)[:, None]

    def rows_of(array):
        part = array.shape[0] // n_seq
        return lax.dynamic_slice_in_dim(array, me * part, part, 0)

    small_blocks = pack_small(
        gain1,
        gain2,
        (q_weight, k_weight, v_weight, q_down, k_down, v_down),
        (gate_down, up_down),
        (q_up, k_up, v_up),
        (o_up, down_up),
        (o_weight, o_down),
        n_seq,
    )

    slabs = Gathering(
        ring, cut_columns((gate_weight, up_weight), (gate_up, up_up), gain2, n_f, n_seq, slab)
    )
    d_lower = rows_of(down_down)
    downs = Gathering(ring, jnp.concatenate([rows_of(down_weight), d_lower], axis=1))

    depth_ids = jnp.arange(DEPTHS, dtype=jnp.int32)
    matches = (exits.reshape(tokens)[:, None] == depth_ids[None, :]).astype(wide)
    counted = Summing(
        jnp.concatenate(
            [jnp.sum(matches, axis=0), jnp.sum(matches * confidence.reshape(tokens)[:, None], axis=0)]
        ),
        ("seq", "fsdp"),
    )
    resid = inputs.reshape(tokens, width).astype(wide)
    active = (exits.reshape(tokens) >= LOOP).astype(wide)[:, None]
    cot = cotangent.reshape(tokens, width).astype(wide)
    g_mlp = (active * cot).astype(low)
    places = me * length + jnp.arange(length, dtype=jnp.int32)
    frequency = rope_base ** (-2.0 * jnp.arange(HD // 2, dtype=wide) / HD)
    angles = jnp.tile(places, rows).astype(wide)[:, None] * frequency[None, :]
    cosine, sine = jnp.cos(angles), jnp.sin(angles)
    r1 = lax.rsqrt(jnp.mean(resid * resid, axis=-1, keepdims=True) + epsilon)
    unit1 = (resid * r1).astype(low)

    slabs.advance()
    seg_pieces = group.over(segments.astype(low))
    whole = gather_whole(small_blocks, (False, False, True, True, True), 0, n_f, n_seq)
    whole, seg_pieces, unit1, cosine, sine, g_mlp = tie(
        (slabs, downs), (whole, seg_pieces, unit1, cosine, sine, g_mlp)
    )
    qkv_side, ups, side_o, ups2, adapters = (part.reshape(-1, part.shape[2]) for part in whole)
    kv = HD
    lin = hq + 2 * kv
    gate_adapter, up_adapter = adapters[:, :rank], adapters[:, rank : 2 * rank]
    side_o = side_o[:, : width + rank]
    q_raise, k_raise, v_raise = ups[:, :hq], ups[:, hq : hq + kv], ups[:, hq + kv : lin]
    o_raise, d_raise = ups2[:, :width], ups2[:, width : 2 * width]

    slabs.advance()
    seg_pieces = group.across(seg_pieces)
    half = HD // 2
    queries, both, inner = project(unit1, qkv_side, ups, cosine, sine, hq, rank)
    both = gather_group(both, 2, n_seq)
    key_seg = jnp.concatenate(seg_pieces, axis=1).astype(jnp.int32)
    key_place = jnp.concatenate(
        [
            group.index(k, c) * length + jnp.arange(length, dtype=jnp.int32)
            for k, c in group.order
        ]
    )
    allowed = (segments[:, :, None] == key_seg[:, None, :]) & (
        key_place[None, None, :] <= places[None, :, None]
    )
    mask = jnp.where(allowed, 0.0, -1e30).astype(wide)
    both, queries, mask, inner, g_mlp = tie((slabs,), (both, queries, mask, inner, g_mlp))
    q_inner, k_inner, v_inner = inner[:, :rank], inner[:, rank : 2 * rank], inner[:, 2 * rank :]

    slabs.advance()
    g_mlp = group.over(g_mlp)
    attn_low, log_total = attention(queries, both, mask, rows)
    projected = mul(attn_low, side_o)
    o_inner = projected[:, width:].astype(low)
    mid = resid + active * (projected[:, :width] + mul(o_inner, o_raise))
    r2 = lax.rsqrt(jnp.mean(mid * mid, axis=-1, keepdims=True) + epsilon)
    unit2 = (mid * r2).astype(low)
    unit2, mid, r2, g_mlp, attn_low, o_inner, log_total = tie(
        (slabs,), (unit2, mid, r2, g_mlp, attn_low, o_inner, log_total)
    )

    slabs.advance()
    downs.advance()
    unit2 = gather_group(unit2, 3, n_seq).reshape(-1, width)
    unit2, g_mlp = tie((slabs, downs), (unit2, g_mlp))

    downs.advance()
    g_mlp = group.across(g_mlp)
    tiles = slab // (256 if slab % 256 == 0 else 128)
    arrived = slabs.done()

    def forward(first, stop, before):
        return mlp_forward(
            arrived,
            unit2,
            (gate_adapter, up_adapter),
            before,
            (first, stop),
            n_f,
            n_seq,
            rank_rows,
            own_rows,
            slab,
        )

    half_way = forward(0, (tiles + 1) // 2, ())
    half_way, g_mlp = tie((downs,), (half_way, g_mlp))
    downs.advance()
    counted.advance()
    hidden, back_g, back_u, gate_full, up_full, g_raise, u_raise = forward(
        (tiles + 1) // 2, tiles, half_way
    )
    hidden, back_g, back_u, g_mlp = tie((downs, counted), (hidden, back_g, back_u, g_mlp))
    g_mlp = jnp.concatenate(g_mlp, axis=0)

    downs.advance()
    counted.advance()
    g_down = t_mul(hidden, g_mlp).astype(low)
    g_down, g_mlp, back_g, back_u = tie((downs, counted), (g_down, g_mlp, back_g, back_u))

    down_sums = Scattering(ring, [[g_down[: n_f * cut].reshape(n_f, cut, width)]], n_seq)

    down_sums.advance()
    counted.advance()
    g_gate, g_up, down_full = mlp_backward(
        downs.done(), d_raise, g_mlp, back_g, back_u, n_f, n_seq, cut, slab
    )
    g_gate, g_up, down_full = tie((down_sums, counted), (g_gate, g_up, down_full))

    down_sums.advance()
    counted.advance()
    gg = t_mul(unit2, g_gate).astype(low)
    gg_raise = t_mul(gate_adapter, gg).astype(low)
    gg, gg_raise, g_gate, g_up, unit2 = tie(
        (down_sums, counted), (gg, gg_raise, g_gate, g_up, unit2)
    )
    down_sums.advance()
    gu = t_mul(unit2, g_up).astype(low)
    gu_raise = t_mul(up_adapter, gu).astype(low)
    gg, gu, gg_raise, gu_raise, g_gate, g_up = tie(
        (down_sums,), (gg, gu, gg_raise, gu_raise, g_gate, g_up)
    )
    slab_sums = Scattering(
        ring,
        [
            [part.reshape(n_f, -1, slab) for part in side]
            for side in ((gg_raise, gg), (gu_raise, gu))
        ],
        n_seq,
    )
    chips = range(n_seq // CORES)
    here_tokens = CORES * tokens

    def token_gradient(at):
        result = mul_t(g_gate[at], gate_full.reshape(width, slab))
        return (result + mul_t(g_up[at], up_full.reshape(width, slab))).astype(low)

    slab_sums.advance()
    e2_there = token_gradient(slice(here_tokens, None))
    g_down = down_sums.done(low)
    down_rows = jnp.concatenate([g_down, mul_t(g_down, d_raise).astype(low)], axis=1)
    gd_raise = t_mul(d_lower, g_down).astype(low)
    e2_there, g_gate, g_up, down_rows, gd_raise = tie(
        (slab_sums,), (e2_there, g_gate, g_up, down_rows, gd_raise)
    )

    slab_sums.advance()
    there = [e2_there[i * tokens : (i + 1) * tokens] for i in range(n_seq - CORES)]
    e2_near = [group.swap(there[(k - 1) * CORES + 1]) for k in chips[1:]]
    down_rows = group.over(down_rows)
    e2_here = token_gradient(slice(0, here_tokens))
    e2_here, e2_near, hidden, down_rows = tie((slab_sums,), (e2_here, e2_near, hidden, down_rows))

    slab_sums.advance()
    e2_sums = [
        there[(k - 1) * CORES].astype(wide) + e2_near[k - 1].astype(wide) for k in chips[1:]
    ]
    e2_far = group.send([None, *e2_sums])
    e2_own = group.swap(e2_here[tokens:])
    branch = mul(hidden, down_full).astype(low)
    branch, e2_far, e2_own, e2_here = tie((slab_sums,), (branch, e2_far, e2_own, e2_here))
    terms = [branch[i * tokens : (i + 1) * tokens] for i in range(n_seq)]
    e2 = e2_here[:tokens].astype(wide) + e2_own.astype(wide)
    for block in e2_far:
        e2 = e2 + block.astype(wide)

    slab_sums.advance()
    near = group.cross(terms)
    g_mid = cot + r2 * e2 - mid * (r2 * r2 * r2 * jnp.mean(e2 * mid, axis=-1, keepdims=True))
    g_branch = (active * g_mid).astype(low)
    g_inner = mul_t(g_branch, o_raise).astype(low)
    g_attn = mul_t(jnp.concatenate([g_branch, g_inner], axis=1), side_o).astype(low)
    g_attn, terms, near, g_mid, g_branch, down_rows = tie(
        (slab_sums,), (g_attn, terms, near, g_mid, g_branch, down_rows)
    )

    down_rows = group.across(down_rows)
    sums = [terms[k * CORES].astype(wide) + near[k].astype(wide) for k in chips]
    middle = tokens // 2
    far_first = group.send([block[:middle] for block in sums])
    g_q, d_terms = attention_back(
        queries, both, mask, log_total, attn_low, g_attn, cosine, sine, rows
    )
    o_pack = output_gradients(
        attn_low, o_inner, g_branch, gd_raise.reshape(n_f, rank_rows, width), n_f
    )
    d_terms, g_q, g_mid, o_pack, down_rows, sums, far_first = tie(
        (), (d_terms, g_q, g_mid, o_pack, down_rows, sums, far_first)
    )

    d_near = group.cross([d_terms[i] for i in range(n_seq)])
    d_sums = [d_terms[k * CORES].astype(wide) + d_near[k].astype(wide) for k in chips]
    d_far = group.send(d_sums)
    e1, q_pack = query_gradients(unit1, q_inner, g_q, ups, qkv_side, hq, rank, n_f)
    grad_down_weight, grad_down_down = lay_rows(down_rows, width, n_seq)
    d_far, e1, d_both, q_pack, grad_down_weight, grad_down_down = tie(
        (), (d_far, e1, d_sums[0], q_pack, grad_down_weight, grad_down_down)
    )

    for block in d_far:
        d_both = d_both + block.astype(wide)
    first, second = d_both[:, :half], d_both[:, half:HD]
    g_k = jnp.concatenate(
        [first * cosine + second * sine, second * cosine - first * sine], axis=1
    ).astype(low)
    g_v = d_both[:, HD:].astype(low)
    gi_k = mul_t(g_k, k_raise).astype(low)
    gi_v = mul_t(g_v, v_raise).astype(low)
    g_kv = jnp.concatenate([g_k, g_v], axis=1)
    e1 = e1 + mul_t(g_kv, qkv_side[:, hq:lin])
    e1 = e1 + mul_t(jnp.concatenate([gi_k, gi_v], axis=1), qkv_side[:, lin + rank :])
    input_grad = g_mid + r1 * e1 - resid * (
        r1 * r1 * r1 * jnp.mean(e1 * resid, axis=-1, keepdims=True)
    )
    input_grad = input_grad.astype(low).reshape(rows, length, width)
    kv_pack = jnp.concatenate(
        [
            t_mul(unit1, g_kv).astype(low).reshape(n_f, own_rows, 2 * kv),
            jnp.concatenate([t_mul(k_inner, g_k), t_mul(v_inner, g_v)], axis=1)
            .astype(low)
            .reshape(n_f, rank_rows, 2 * kv),
        ],
        axis=1,
    )
    kv_pack, input_grad, sums = tie((), (kv_pack, input_grad, sums))

    g_slab = slab_sums.done(wide)
    unit_grad = g_slab[rank_rows:]
    own_full = [
        lax.dynamic_index_in_dim(full, lax.axis_index("fsdp"), 0, False)
        for full in (gate_full, up_full)
    ]
    merged = jnp.concatenate(own_full, axis=1).astype(wide)
    weight_grad = (unit_grad * gain2).astype(low)
    mlp_small = jnp.concatenate(
        [
            mul_t(weight_grad[:, :slab], g_raise),
            mul_t(weight_grad[:, slab:], u_raise),
            jnp.broadcast_to(
                jnp.sum(unit_grad * merged, axis=1, keepdims=True) / gain2, (own_rows, 128)
            ),
        ],
        axis=1,
    ).astype(low)
    far = group.send([block[middle:] for block in sums])
    packs, slab_pieces, mlp_small = scatter_whole(
        (o_pack, q_pack, kv_pack), g_slab.astype(low), mlp_small, 6, n_seq
    )
    packs, slab_pieces, mlp_small, far = tie((), (packs, slab_pieces, mlp_small, far))
    own_branch = sums[0]
    for first, second in zip(far_first, far, strict=True):
        own_branch = own_branch + jnp.concatenate([first, second], axis=0).astype(wide)
    outputs = (mid + active * own_branch).astype(low).reshape(rows, length, width)
    o_pack, q_pack, kv_pack = (pack.astype(wide) for pack in packs)

    grad_o_weight = o_pack[:o_rows]
    grad_o_up = o_pack[o_rows : o_rows + rank_rows]
    grad_down_up = o_pack[o_rows + rank_rows :]
    grad_o_down = mul_t(packs[0][:o_rows], o_raise)
    grad_q_weight = q_pack[:own_rows] * gain1
    grad_kv = kv_pack[:own_rows] * gain1
    grad_k_weight, grad_v_weight = grad_kv[:, :kv], grad_kv[:, kv:]
    grad_q_up = q_pack[own_rows:]
    grad_k_up, grad_v_up = kv_pack[own_rows:, :kv], kv_pack[own_rows:, kv:]
    grad_q_down = mul_t(grad_q_weight.astype(low), q_raise)
    grad_k_down = mul_t(grad_k_weight.astype(low), k_raise)
    grad_v_down = mul_t(grad_v_weight.astype(low), v_raise)
    own_q = q_weight.astype(wide) + mul(q_down, q_raise)
    own_kv = jnp.concatenate(
        [
            k_weight.astype(wide) + mul(k_down, k_raise),
            v_weight.astype(wide) + mul(v_down, v_raise),
        ],
        axis=1,
    )
    grad_attn_gain = jnp.sum(q_pack[:own_rows] * own_q, axis=1) + jnp.sum(
        kv_pack[:own_rows] * own_kv, axis=1
    )

    grad_gate_down, grad_up_down = mlp_small[:, :rank], mlp_small[:, rank : 2 * rank]
    grad_mlp_gain = mlp_small[:, 2 * rank]
    grad_gate_weight, grad_up_weight, grad_gate_up, grad_up_up = place_columns(
        slab_pieces, gain2, n_f, n_seq, rank_rows, ff, slab
    )

    counted = counted.done()
    mean_confidence = counted[DEPTHS:] / counted[:DEPTHS]
    return (
        outputs,
        input_grad,
        grad_attn_gain,
        grad_q_weight,
        grad_k_weight,
        grad_v_weight,
        grad_o_weight,
        grad_q_down,
        grad_q_up,
        grad_k_down,
        grad_k_up,
        grad_v_down,
        grad_v_up,
        grad_o_down,
        grad_o_up,
        grad_mlp_gain,
        grad_gate_weight,
        grad_up_weight,
        grad_down_weight,
        grad_gate_down,
        grad_gate_up,
        grad_up_down,
        grad_up_up,
        grad_down_down,
        grad_down_up,
        counted[:DEPTHS].astype(jnp.int32),
        mean_confidence,
    )


def solution(mesh):
    tokens3 = P("fsdp", "seq", None)
    tokens2 = P("fsdp", "seq")
    vector, matrix = P("fsdp"), P("fsdp", None)
    in_specs = (tokens3,) * 2 + (tokens2,) * 3 + (vector,) + (matrix,) * 12 + (vector,) + (matrix,) * 9
    out_specs = (
        (tokens3,) * 2 + (vector,) + (matrix,) * 12 + (vector,) + (matrix,) * 9 + (P(), P())
    )
    return jax.shard_map(shards, mesh=mesh, in_specs=in_specs, out_specs=out_specs, check_vma=False)
```

```python
import jax
import jax.numpy as jnp
from jax import lax
from jax.experimental import pallas as pl
from jax.experimental.pallas import tpu as pltpu
from jax.sharding import PartitionSpec as P

H = 4
HD = 256
DEPTHS = 3
LOOP = 1
CORES = 2

epsilon = 1e-06
rope_base = 10000.0
low = jnp.bfloat16
wide = jnp.float32


def mul(left, right):
    return jnp.dot(left, right, preferred_element_type=wide)


def mul_t(left, right):
    return lax.dot_general(left, right, (((1,), (1,)), ((), ())), preferred_element_type=wide)


def t_mul(left, right):
    return lax.dot_general(left, right, (((0,), (0,)), ((), ())), preferred_element_type=wide)


def ring_order(count, width):
    if width < 2 or count % width or (count // width) % 2:
        return list(range(count))
    depth = count // width
    walk = [0]
    for z in range(depth):
        columns = range(1, width) if z % 2 == 0 else range(width - 1, 0, -1)
        walk += [z * width + x for x in columns]
    walk += [z * width for z in range(depth - 1, 0, -1)]
    return walk


MESH = pl.DeviceIdType.MESH
ANY = pl.BlockSpec(memory_space=pl.ANY)
VMEM = pl.BlockSpec(memory_space=pltpu.VMEM)


def pick(index, table):
    result = jnp.int32(table[0])
    for spot, value in enumerate(table):
        if spot:
            result = jnp.where(index == spot, jnp.int32(value), result)
    return result


class Places:
    def __init__(self, n_f, n_seq):
        self.n_f, self.n_seq, self.chips = n_f, n_seq, n_seq // CORES
        self.walk = ring_order(n_f, n_seq // CORES)
        spots = [0] * n_f
        for spot, device in enumerate(self.walk):
            spots[device] = spot
        self.f, self.me = lax.axis_index("fsdp"), lax.axis_index("seq")
        self.spot = pick(self.f, spots)
        self.y, self.core = self.me // CORES, lax.rem(self.me, CORES)

    def at(self, offset):
        return pick(lax.rem(self.spot + offset + self.n_f, self.n_f), self.walk)

    def seq(self, k, c):
        return lax.rem(self.y + k + self.chips, self.chips) * CORES + lax.rem(
            self.core + c, CORES
        )

    def greet(self, ring):
        barrier = pltpu.get_barrier_semaphore()
        friends = [{"seq": self.seq(0, 1)}]
        friends += [{"seq": self.seq(k, 0)} for k in range(1, self.chips)]
        if ring:
            friends += [{"fsdp": self.at(1)}, {"fsdp": self.at(-1)}]
        for friend in friends:
            pl.semaphore_signal(barrier, inc=1, device_id=friend, device_id_type=MESH)
        pl.semaphore_wait(barrier, len(friends))


def remote(source, target, send, receive, device):
    return pltpu.make_async_remote_copy(
        src_ref=source,
        dst_ref=target,
        send_sem=send,
        recv_sem=receive,
        device_id=device,
        device_id_type=MESH,
    )


def brief(us):
    return pl.CostEstimate(
        flops=int(us * 1.0e9), bytes_accessed=int(us * 1.0e6), transcendentals=0
    )


def params(number):
    return pltpu.CompilerParams(
        collective_id=number, has_side_effects=True, vmem_limit_bytes=56 * 2**20
    )


def ring_steps(n_f):
    order = []
    for step in range(1, n_f // 2 + 1):
        order.append((step, 1))
        if step <= (n_f - 1) // 2:
            order.append((step, -1))
    return order


def pack_small(gain1, gain2, attention, lower, raises, raises2, outward, n_seq):
    groups = [(attention, gain1), (raises, None), (outward, None), (raises2, None), (lower, gain2)]
    shares = (CORES, CORES, n_seq, n_seq, n_seq)

    def body(*refs):
        refs = list(refs)
        for (parts, gain), out in zip(groups, refs[-len(groups) :], strict=True):
            factor = None if gain is None else refs.pop(0)[...]
            at = 0
            for part in parts:
                block = refs.pop(0)[...]
                if factor is not None:
                    block = (block.astype(wide) * factor).astype(low)
                out[:, at : at + part.shape[1]] = block
                at += part.shape[1]
            if at < out.shape[1]:
                out[:, at:] = jnp.zeros((out.shape[0], out.shape[1] - at), low)

    sizes = []
    for (parts, _), ways in zip(groups, shares, strict=True):
        total = sum(part.shape[1] for part in parts)
        sizes.append((parts[0].shape[0], total + -total % (128 * ways)))
    operands = []
    for parts, gain in groups:
        operands += ([] if gain is None else [gain]) + list(parts)
    return pl.pallas_call(
        body,
        out_shape=tuple(jax.ShapeDtypeStruct(size, low) for size in sizes),
        compiler_params=pltpu.CompilerParams(vmem_limit_bytes=48 * 2**20),
    )(*operands)


def gather_whole(blocks, spread, number, n_f, n_seq):
    count = len(blocks)
    chips = n_seq // CORES
    steps = ring_steps(n_f)
    order = [j for j in range(count) if spread[j]] + [j for j in range(count) if not spread[j]]

    def body(*refs):
        ins, outs = refs[:count], refs[count : 2 * count]
        local, ring_s, ring_r, y_s, y_r, core_s, core_r = refs[2 * count :]
        here = Places(n_f, n_seq)
        started = []

        def share(j, k, c):
            spot = here.seq(k, c) if spread[j] else lax.rem(here.core + c, CORES)
            width = ins[j].shape[-1] // (n_seq if spread[j] else CORES)
            return (slice(None), pl.ds(pl.multiple_of(spot * width, 128), width))

        def far(j):
            return range(1, chips if spread[j] else 1)

        copies = []
        for j in range(count):
            copy = pltpu.make_async_copy(ins[j], outs[j].at[here.f], local.at[j])
            copy.start()
            copies.append(copy)
        here.greet(True)

        def flip(j):
            return 1 if j == 0 else -1

        def forward(j, step, way):
            owner = here.at(-flip(j) * way * (step - 1))
            mine = share(j, 0, 0)
            source = ins[j].at[mine] if step == 1 else outs[j].at[(owner, *mine)]
            at = steps.index((step, way))
            copy = remote(
                source,
                outs[j].at[(owner, *mine)],
                ring_s.at[j, at],
                ring_r.at[j, at],
                {"fsdp": here.at(flip(j) * way)},
            )
            copy.start()
            started.append(copy)

        def landed(j, step, way):
            owner = here.at(-flip(j) * way * step)
            at = steps.index((step, way))
            block = outs[j].at[(owner, *share(j, 0, 0))]
            remote(block, block, ring_s.at[j, at], ring_r.at[j, at], {"fsdp": here.at(flip(j) * way)}).wait_recv()
            return owner

        def to_core(j, at, k, owner):
            block = outs[j].at[(owner, *share(j, k, 0))]
            copy = remote(
                block, block, core_s.at[j, at, k], core_r.at[j, at, k], {"seq": here.seq(0, 1)}
            )
            copy.start()
            started.append(copy)

        for j in order:
            for way in (1, -1):
                forward(j, 1, way)
        for at, (step, way) in enumerate(steps):
            for j in order:
                owner = landed(j, step, way)
                if (step + 1, way) in steps:
                    forward(j, step + 1, way)
                block = outs[j].at[(owner, *share(j, 0, 0))]
                for k in far(j):
                    copy = remote(
                        block, block, y_s.at[j, at, k], y_r.at[j, at, k], {"seq": here.seq(-k, 0)}
                    )
                    copy.start()
                    started.append(copy)
                to_core(j, at, 0, owner)
        for at, (step, way) in enumerate(steps):
            for j in order:
                owner = here.at(-flip(j) * way * step)
                for k in far(j):
                    block = outs[j].at[(owner, *share(j, k, 0))]
                    remote(
                        block, block, y_s.at[j, at, k], y_r.at[j, at, k], {"seq": here.seq(-k, 0)}
                    ).wait_recv()
                    to_core(j, at, k, owner)
        for at, (step, way) in enumerate(steps):
            for j in order:
                owner = here.at(-flip(j) * way * step)
                for k in [0, *far(j)]:
                    block = outs[j].at[(owner, *share(j, k, 1))]
                    remote(
                        block, block, core_s.at[j, at, k], core_r.at[j, at, k], {"seq": here.seq(0, 1)}
                    ).wait_recv()
        for copy in started:
            copy.wait_send()
        for copy in copies:
            copy.wait()

    sems = pltpu.SemaphoreType.DMA
    return pl.pallas_call(
        body,
        out_shape=tuple(jax.ShapeDtypeStruct((n_f,) + b.shape, b.dtype) for b in blocks),
        in_specs=[ANY] * count,
        out_specs=(ANY,) * count,
        scratch_shapes=[sems((count,))]
        + [sems((count, len(steps)))] * 2
        + [sems((count, len(steps), chips))] * 4,
        compiler_params=params(number),
    )(*blocks)


def gather_group(block, number, n_seq):
    rows = block.shape[0]
    chips = n_seq // CORES
    parts = 4 if rows % 64 == 0 else 1
    size = rows // parts

    def body(x, out, local, y_s, y_r, core_s, core_r):
        here = Places(1, n_seq)
        own = pltpu.make_async_copy(x, out.at[0], local)
        own.start()
        here.greet(False)
        started = []

        def to_core(source, k, part):
            cut = pl.ds(part * size, size)
            copy = remote(
                source.at[cut],
                out.at[k * CORES + 1, cut],
                core_s.at[k, part],
                core_r.at[k, part],
                {"seq": here.seq(0, 1)},
            )
            copy.start()
            started.append(copy)

        def over(k, part):
            cut = pl.ds(part * size, size)
            return remote(
                x.at[cut],
                out.at[k * CORES, cut],
                y_s.at[k, part],
                y_r.at[k, part],
                {"seq": here.seq(-k, 0)},
            )

        for part in range(parts):
            for k in range(1, chips):
                copy = over(k, part)
                copy.start()
                started.append(copy)
            to_core(x, 0, part)
        for part in range(parts):
            for k in range(1, chips):
                over(k, part).wait_recv()
                to_core(out.at[k * CORES], k, part)
        for part in range(parts):
            for k in range(chips):
                cut = pl.ds(part * size, size)
                block = out.at[k * CORES + 1, cut]
                remote(
                    block, block, core_s.at[k, part], core_r.at[k, part], {"seq": here.seq(0, 1)}
                ).wait_recv()
        for copy in started:
            copy.wait_send()
        own.wait()

    sems = pltpu.SemaphoreType.DMA
    return pl.pallas_call(
        body,
        out_shape=jax.ShapeDtypeStruct((n_seq,) + block.shape, block.dtype),
        in_specs=[ANY],
        out_specs=ANY,
        scratch_shapes=[sems(())] + [sems((chips, parts))] * 4,
        compiler_params=params(number),
    )(block)


def scatter_group(terms, number):
    n_seq, rows, columns = terms.shape
    chips = n_seq // CORES
    parts = 4 if rows % 64 == 0 else 1
    size = rows // parts

    def body(x, out, near, sums, far, y_s, y_r, core_s, core_r):
        here = Places(1, n_seq)
        here.greet(False)
        started = []

        def cross(k, part):
            cut = pl.ds(part * size, size)
            return remote(
                x.at[k * CORES + 1, cut],
                near.at[k, cut],
                core_s.at[k, part],
                core_r.at[k, part],
                {"seq": here.seq(0, 1)},
            )

        def over(k, part):
            cut = pl.ds(part * size, size)
            return remote(
                sums.at[k, cut],
                far.at[k, cut],
                y_s.at[k, part],
                y_r.at[k, part],
                {"seq": here.seq(k, 0)},
            )

        for k in [*range(1, chips), 0]:
            for part in range(parts):
                copy = cross(k, part)
                copy.start()
                started.append(copy)
        for k in range(1, chips):
            for part in range(parts):
                cut = pl.ds(part * size, size)
                cross(k, part).wait_recv()
                total = x[k * CORES, cut, :].astype(wide) + near[k, cut, :].astype(wide)
                sums[k, cut, :] = total.astype(low)
                copy = over(k, part)
                copy.start()
                started.append(copy)
        for part in range(parts):
            cut = pl.ds(part * size, size)
            cross(0, part).wait_recv()
            out[cut, :] = x[0, cut, :].astype(wide) + near[0, cut, :].astype(wide)
        for part in range(parts):
            cut = pl.ds(part * size, size)
            for k in range(1, chips):
                over(k, part).wait_recv()
                out[cut, :] = out[cut, :] + far[k, cut, :].astype(wide)
        for copy in started:
            copy.wait_send()

    sems = pltpu.SemaphoreType.DMA
    buffer = pltpu.VMEM((chips, rows, columns), low)
    return pl.pallas_call(
        body,
        out_shape=jax.ShapeDtypeStruct((rows, columns), wide),
        in_specs=[VMEM],
        out_specs=VMEM,
        scratch_shapes=[buffer] * 3 + [sems((chips, parts))] * 4,
        compiler_params=params(number),
    )(terms)


def scatter_whole(packs, block, small, number, n_seq):
    wanted = [pack.shape[2] for pack in packs]
    gaps = [-count % (128 * CORES) for count in wanted]
    packs = [
        jnp.pad(pack, ((0, 0), (0, 0), (0, gap))) if gap else pack
        for pack, gap in zip(packs, gaps, strict=True)
    ]
    n_f, count = packs[0].shape[0], len(packs)
    chips = n_seq // CORES
    widths = [pack.shape[2] // CORES for pack in packs]
    steps = ring_steps(n_f)
    offsets = [way * step for step, way in reversed(steps)] + [0]
    last = {way: max(step for step, w in steps if w == way) for way in (1, -1)}

    def body(*refs):
        refs = list(refs)

        def take(n):
            taken, refs[:] = refs[:n], refs[n:]
            return taken

        xs = take(count)
        block_in, small_in = take(2)
        outs = take(count)
        block_out, small_out = take(2)
        nears, terms, moves, parts = (take(count) for _ in range(4))
        (smalls,) = take(1)
        core_s, core_r, ring_s, ring_r, y_s, y_r, side_s, side_r = take(8)
        local, far_s, far_r, near_s, near_r = take(5)
        here = Places(n_f, n_seq)
        own = pltpu.make_async_copy(block_in, block_out.at[0], local)
        own.start()
        smalls[here.me] = small_in[...]
        here.greet(True)
        started = []

        def flip(j):
            return 1 if j == 0 else -1

        def go(copy):
            copy.start()
            started.append(copy)

        def share(j, spot):
            return pl.ds(pl.multiple_of(spot * widths[j], 128), widths[j])

        other = lax.rem(here.core + 1, CORES)

        def cross(j, i):
            return remote(
                xs[j].at[here.at(flip(j) * offsets[i]), :, share(j, other)],
                nears[j].at[i],
                core_s.at[j, i],
                core_r.at[j, i],
                {"seq": here.seq(0, 1)},
            )

        def hop(j, step, way):
            at = steps.index((step, way))
            return remote(
                terms[j].at[at],
                moves[j].at[at],
                ring_s.at[j, at],
                ring_r.at[j, at],
                {"fsdp": here.at(flip(j) * way)},
            )

        def swap(j, k, spot):
            slot = parts[j].at[spot]
            return remote(slot, slot, y_s.at[j, k], y_r.at[j, k], {"seq": here.seq(-k, 0)})

        def far_block(k):
            return remote(
                block_in, block_out.at[k * CORES], far_s.at[k], far_r.at[k], {"seq": here.seq(-k, 0)}
            )

        def near_block(k):
            source = block_in if k == 0 else block_out.at[k * CORES]
            return remote(
                source,
                block_out.at[k * CORES + 1],
                near_s.at[k],
                near_r.at[k],
                {"seq": here.seq(0, 1)},
            )

        def far_small(k, spot):
            slot = smalls.at[spot]
            return remote(
                slot, slot, far_s.at[chips + k], far_r.at[chips + k], {"seq": here.seq(-k, 0)}
            )

        def near_small(k, spot):
            slot = smalls.at[spot]
            return remote(
                slot, slot, near_s.at[chips + k], near_r.at[chips + k], {"seq": here.seq(0, 1)}
            )

        for k in range(1, chips):
            go(far_small(k, here.me))
            go(far_block(k))
        for i in range(n_f):
            for j in range(count):
                go(cross(j, i))
        go(near_small(0, here.me))
        go(near_block(0))
        for i in range(n_f):
            for j in range(count):
                cross(j, i).wait_recv()
                total = xs[j][here.at(flip(j) * offsets[i]), :, share(j, here.core)].astype(wide)
                total = total + nears[j][i].astype(wide)
                if offsets[i]:
                    step, way = abs(offsets[i]), 1 if offsets[i] > 0 else -1
                    if step < last[way]:
                        hop(j, step + 1, way).wait_recv()
                        total = total + moves[j][steps.index((step + 1, way))].astype(wide)
                    terms[j][steps.index((step, way))] = total.astype(low)
                    go(hop(j, step, way))
                else:
                    for way in (1, -1):
                        if last[way] >= 1:
                            hop(j, 1, way).wait_recv()
                            total = total + moves[j][steps.index((1, way))].astype(wide)
                    parts[j][here.y] = total.astype(low)
                    for k in range(1, chips):
                        go(swap(j, k, here.y))

        def side(j, core):
            columns = outs[j].at[:, share(j, core)]
            return remote(columns, columns, side_s.at[j], side_r.at[j], {"seq": here.seq(0, 1)})

        for k in range(1, chips):
            far_small(k, here.seq(k, 0)).wait_recv()
            go(near_small(k, here.seq(k, 0)))
            far_block(k).wait_recv()
            go(near_block(k))
        for j in range(count):
            for k in range(1, chips):
                swap(j, k, lax.rem(here.y + k, chips)).wait_recv()
            total = parts[j][0].astype(wide)
            for y in range(1, chips):
                total = total + parts[j][y].astype(wide)
            outs[j][:, share(j, here.core)] = total.astype(low)
            go(side(j, here.core))
        for k in range(chips):
            near_small(k, here.seq(k, 1)).wait_recv()
        total = smalls[0].astype(wide)
        for spot in range(1, n_seq):
            total = total + smalls[spot].astype(wide)
        small_out[...] = total
        for k in range(chips):
            near_block(k).wait_recv()
        for j in range(count):
            side(j, other).wait_recv()
        for copy in started:
            copy.wait_send()
        own.wait()

    sems = pltpu.SemaphoreType.DMA
    shapes = [(pack.shape[1], width) for pack, width in zip(packs, widths, strict=True)]
    near = [pltpu.VMEM((n_f, *shape), low) for shape in shapes]
    ring = [pltpu.VMEM((len(steps), *shape), low) for shape in shapes]
    part = [pltpu.VMEM((chips, *shape), low) for shape in shapes]
    results = pl.pallas_call(
        body,
        out_shape=tuple(jax.ShapeDtypeStruct(pack.shape[1:], low) for pack in packs)
        + (
            jax.ShapeDtypeStruct((n_seq, *block.shape), low),
            jax.ShapeDtypeStruct(small.shape, wide),
        ),
        in_specs=[VMEM] * count + [ANY, VMEM],
        out_specs=(VMEM,) * count + (ANY, VMEM),
        scratch_shapes=near
        + ring * 2
        + part
        + [pltpu.VMEM((n_seq, *small.shape), low)]
        + [sems((count, n_f))] * 2
        + [sems((count, len(steps)))] * 2
        + [sems((count, chips))] * 2
        + [sems((count,))] * 2
        + [sems(())]
        + [sems((2 * chips,))] * 4,
        compiler_params=params(number),
    )(*packs, block, small)
    sums = [result[:, :size] for result, size in zip(results[:count], wanted, strict=True)]
    return sums, results[count], results[count + 1]


def ring_terms(sides, outs, n_f, n_seq, dtype):
    flat, spots = [], []
    left = 0
    for side in sides:
        top = 0
        for part in side:
            flat.append(part)
            spots.append((top, left))
            top += part.shape[1]
        left += side[0].shape[2]
    moved = [block for _, _, _, came in outs for block, _ in came]

    def body(*refs):
        parts, moves = refs[: len(flat)], list(refs[len(flat) : len(flat) + len(moved)])
        results = refs[len(flat) + len(moved) : len(flat) + len(moved) + len(outs)]
        scratch, sem = refs[len(flat) + len(moved) + len(outs) : -1], refs[-1]
        here = Places(n_f, n_seq)
        copies = []
        for i, (offset, first, stop, _) in enumerate(outs):
            owner = here.at(offset)
            for at, (part, (above, before)) in enumerate(zip(parts, spots, strict=True)):
                start, end = max(first, before), min(stop, before + part.shape[2])
                if start < end:
                    copies.append(
                        pltpu.make_async_copy(
                            part.at[owner, :, start - before : end - before],
                            scratch[i].at[
                                above : above + part.shape[1], start - first : end - first
                            ],
                            sem.at[i, at],
                        )
                    )
        for copy in copies:
            copy.start()
        for copy in copies:
            copy.wait()
        for i, (_, first, stop, came) in enumerate(outs):
            edges = sorted(
                {first, stop}
                | {c for _, c in came}
                | {c + block.shape[1] for block, c in came}
            )
            here_moves = [(moves.pop(0), c) for _, c in came]
            for start, end in zip(edges, edges[1:]):
                total = scratch[i][:, start - first : end - first].astype(wide)
                for ref, c in here_moves:
                    if c <= start and end <= c + ref.shape[1]:
                        total = total + ref[:, start - c : end - c].astype(wide)
                results[i][:, start - first : end - first] = total.astype(dtype)

    rows = sum(part.shape[1] for part in sides[0])
    shapes = [(rows, stop - first) for _, first, stop, _ in outs]
    return pl.pallas_call(
        body,
        out_shape=tuple(jax.ShapeDtypeStruct(shape, dtype) for shape in shapes),
        in_specs=[ANY] * len(flat) + [VMEM] * len(moved),
        out_specs=(VMEM,) * len(outs),
        scratch_shapes=[pltpu.VMEM(shape, low) for shape in shapes]
        + [pltpu.SemaphoreType.DMA((len(outs), len(flat)))],
        cost_estimate=brief(1),
        compiler_params=pltpu.CompilerParams(vmem_limit_bytes=32 * 2**20),
    )(*flat, *moved)


class Ring:
    def __init__(self, count, width):
        self.count = count
        walk = ring_order(count, width)
        self.up = [(walk[i], walk[(i + 1) % count]) for i in range(count)]
        self.down = [(b, a) for a, b in self.up]

    def hop(self, block, way):
        return lax.ppermute(block, "fsdp", self.up if way > 0 else self.down)


class Gathering:
    def __init__(self, ring, block):
        self.ring = ring
        self.step, self.steps = 0, ring.count // 2
        self.moving = (block, block)
        self.places = [(0, 0)]
        self.blocks = [block]

    def advance(self):
        if self.step == self.steps:
            return
        self.step += 1
        first, second = self.moving
        if self.step < self.steps:
            self.moving = (self.ring.hop(first, 1), self.ring.hop(second, -1))
            self.places += [(-self.step, 0), (self.step, 0)]
        else:
            half = first.shape[1] // 256 * 128
            self.moving = (
                self.ring.hop(first[:, :half], 1),
                self.ring.hop(second[:, half:], -1),
            )
            self.places += [(self.step, 0), (self.step, half)]
        self.blocks += list(self.moving)

    def done(self):
        while self.step < self.steps:
            self.advance()
        return [
            (offset, block, column)
            for (offset, column), block in zip(self.places, self.blocks, strict=True)
        ]

    def live(self):
        return (self.moving, self.blocks)

    def restore(self, live):
        self.moving, self.blocks = live


class Scattering:
    def __init__(self, ring, sides, n_seq):
        self.ring, self.sides, self.n_seq = ring, sides, n_seq
        self.width = sum(side[0].shape[2] for side in sides)
        self.half = self.width // 256 * 128
        self.step, self.steps = 0, ring.count // 2
        self.moving = ()

    def terms(self, outs, dtype):
        return ring_terms(self.sides, outs, self.ring.count, self.n_seq, dtype)

    def advance(self):
        if self.step == self.steps:
            return
        self.step += 1
        offset = self.steps - self.step + 1
        if self.step == 1:
            outs = [(offset, 0, self.half, []), (offset, self.half, self.width, [])]
        else:
            ahead, back = self.moving
            right = self.half if self.step == 2 else 0
            outs = [
                (offset, 0, self.width, [(ahead, 0)]),
                (-offset, 0, self.width, [(back, right)]),
            ]
        ahead, back = self.terms(outs, low)
        self.moving = (self.ring.hop(ahead, 1), self.ring.hop(back, -1))

    def done(self, dtype):
        while self.step < self.steps:
            self.advance()
        right = self.half if self.steps == 1 else 0
        ahead, back = self.moving
        (total,) = self.terms([(0, 0, self.width, [(ahead, 0), (back, right)])], dtype)
        return total

    def live(self):
        return self.moving

    def restore(self, live):
        self.moving = live


def tie(movers, values):
    lives, values = lax.optimization_barrier(([mover.live() for mover in movers], values))
    for mover, live in zip(movers, lives, strict=True):
        mover.restore(live)
    return values


class Group:
    def __init__(self, count):
        self.count = count
        self.chips = count // CORES
        me = lax.axis_index("seq")
        self.y, self.core = me // CORES, lax.rem(me, CORES)
        self.sibling = [(i, i ^ 1) for i in range(count)]
        self.order = [(k, c) for k in range(self.chips) for c in range(CORES)]

    def shift(self, k):
        n = self.chips
        return [(i, ((i // CORES + k) % n) * CORES + i % CORES) for i in range(self.count)]

    def index(self, k, c):
        return lax.rem(self.y + k, self.chips) * CORES + (self.core + c) % CORES

    def over(self, block):
        return [block] + [
            lax.ppermute(block, "seq", self.shift(-k)) for k in range(1, self.chips)
        ]

    def across(self, blocks):
        out = []
        for block in blocks:
            out += [block, lax.ppermute(block, "seq", self.sibling)]
        return out

    def swap(self, block):
        return lax.ppermute(block, "seq", self.sibling)

    def cross(self, terms):
        return [
            lax.ppermute(terms[k * CORES + 1], "seq", self.sibling) for k in range(self.chips)
        ]

    def send(self, sums):
        return [
            lax.ppermute(sums[k].astype(low), "seq", self.shift(k)) for k in range(1, self.chips)
        ]

    def laid(self, pieces, axis, dtype):
        width = pieces[0].shape[axis]
        shape = list(pieces[0].shape)
        shape[axis] = width * self.count
        out = jnp.zeros(shape, dtype)
        for (k, c), piece in zip(self.order, pieces, strict=True):
            out = lax.dynamic_update_slice_in_dim(
                out, piece.astype(dtype), self.index(k, c) * width, axis
            )
        return out


class Summing:
    def __init__(self, values, axes):
        self.values = values
        self.steps = [
            (axis, 1 << bit)
            for axis in axes
            for bit in range((lax.axis_size(axis) - 1).bit_length())
        ]
        assert all(lax.axis_size(axis) & (lax.axis_size(axis) - 1) == 0 for axis in axes)

    def advance(self):
        if self.steps:
            axis, step = self.steps.pop(0)
            pairs = [(i, i ^ step) for i in range(lax.axis_size(axis))]
            self.values = self.values + lax.ppermute(self.values, axis, pairs)

    def done(self):
        while self.steps:
            self.advance()
        return self.values

    def live(self):
        return self.values

    def restore(self, live):
        self.values = live


def cut_columns(weights, raises, gains, n_f, n_seq, slab):
    rows, ff = weights[0].shape
    rank_rows = raises[0].shape[0]
    block, cut = ff // n_f, ff // (n_f * n_seq)

    def body(gain_ref, w0, w1, r0, r1, out):
        me = lax.axis_index("seq")

        def run(ref, spot):
            runs = [
                ref[:, f * block + spot * cut : f * block + (spot + 1) * cut] for f in range(n_f)
            ]
            gap = slab - n_f * cut
            if gap:
                runs.append(jnp.zeros((ref.shape[0], gap), ref.dtype))
            return jnp.concatenate(runs, axis=1)

        for spot in range(n_seq):

            @pl.when(me == spot)
            def _():
                for side, (weight, raised) in enumerate(((w0, r0), (w1, r1))):
                    at = side * slab
                    out[:rank_rows, at : at + slab] = run(raised, spot)
                    scaled = run(weight, spot).astype(wide) * gain_ref[...]
                    out[rank_rows:, at : at + slab] = scaled.astype(low)

    return pl.pallas_call(
        body,
        out_shape=jax.ShapeDtypeStruct((rank_rows + rows, 2 * slab), low),
        compiler_params=pltpu.CompilerParams(vmem_limit_bytes=48 * 2**20),
    )(gains, *weights, *raises)


def place_columns(pieces, gains, n_f, n_seq, rank_rows, ff, slab):
    rows = pieces.shape[1] - rank_rows
    cut = ff // (n_f * n_seq)
    chips = n_seq // CORES

    def body(gain_ref, x, w0, w1, r0, r1):
        me = lax.axis_index("seq")
        y, core = me // CORES, lax.rem(me, CORES)

        def spot_of(spot):
            ahead = lax.rem(spot // CORES - y + chips, chips)
            return ahead * CORES + lax.rem(spot % CORES + core, CORES)

        def fill(out, first, count, at, gain):
            whole = [x[spot_of(spot), first : first + count, at : at + slab] for spot in range(n_seq)]
            runs = [
                whole[spot][:, f * cut : (f + 1) * cut] for f in range(n_f) for spot in range(n_seq)
            ]
            result = jnp.concatenate(runs, axis=1).astype(wide)
            out[...] = result if gain is None else result * gain

        for side, (weight, raised) in enumerate(((w0, r0), (w1, r1))):
            fill(raised, 0, rank_rows, side * slab, None)
            fill(weight, rank_rows, rows, side * slab, gain_ref[...])

    return pl.pallas_call(
        body,
        out_shape=(jax.ShapeDtypeStruct((rows, ff), wide),) * 2
        + (jax.ShapeDtypeStruct((rank_rows, ff), wide),) * 2,
        compiler_params=pltpu.CompilerParams(vmem_limit_bytes=56 * 2**20),
    )(gains, pieces)


def gelu_parts(gate):
    scale = (2.0 / jnp.pi) ** 0.5
    cube = 0.044715
    square = gate * gate
    half = 0.5 * jnp.tanh(gate * (scale + scale * cube * square)) + 0.5
    value = gate * half
    slope = half + value * (1.0 - half) * (2.0 * scale + 6.0 * scale * cube * square)
    return value, slope


def project(unit, side, ups, cosine, sine, hq, rank):
    tokens = unit.shape[0]
    lin = hq + 2 * HD
    half = HD // 2

    def body(x, weights, raises, cos, sin, queries, both, inner):
        low_inner = mul(x[...], weights[:, lin:]).astype(low)
        inner[...] = low_inner

        def head(at, own):
            columns = slice(at, at + HD)
            return mul(x[...], weights[:, columns]) + mul(
                low_inner[:, own * rank : (own + 1) * rank], raises[:, columns]
            )

        def turned(values):
            first, second = values[:, :half], values[:, half:]
            c, s = cos[...], sin[...]
            return jnp.concatenate(
                [first * c - second * s, second * c + first * s], axis=1
            ).astype(low)

        for at in range(0, hq, HD):
            queries[:, at : at + HD] = turned(head(at, 0))
        both[:, :HD] = turned(head(hq, 1))
        both[:, HD:] = head(hq + HD, 2).astype(low)

    return pl.pallas_call(
        body,
        out_shape=(
            jax.ShapeDtypeStruct((tokens, hq), low),
            jax.ShapeDtypeStruct((tokens, 2 * HD), low),
            jax.ShapeDtypeStruct((tokens, 3 * rank), low),
        ),
        cost_estimate=brief(2),
        compiler_params=pltpu.CompilerParams(vmem_limit_bytes=48 * 2**20),
    )(unit, side, ups, cosine, sine)


def attention(queries, both, mask, rows):
    n_seq, tokens, _ = both.shape
    length = tokens // rows
    scale = HD ** (-0.5)

    def body(q, kv, hidden, out, log_total):
        for r in range(rows):
            at = slice(r * length, (r + 1) * length)
            keys = kv[:, at, :HD].reshape(n_seq * length, HD)
            values = kv[:, at, HD:].reshape(n_seq * length, HD)
            for h in range(H):
                head = slice(h * HD, (h + 1) * HD)
                scores = mul_t(q[at, head], keys) * scale + hidden[r]
                top = jnp.max(scores, axis=-1, keepdims=True)
                weights = jnp.exp(scores - top)
                total = jnp.sum(weights, axis=-1, keepdims=True)
                out[at, head] = (mul(weights.astype(low), values) / total).astype(low)
                log_total[r, h] = top + jnp.log(total)

    return pl.pallas_call(
        body,
        out_shape=(
            jax.ShapeDtypeStruct(queries.shape, low),
            jax.ShapeDtypeStruct((rows, H, length, 1), wide),
        ),
        cost_estimate=brief(2),
        compiler_params=pltpu.CompilerParams(vmem_limit_bytes=48 * 2**20),
    )(queries, both, mask)


def attention_back(queries, both, mask, log_total, out, g_out, cosine, sine, rows):
    n_seq, tokens, _ = both.shape
    length = tokens // rows
    scale = HD ** (-0.5)
    half = HD // 2

    def body(q, kv, hidden, logs, o, g, cos, sin, g_q, g_both):
        for r in range(rows):
            at = slice(r * length, (r + 1) * length)
            keys = kv[:, at, :HD].reshape(n_seq * length, HD)
            values = kv[:, at, HD:].reshape(n_seq * length, HD)
            d_keys = d_values = None
            for h in range(H):
                head = slice(h * HD, (h + 1) * HD)
                scores = mul_t(q[at, head], keys) * scale + hidden[r]
                probs = jnp.exp(scores - logs[r, h])
                grad = g[at, head]
                dots = jnp.sum(
                    grad.astype(wide) * o[at, head].astype(wide), axis=-1, keepdims=True
                )
                d_scores = (probs * (mul_t(grad, values) - dots)).astype(low)
                d_query = mul(d_scores, keys) * scale
                first, second = d_query[:, :half], d_query[:, half:]
                c, s = cos[at, :], sin[at, :]
                turned = jnp.concatenate([first * c + second * s, second * c - first * s], axis=1)
                g_q[at, head] = turned.astype(low)
                d_key = t_mul(d_scores, q[at, head])
                d_value = t_mul(probs.astype(low), grad)
                d_keys = d_key if d_keys is None else d_keys + d_key
                d_values = d_value if d_values is None else d_values + d_value
            g_both[:, at, :HD] = (d_keys * scale).astype(low).reshape(n_seq, length, HD)
            g_both[:, at, HD:] = d_values.astype(low).reshape(n_seq, length, HD)

    return pl.pallas_call(
        body,
        out_shape=(
            jax.ShapeDtypeStruct(queries.shape, low),
            jax.ShapeDtypeStruct(both.shape, low),
        ),
        cost_estimate=brief(3),
        compiler_params=pltpu.CompilerParams(vmem_limit_bytes=56 * 2**20),
    )(queries, both, mask, log_total, out, g_out, cosine, sine)


def by_owner(out, first, product, n_f):
    rows = product.shape[0] // n_f
    for f in range(n_f):
        out[f, first : first + rows, :] = product[f * rows : (f + 1) * rows].astype(low)
    return first + rows


def output_gradients(attn, inner, g_branch, ready, n_f):
    columns = g_branch.shape[1]
    wide_columns = columns + -columns % (128 * CORES)
    sizes = [part.shape[-2] if part.ndim == 3 else part.shape[1] // n_f for part in (attn, inner, ready)]

    def body(a, b, g, done, out):
        main = out.at[:, :, :columns]
        first = by_owner(main, 0, t_mul(a[...], g[...]), n_f)
        first = by_owner(main, first, t_mul(b[...], g[...]), n_f)
        out[:, first:, :columns] = done[...]
        if columns < wide_columns:
            out[:, :, columns:] = jnp.zeros((n_f, sum(sizes), wide_columns - columns), low)

    return pl.pallas_call(
        body,
        out_shape=jax.ShapeDtypeStruct((n_f, sum(sizes), wide_columns), low),
        cost_estimate=brief(2),
        compiler_params=pltpu.CompilerParams(vmem_limit_bytes=40 * 2**20),
    )(attn, inner, g_branch, ready)


def query_gradients(unit, inner, g_q, raises, side, hq, rank, n_f):
    tokens, width = unit.shape
    lin = hq + 2 * HD
    rows = width // n_f + rank // n_f

    def body(x, low_inner, g, ups, weights, e1, out):
        g_inner = mul_t(g[...], ups[:, :hq]).astype(low)
        e1[...] = mul_t(g[...], weights[:, :hq]) + mul_t(g_inner, weights[:, lin : lin + rank])
        first = by_owner(out, 0, t_mul(x[...], g[...]), n_f)
        by_owner(out, first, t_mul(low_inner[...], g[...]), n_f)

    return pl.pallas_call(
        body,
        out_shape=(
            jax.ShapeDtypeStruct((tokens, width), wide),
            jax.ShapeDtypeStruct((n_f, rows, hq), low),
        ),
        cost_estimate=brief(2),
        compiler_params=pltpu.CompilerParams(vmem_limit_bytes=48 * 2**20),
    )(unit, inner, g_q, raises, side)


def lay_rows(pieces, cut_at, n_seq):
    rows, columns = pieces[0].shape
    chips = n_seq // CORES

    def body(*refs):
        me = lax.axis_index("seq")
        y, core = me // CORES, lax.rem(me, CORES)
        for at, ref in enumerate(refs[:n_seq]):
            spot = lax.rem(y + at // CORES, chips) * CORES + lax.rem(core + at % CORES, CORES)
            refs[n_seq][spot] = ref[:, :cut_at].astype(wide)
            refs[n_seq + 1][spot] = ref[:, cut_at:].astype(wide)

    results = pl.pallas_call(
        body,
        out_shape=(
            jax.ShapeDtypeStruct((n_seq, rows, cut_at), wide),
            jax.ShapeDtypeStruct((n_seq, rows, columns - cut_at), wide),
        ),
        cost_estimate=brief(1),
        compiler_params=pltpu.CompilerParams(vmem_limit_bytes=32 * 2**20),
    )(*pieces)
    return [result.reshape(n_seq * rows, -1) for result in results]


def landing(items, buffers, rows_first, sem, here):
    copies = []
    for at, (offset, ref, column) in enumerate(items):
        owner = here.at(offset)
        first = 0
        for part, buffer in enumerate(buffers):
            count = rows_first[part]
            copies.append(
                pltpu.make_async_copy(
                    ref.at[first : first + count],
                    buffer.at[owner, :, column : column + ref.shape[1]],
                    sem.at[at, part],
                )
            )
            first += count
    for copy in copies:
        copy.start()
    for copy in copies:
        copy.wait()


def mlp_forward(
    items, tokens2, adapters, before, part, n_f, n_seq, rank_rows, own_rows, slab
):
    count, width = tokens2.shape
    rank = rank_rows * n_f
    tile = 256 if slab % 256 == 0 else 128
    chunk = 512
    first, stop = part
    wanted = []
    for side in range(2):
        start, end = side * slab + first * tile, side * slab + stop * tile
        for at, (offset, block, column) in enumerate(items):
            low_end, high_end = max(start, column), min(end, column + block.shape[1])
            if low_end < high_end:
                wanted.append((at, offset, low_end - column, high_end - column, side, low_end - start))

    def body(x, lower_g, lower_u, *refs):
        blocks, refs = refs[: len(items)], refs[len(items) + len(before) :]
        hidden, back_g, back_u, full_g, full_u, raised_g, raised_u = refs[:7]
        raises, weights, merged, sem = refs[7:]
        here = Places(n_f, n_seq)
        step = pl.program_id(0)

        @pl.when(step == 0)
        def _():
            copies = []
            for number, (at, offset, start, end, side, column) in enumerate(wanted):
                owner = here.at(offset)
                for which, (buffer, rows) in enumerate(
                    (
                        (raises, slice(0, rank_rows)),
                        (weights, slice(rank_rows, rank_rows + own_rows)),
                    )
                ):
                    copies.append(
                        pltpu.make_async_copy(
                            blocks[at].at[rows, start:end],
                            buffer.at[side, owner, :, column : column + end - start],
                            sem.at[number, which],
                        )
                    )
            for copy in copies:
                copy.start()
            for copy in copies:
                copy.wait()

        for side, (lower, full, raised) in enumerate(
            ((lower_g, full_g, raised_g), (lower_u, full_u, raised_u))
        ):
            columns = pl.ds(pl.multiple_of(step * tile, 128), tile)
            up_matrix = raises[side, :, :, columns].reshape(rank, tile)
            raised[...] = up_matrix
            for f in range(n_f):
                total = weights[side, f, :, columns].astype(wide) + mul(lower[f], up_matrix)
                total = total.astype(low)
                full[f] = total
                merged[side, f * own_rows : (f + 1) * own_rows, :] = total

        def some(i, carry):
            at = pl.ds(pl.multiple_of(i * chunk, chunk), chunk)
            gate = mul(x[at, :], merged[0])
            up = mul(x[at, :], merged[1])
            value, slope = gelu_parts(gate)
            hidden[at, :] = (value * up).astype(low)
            back_g[at, :] = (up * slope).astype(low)
            back_u[at, :] = value.astype(low)
            return carry

        lax.fori_loop(0, count // chunk, some, 0, unroll=True)

    by_column = pl.BlockSpec((count, tile), lambda j: (0, j + first))
    by_weight = pl.BlockSpec((n_f, own_rows, tile), lambda j: (0, 0, j + first))
    by_raise = pl.BlockSpec((rank, tile), lambda j: (0, j + first))
    return pl.pallas_call(
        body,
        grid=(stop - first,),
        out_shape=(jax.ShapeDtypeStruct((count, slab), low),) * 3
        + (jax.ShapeDtypeStruct((n_f, own_rows, slab), low),) * 2
        + (jax.ShapeDtypeStruct((rank, slab), low),) * 2,
        in_specs=[VMEM] * 3 + [ANY] * (len(items) + len(before)),
        input_output_aliases={3 + len(items) + i: i for i in range(len(before))},
        out_specs=(by_column,) * 3 + (by_weight,) * 2 + (by_raise,) * 2,
        scratch_shapes=[
            pltpu.VMEM((2, n_f, rank_rows, (stop - first) * tile), low),
            pltpu.VMEM((2, n_f, own_rows, (stop - first) * tile), low),
            pltpu.VMEM((2, width, tile), low),
            pltpu.SemaphoreType.DMA((len(wanted), 2)),
        ],
        cost_estimate=brief(3),
        compiler_params=pltpu.CompilerParams(vmem_limit_bytes=56 * 2**20),
    )(tokens2, *adapters, *(block for _, block, _ in items), *before)


def mlp_backward(items, d_raise, g_tokens, back_g, back_u, n_f, n_seq, cut, slab):
    count, width = g_tokens.shape
    rank = d_raise.shape[0]
    tile = 256 if slab % 256 == 0 else 128
    chunk = 512
    offsets = [(offset, column) for offset, _, column in items]

    def body(g, raised, mul_g, mul_u, *refs):
        blocks = refs[: len(items)]
        grad_g, grad_u, full, raw, merged, sem = refs[len(items) :]
        here = Places(n_f, n_seq)
        step = pl.program_id(0)

        @pl.when(step == 0)
        def _():
            landing(
                [(o, ref, c) for (o, c), ref in zip(offsets, blocks, strict=True)],
                (raw,),
                (cut,),
                sem,
                here,
            )
            for f in range(n_f):
                merged[f * cut : (f + 1) * cut, :] = raw[f, :, :width].astype(wide) + mul(
                    raw[f, :, width:], raised[...]
                )
            if slab > n_f * cut:
                merged[n_f * cut :, :] = jnp.zeros((slab - n_f * cut, width), wide)

        weight = merged[pl.ds(pl.multiple_of(step * tile, tile), tile), :].astype(low)
        full[...] = weight

        def some(i, carry):
            at = pl.ds(pl.multiple_of(i * chunk, chunk), chunk)
            g_hidden = mul_t(g[at, :], weight)
            grad_g[at, :] = (g_hidden * mul_g[at, :].astype(wide)).astype(low)
            grad_u[at, :] = (g_hidden * mul_u[at, :].astype(wide)).astype(low)
            return carry

        lax.fori_loop(0, count // chunk, some, 0, unroll=True)

    by_column = pl.BlockSpec((count, tile), lambda j: (0, j))
    return pl.pallas_call(
        body,
        grid=(slab // tile,),
        out_shape=(jax.ShapeDtypeStruct((count, slab), low),) * 2
        + (jax.ShapeDtypeStruct((slab, width), low),),
        in_specs=[VMEM] * 2 + [by_column] * 2 + [ANY] * len(items),
        out_specs=(by_column,) * 2 + (pl.BlockSpec((tile, width), lambda j: (j, 0)),),
        scratch_shapes=[
            pltpu.VMEM((n_f, cut, width + rank), low),
            pltpu.VMEM((slab, width), wide),
            pltpu.SemaphoreType.DMA((len(items), 1)),
        ],
        cost_estimate=brief(3),
        compiler_params=pltpu.CompilerParams(vmem_limit_bytes=56 * 2**20),
    )(g_tokens, d_raise, back_g, back_u, *(block for _, block, _ in items))


def shards(
    inputs,
    cotangent,
    segments,
    exits,
    confidence,
    attn_gain,
    q_weight,
    k_weight,
    v_weight,
    o_weight,
    q_down,
    q_up,
    k_down,
    k_up,
    v_down,
    v_up,
    o_down,
    o_up,
    mlp_gain,
    gate_weight,
    up_weight,
    down_weight,
    gate_down,
    gate_up,
    up_down,
    up_up,
    down_down,
    down_up,
):
    n_seq, n_f = lax.axis_size("seq"), lax.axis_size("fsdp")
    me = lax.axis_index("seq")
    ring = Ring(n_f, n_seq // CORES)
    group = Group(n_seq)
    rows, length, width = inputs.shape
    tokens = rows * length
    rank = q_down.shape[1]
    hq = q_weight.shape[1]
    ff = gate_weight.shape[1]
    own_rows = q_weight.shape[0]
    rank_rows = q_up.shape[0]
    o_rows = o_weight.shape[0]
    cut = ff // (n_f * n_seq)
    slab = -(-n_f * cut // 128) * 128
    scale = HD ** (-0.5)

    gain1 = attn_gain.astype(wide)[:, None]
    gain2 = mlp_gain.astype(wide)[:, None]

    def rows_of(array):
        part = array.shape[0] // n_seq
        return lax.dynamic_slice_in_dim(array, me * part, part, 0)

    small_blocks = pack_small(
        gain1,
        gain2,
        (q_weight, k_weight, v_weight, q_down, k_down, v_down),
        (gate_down, up_down),
        (q_up, k_up, v_up),
        (o_up, down_up),
        (o_weight, o_down),
        n_seq,
    )

    slabs = Gathering(
        ring, cut_columns((gate_weight, up_weight), (gate_up, up_up), gain2, n_f, n_seq, slab)
    )
    d_lower = rows_of(down_down)
    downs = Gathering(ring, jnp.concatenate([rows_of(down_weight), d_lower], axis=1))

    depth_ids = jnp.arange(DEPTHS, dtype=jnp.int32)
    matches = (exits.reshape(tokens)[:, None] == depth_ids[None, :]).astype(wide)
    counted = Summing(
        jnp.concatenate(
            [jnp.sum(matches, axis=0), jnp.sum(matches * confidence.reshape(tokens)[:, None], axis=0)]
        ),
        ("seq", "fsdp"),
    )
    resid = inputs.reshape(tokens, width).astype(wide)
    active = (exits.reshape(tokens) >= LOOP).astype(wide)[:, None]
    cot = cotangent.reshape(tokens, width).astype(wide)
    g_mlp = (active * cot).astype(low)
    places = me * length + jnp.arange(length, dtype=jnp.int32)
    frequency = rope_base ** (-2.0 * jnp.arange(HD // 2, dtype=wide) / HD)
    angles = jnp.tile(places, rows).astype(wide)[:, None] * frequency[None, :]
    cosine, sine = jnp.cos(angles), jnp.sin(angles)
    r1 = lax.rsqrt(jnp.mean(resid * resid, axis=-1, keepdims=True) + epsilon)
    unit1 = (resid * r1).astype(low)

    slabs.advance()
    seg_pieces = group.over(segments.astype(low))
    whole = gather_whole(small_blocks, (False, False, True, True, True), 0, n_f, n_seq)
    whole, seg_pieces, unit1, cosine, sine, g_mlp = tie(
        (slabs, downs), (whole, seg_pieces, unit1, cosine, sine, g_mlp)
    )
    qkv_side, ups, side_o, ups2, adapters = (part.reshape(-1, part.shape[2]) for part in whole)
    kv = HD
    lin = hq + 2 * kv
    gate_adapter, up_adapter = adapters[:, :rank], adapters[:, rank : 2 * rank]
    side_o = side_o[:, : width + rank]
    q_raise, k_raise, v_raise = ups[:, :hq], ups[:, hq : hq + kv], ups[:, hq + kv : lin]
    o_raise, d_raise = ups2[:, :width], ups2[:, width : 2 * width]

    slabs.advance()
    seg_pieces = group.across(seg_pieces)
    half = HD // 2
    queries, both, inner = project(unit1, qkv_side, ups, cosine, sine, hq, rank)
    both = gather_group(both, 2, n_seq)
    key_seg = jnp.concatenate(seg_pieces, axis=1).astype(jnp.int32)
    key_place = jnp.concatenate(
        [
            group.index(k, c) * length + jnp.arange(length, dtype=jnp.int32)
            for k, c in group.order
        ]
    )
    allowed = (segments[:, :, None] == key_seg[:, None, :]) & (
        key_place[None, None, :] <= places[None, :, None]
    )
    mask = jnp.where(allowed, 0.0, -1e30).astype(wide)
    both, queries, mask, inner, g_mlp = tie((slabs,), (both, queries, mask, inner, g_mlp))
    q_inner, k_inner, v_inner = inner[:, :rank], inner[:, rank : 2 * rank], inner[:, 2 * rank :]

    slabs.advance()
    g_mlp = group.over(g_mlp)
    attn_low, log_total = attention(queries, both, mask, rows)
    projected = mul(attn_low, side_o)
    o_inner = projected[:, width:].astype(low)
    mid = resid + active * (projected[:, :width] + mul(o_inner, o_raise))
    r2 = lax.rsqrt(jnp.mean(mid * mid, axis=-1, keepdims=True) + epsilon)
    unit2 = (mid * r2).astype(low)
    unit2, mid, r2, g_mlp, attn_low, o_inner, log_total, gate_adapter, up_adapter, d_raise = tie(
        (slabs,),
        (
            unit2,
            mid,
            r2,
            g_mlp,
            attn_low,
            o_inner,
            log_total,
            gate_adapter.reshape(n_f, own_rows, rank),
            up_adapter.reshape(n_f, own_rows, rank),
            d_raise,
        ),
    )

    slabs.advance()
    downs.advance()
    unit2 = gather_group(unit2, 3, n_seq).reshape(-1, width)
    unit2, g_mlp = tie((slabs, downs), (unit2, g_mlp))

    downs.advance()
    g_mlp = group.across(g_mlp)
    tiles = slab // (256 if slab % 256 == 0 else 128)
    arrived = slabs.done()

    def forward(first, stop, before):
        return mlp_forward(
            arrived,
            unit2,
            (gate_adapter, up_adapter),
            before,
            (first, stop),
            n_f,
            n_seq,
            rank_rows,
            own_rows,
            slab,
        )

    half_way = forward(0, (tiles + 1) // 2, ())
    half_way, g_mlp = tie((downs,), (half_way, g_mlp))
    downs.advance()
    counted.advance()
    hidden, back_g, back_u, gate_full, up_full, g_raise, u_raise = forward(
        (tiles + 1) // 2, tiles, half_way
    )
    hidden, back_g, back_u, g_mlp = tie((downs, counted), (hidden, back_g, back_u, g_mlp))
    g_mlp = jnp.concatenate(g_mlp, axis=0)

    downs.advance()
    counted.advance()
    g_down = t_mul(hidden, g_mlp).astype(low)
    g_down, g_mlp, back_g, back_u = tie((downs, counted), (g_down, g_mlp, back_g, back_u))

    down_sums = Scattering(ring, [[g_down[: n_f * cut].reshape(n_f, cut, width)]], n_seq)

    down_sums.advance()
    counted.advance()
    g_gate, g_up, down_full = mlp_backward(
        downs.done(), d_raise, g_mlp, back_g, back_u, n_f, n_seq, cut, slab
    )
    g_gate, g_up, down_full = tie((down_sums, counted), (g_gate, g_up, down_full))

    down_sums.advance()
    counted.advance()
    gg = t_mul(unit2, g_gate).astype(low)
    gg_raise = t_mul(gate_adapter.reshape(width, rank), gg).astype(low)
    gg, gg_raise, g_gate, g_up, unit2 = tie(
        (down_sums, counted), (gg, gg_raise, g_gate, g_up, unit2)
    )
    down_sums.advance()
    gu = t_mul(unit2, g_up).astype(low)
    gu_raise = t_mul(up_adapter.reshape(width, rank), gu).astype(low)
    gg, gu, gg_raise, gu_raise, g_gate, g_up = tie(
        (down_sums,), (gg, gu, gg_raise, gu_raise, g_gate, g_up)
    )
    slab_sums = Scattering(
        ring,
        [
            [part.reshape(n_f, -1, slab) for part in side]
            for side in ((gg_raise, gg), (gu_raise, gu))
        ],
        n_seq,
    )
    chips = range(n_seq // CORES)
    here_tokens = CORES * tokens

    def token_gradient(at):
        result = mul_t(g_gate[at], gate_full.reshape(width, slab))
        return (result + mul_t(g_up[at], up_full.reshape(width, slab))).astype(low)

    slab_sums.advance()
    e2_there = token_gradient(slice(here_tokens, None))
    g_down = down_sums.done(low)
    down_rows = jnp.concatenate([g_down, mul_t(g_down, d_raise).astype(low)], axis=1)
    gd_raise = t_mul(d_lower, g_down).astype(low)
    e2_there, g_gate, g_up, down_rows, gd_raise = tie(
        (slab_sums,), (e2_there, g_gate, g_up, down_rows, gd_raise)
    )

    slab_sums.advance()
    there = [e2_there[i * tokens : (i + 1) * tokens] for i in range(n_seq - CORES)]
    e2_near = [group.swap(there[(k - 1) * CORES + 1]) for k in chips[1:]]
    down_rows = group.over(down_rows)
    e2_here = token_gradient(slice(0, here_tokens))
    e2_here, e2_near, hidden, down_rows = tie((slab_sums,), (e2_here, e2_near, hidden, down_rows))

    slab_sums.advance()
    e2_sums = [
        there[(k - 1) * CORES].astype(wide) + e2_near[k - 1].astype(wide) for k in chips[1:]
    ]
    e2_far = group.send([None, *e2_sums])
    e2_own = group.swap(e2_here[tokens:])
    branch = mul(hidden, down_full).astype(low)
    branch, e2_far, e2_own, e2_here = tie((slab_sums,), (branch, e2_far, e2_own, e2_here))
    terms = [branch[i * tokens : (i + 1) * tokens] for i in range(n_seq)]
    e2 = e2_here[:tokens].astype(wide) + e2_own.astype(wide)
    for block in e2_far:
        e2 = e2 + block.astype(wide)

    slab_sums.advance()
    near = group.cross(terms)
    g_mid = cot + r2 * e2 - mid * (r2 * r2 * r2 * jnp.mean(e2 * mid, axis=-1, keepdims=True))
    g_branch = (active * g_mid).astype(low)
    g_inner = mul_t(g_branch, o_raise).astype(low)
    g_attn = mul_t(jnp.concatenate([g_branch, g_inner], axis=1), side_o).astype(low)
    own_full = [
        lax.dynamic_index_in_dim(full, lax.axis_index("fsdp"), 0, False)
        for full in (gate_full, up_full)
    ]
    merged = jnp.concatenate(own_full, axis=1)
    own_q = q_weight.astype(wide) + mul(q_down, q_raise)
    own_kv = jnp.concatenate(
        [
            k_weight.astype(wide) + mul(k_down, k_raise),
            v_weight.astype(wide) + mul(v_down, v_raise),
        ],
        axis=1,
    )
    g_attn, terms, near, g_mid, g_branch, down_rows, merged, own_q, own_kv = tie(
        (slab_sums,),
        (g_attn, terms, near, g_mid, g_branch, down_rows, merged, own_q, own_kv),
    )

    down_rows = group.across(down_rows)
    sums = [terms[k * CORES].astype(wide) + near[k].astype(wide) for k in chips]
    middle = tokens // 2
    far_first = group.send([block[:middle] for block in sums])
    g_q, d_terms = attention_back(
        queries, both, mask, log_total, attn_low, g_attn, cosine, sine, rows
    )
    o_pack = output_gradients(
        attn_low, o_inner, g_branch, gd_raise.reshape(n_f, rank_rows, width), n_f
    )
    d_terms, g_q, g_mid, o_pack, down_rows, sums, far_first = tie(
        (), (d_terms, g_q, g_mid, o_pack, down_rows, sums, far_first)
    )

    d_near = group.cross([d_terms[i] for i in range(n_seq)])
    d_sums = [d_terms[k * CORES].astype(wide) + d_near[k].astype(wide) for k in chips]
    d_far = group.send(d_sums)
    e1, q_pack = query_gradients(unit1, q_inner, g_q, ups, qkv_side, hq, rank, n_f)
    grad_down_weight, grad_down_down = lay_rows(down_rows, width, n_seq)
    d_far, e1, d_both, q_pack, grad_down_weight, grad_down_down = tie(
        (), (d_far, e1, d_sums[0], q_pack, grad_down_weight, grad_down_down)
    )

    for block in d_far:
        d_both = d_both + block.astype(wide)
    first, second = d_both[:, :half], d_both[:, half:HD]
    g_k = jnp.concatenate(
        [first * cosine + second * sine, second * cosine - first * sine], axis=1
    ).astype(low)
    g_v = d_both[:, HD:].astype(low)
    gi_k = mul_t(g_k, k_raise).astype(low)
    gi_v = mul_t(g_v, v_raise).astype(low)
    g_kv = jnp.concatenate([g_k, g_v], axis=1)
    e1 = e1 + mul_t(g_kv, qkv_side[:, hq:lin])
    e1 = e1 + mul_t(jnp.concatenate([gi_k, gi_v], axis=1), qkv_side[:, lin + rank :])
    input_grad = g_mid + r1 * e1 - resid * (
        r1 * r1 * r1 * jnp.mean(e1 * resid, axis=-1, keepdims=True)
    )
    input_grad = input_grad.astype(low).reshape(rows, length, width)
    kv_pack = jnp.concatenate(
        [
            t_mul(unit1, g_kv).astype(low).reshape(n_f, own_rows, 2 * kv),
            jnp.concatenate([t_mul(k_inner, g_k), t_mul(v_inner, g_v)], axis=1)
            .astype(low)
            .reshape(n_f, rank_rows, 2 * kv),
        ],
        axis=1,
    )
    kv_pack, input_grad, sums = tie((), (kv_pack, input_grad, sums))

    g_slab = slab_sums.done(wide)
    unit_grad = g_slab[rank_rows:]
    weight_grad = (unit_grad * gain2).astype(low)
    mlp_small = jnp.concatenate(
        [
            mul_t(weight_grad[:, :slab], g_raise),
            mul_t(weight_grad[:, slab:], u_raise),
            jnp.broadcast_to(
                jnp.sum(unit_grad * merged.astype(wide), axis=1, keepdims=True) / gain2, (own_rows, 128)
            ),
        ],
        axis=1,
    ).astype(low)
    far = group.send([block[middle:] for block in sums])
    packs, slab_pieces, mlp_small = scatter_whole(
        (o_pack, q_pack, kv_pack), g_slab.astype(low), mlp_small, 6, n_seq
    )
    packs, slab_pieces, mlp_small, far = tie((), (packs, slab_pieces, mlp_small, far))
    own_branch = sums[0]
    for first, second in zip(far_first, far, strict=True):
        own_branch = own_branch + jnp.concatenate([first, second], axis=0).astype(wide)
    outputs = (mid + active * own_branch).astype(low).reshape(rows, length, width)
    packs[0] = packs[0][:, :width]
    o_pack, q_pack, kv_pack = (pack.astype(wide) for pack in packs)

    grad_o_weight = o_pack[:o_rows]
    grad_o_up = o_pack[o_rows : o_rows + rank_rows]
    grad_down_up = o_pack[o_rows + rank_rows :]
    grad_o_down = mul_t(packs[0][:o_rows], o_raise)
    grad_q_weight = q_pack[:own_rows] * gain1
    grad_kv = kv_pack[:own_rows] * gain1
    grad_k_weight, grad_v_weight = grad_kv[:, :kv], grad_kv[:, kv:]
    grad_q_up = q_pack[own_rows:]
    grad_k_up, grad_v_up = kv_pack[own_rows:, :kv], kv_pack[own_rows:, kv:]
    grad_q_down = mul_t(grad_q_weight.astype(low), q_raise)
    grad_k_down = mul_t(grad_k_weight.astype(low), k_raise)
    grad_v_down = mul_t(grad_v_weight.astype(low), v_raise)
    grad_attn_gain = jnp.sum(q_pack[:own_rows] * own_q, axis=1) + jnp.sum(
        kv_pack[:own_rows] * own_kv, axis=1
    )

    grad_gate_down, grad_up_down = mlp_small[:, :rank], mlp_small[:, rank : 2 * rank]
    grad_mlp_gain = mlp_small[:, 2 * rank]
    grad_gate_weight, grad_up_weight, grad_gate_up, grad_up_up = place_columns(
        slab_pieces, gain2, n_f, n_seq, rank_rows, ff, slab
    )

    counted = counted.done()
    mean_confidence = counted[DEPTHS:] / counted[:DEPTHS]
    return (
        outputs,
        input_grad,
        grad_attn_gain,
        grad_q_weight,
        grad_k_weight,
        grad_v_weight,
        grad_o_weight,
        grad_q_down,
        grad_q_up,
        grad_k_down,
        grad_k_up,
        grad_v_down,
        grad_v_up,
        grad_o_down,
        grad_o_up,
        grad_mlp_gain,
        grad_gate_weight,
        grad_up_weight,
        grad_down_weight,
        grad_gate_down,
        grad_gate_up,
        grad_up_down,
        grad_up_up,
        grad_down_down,
        grad_down_up,
        counted[:DEPTHS].astype(jnp.int32),
        mean_confidence,
    )


def solution(mesh):
    tokens3 = P("fsdp", "seq", None)
    tokens2 = P("fsdp", "seq")
    vector, matrix = P("fsdp"), P("fsdp", None)
    in_specs = (tokens3,) * 2 + (tokens2,) * 3 + (vector,) + (matrix,) * 12 + (vector,) + (matrix,) * 9
    out_specs = (
        (tokens3,) * 2 + (vector,) + (matrix,) * 12 + (vector,) + (matrix,) * 9 + (P(), P())
    )
    return jax.shard_map(shards, mesh=mesh, in_specs=in_specs, out_specs=out_specs, check_vma=False)
```

```python
import jax
import jax.numpy as jnp
from jax import lax
from jax.experimental import pallas as pl
from jax.experimental.pallas import tpu as pltpu
from jax.sharding import PartitionSpec as P

H = 4
HD = 256
DEPTHS = 3
LOOP = 1
CORES = 2

epsilon = 1e-06
rope_base = 10000.0
low = jnp.bfloat16
wide = jnp.float32


def mul(left, right):
    return jnp.dot(left, right, preferred_element_type=wide)


def mul_t(left, right):
    return lax.dot_general(left, right, (((1,), (1,)), ((), ())), preferred_element_type=wide)


def t_mul(left, right):
    return lax.dot_general(left, right, (((0,), (0,)), ((), ())), preferred_element_type=wide)


def ring_order(count, width):
    if width < 2 or count % width or (count // width) % 2:
        return list(range(count))
    depth = count // width
    walk = [0]
    for z in range(depth):
        columns = range(1, width) if z % 2 == 0 else range(width - 1, 0, -1)
        walk += [z * width + x for x in columns]
    walk += [z * width for z in range(depth - 1, 0, -1)]
    return walk


MESH = pl.DeviceIdType.MESH
ANY = pl.BlockSpec(memory_space=pl.ANY)
VMEM = pl.BlockSpec(memory_space=pltpu.VMEM)


def pick(index, table):
    result = jnp.int32(table[0])
    for spot, value in enumerate(table):
        if spot:
            result = jnp.where(index == spot, jnp.int32(value), result)
    return result


class Places:
    def __init__(self, n_f, n_seq):
        self.n_f, self.n_seq, self.chips = n_f, n_seq, n_seq // CORES
        self.walk = ring_order(n_f, n_seq // CORES)
        spots = [0] * n_f
        for spot, device in enumerate(self.walk):
            spots[device] = spot
        self.f, self.me = lax.axis_index("fsdp"), lax.axis_index("seq")
        self.spot = pick(self.f, spots)
        self.y, self.core = self.me // CORES, lax.rem(self.me, CORES)

    def at(self, offset):
        return pick(lax.rem(self.spot + offset + self.n_f, self.n_f), self.walk)

    def seq(self, k, c):
        return lax.rem(self.y + k + self.chips, self.chips) * CORES + lax.rem(
            self.core + c, CORES
        )

    def greet(self, ring):
        barrier = pltpu.get_barrier_semaphore()
        friends = [{"seq": self.seq(0, 1)}]
        friends += [{"seq": self.seq(k, 0)} for k in range(1, self.chips)]
        if ring:
            friends += [{"fsdp": self.at(1)}, {"fsdp": self.at(-1)}]
        for friend in friends:
            pl.semaphore_signal(barrier, inc=1, device_id=friend, device_id_type=MESH)
        pl.semaphore_wait(barrier, len(friends))


def remote(source, target, send, receive, device):
    return pltpu.make_async_remote_copy(
        src_ref=source,
        dst_ref=target,
        send_sem=send,
        recv_sem=receive,
        device_id=device,
        device_id_type=MESH,
    )


def brief(us):
    return pl.CostEstimate(
        flops=int(us * 1.0e9), bytes_accessed=int(us * 1.0e6), transcendentals=0
    )


def params(number):
    return pltpu.CompilerParams(
        collective_id=number, has_side_effects=True, vmem_limit_bytes=56 * 2**20
    )


def ring_steps(n_f):
    order = []
    for step in range(1, n_f // 2 + 1):
        order.append((step, 1))
        if step <= (n_f - 1) // 2:
            order.append((step, -1))
    return order


def pack_small(gain1, gain2, attention, lower, raises, raises2, outward, n_seq):
    groups = [(attention, gain1), (raises, None), (outward, None), (raises2, None), (lower, gain2)]
    shares = (CORES, CORES, n_seq, n_seq, n_seq)

    def body(*refs):
        refs = list(refs)
        for (parts, gain), out in zip(groups, refs[-len(groups) :], strict=True):
            factor = None if gain is None else refs.pop(0)[...]
            at = 0
            for part in parts:
                block = refs.pop(0)[...]
                if factor is not None:
                    block = (block.astype(wide) * factor).astype(low)
                out[:, at : at + part.shape[1]] = block
                at += part.shape[1]
            if at < out.shape[1]:
                out[:, at:] = jnp.zeros((out.shape[0], out.shape[1] - at), low)

    sizes = []
    for (parts, _), ways in zip(groups, shares, strict=True):
        total = sum(part.shape[1] for part in parts)
        sizes.append((parts[0].shape[0], total + -total % (128 * ways)))
    operands = []
    for parts, gain in groups:
        operands += ([] if gain is None else [gain]) + list(parts)
    return pl.pallas_call(
        body,
        out_shape=tuple(jax.ShapeDtypeStruct(size, low) for size in sizes),
        compiler_params=pltpu.CompilerParams(vmem_limit_bytes=48 * 2**20),
    )(*operands)


def gather_whole(blocks, spread, number, n_f, n_seq):
    count = len(blocks)
    chips = n_seq // CORES
    steps = ring_steps(n_f)
    order = [j for j in range(count) if spread[j]] + [j for j in range(count) if not spread[j]]

    def body(*refs):
        ins, outs = refs[:count], refs[count : 2 * count]
        local, ring_s, ring_r, y_s, y_r, core_s, core_r = refs[2 * count :]
        here = Places(n_f, n_seq)
        started = []

        def share(j, k, c):
            spot = here.seq(k, c) if spread[j] else lax.rem(here.core + c, CORES)
            width = ins[j].shape[-1] // (n_seq if spread[j] else CORES)
            return (slice(None), pl.ds(pl.multiple_of(spot * width, 128), width))

        def far(j):
            return range(1, chips if spread[j] else 1)

        copies = []
        for j in range(count):
            copy = pltpu.make_async_copy(ins[j], outs[j].at[here.f], local.at[j])
            copy.start()
            copies.append(copy)
        here.greet(True)

        def flip(j):
            return 1 if j == 0 else -1

        def forward(j, step, way):
            owner = here.at(-flip(j) * way * (step - 1))
            mine = share(j, 0, 0)
            source = ins[j].at[mine] if step == 1 else outs[j].at[(owner, *mine)]
            at = steps.index((step, way))
            copy = remote(
                source,
                outs[j].at[(owner, *mine)],
                ring_s.at[j, at],
                ring_r.at[j, at],
                {"fsdp": here.at(flip(j) * way)},
            )
            copy.start()
            started.append(copy)

        def landed(j, step, way):
            owner = here.at(-flip(j) * way * step)
            at = steps.index((step, way))
            block = outs[j].at[(owner, *share(j, 0, 0))]
            remote(block, block, ring_s.at[j, at], ring_r.at[j, at], {"fsdp": here.at(flip(j) * way)}).wait_recv()
            return owner

        def to_core(j, at, k, owner):
            block = outs[j].at[(owner, *share(j, k, 0))]
            copy = remote(
                block, block, core_s.at[j, at, k], core_r.at[j, at, k], {"seq": here.seq(0, 1)}
            )
            copy.start()
            started.append(copy)

        for j in order:
            for way in (1, -1):
                forward(j, 1, way)
        for at, (step, way) in enumerate(steps):
            for j in order:
                owner = landed(j, step, way)
                if (step + 1, way) in steps:
                    forward(j, step + 1, way)
                block = outs[j].at[(owner, *share(j, 0, 0))]
                for k in far(j):
                    copy = remote(
                        block, block, y_s.at[j, at, k], y_r.at[j, at, k], {"seq": here.seq(-k, 0)}
                    )
                    copy.start()
                    started.append(copy)
                to_core(j, at, 0, owner)
        for at, (step, way) in enumerate(steps):
            for j in order:
                owner = here.at(-flip(j) * way * step)
                for k in far(j):
                    block = outs[j].at[(owner, *share(j, k, 0))]
                    remote(
                        block, block, y_s.at[j, at, k], y_r.at[j, at, k], {"seq": here.seq(-k, 0)}
                    ).wait_recv()
                    to_core(j, at, k, owner)
        for at, (step, way) in enumerate(steps):
            for j in order:
                owner = here.at(-flip(j) * way * step)
                for k in [0, *far(j)]:
                    block = outs[j].at[(owner, *share(j, k, 1))]
                    remote(
                        block, block, core_s.at[j, at, k], core_r.at[j, at, k], {"seq": here.seq(0, 1)}
                    ).wait_recv()
        for copy in started:
            copy.wait_send()
        for copy in copies:
            copy.wait()

    sems = pltpu.SemaphoreType.DMA
    return pl.pallas_call(
        body,
        out_shape=tuple(jax.ShapeDtypeStruct((n_f,) + b.shape, b.dtype) for b in blocks),
        in_specs=[ANY] * count,
        out_specs=(ANY,) * count,
        scratch_shapes=[sems((count,))]
        + [sems((count, len(steps)))] * 2
        + [sems((count, len(steps), chips))] * 4,
        compiler_params=params(number),
    )(*blocks)


def gather_group(block, number, n_seq):
    rows = block.shape[0]
    chips = n_seq // CORES
    parts = 4 if rows % 64 == 0 else 1
    size = rows // parts

    def body(x, out, local, y_s, y_r, core_s, core_r):
        here = Places(1, n_seq)
        own = pltpu.make_async_copy(x, out.at[0], local)
        own.start()
        here.greet(False)
        started = []

        def to_core(source, k, part):
            cut = pl.ds(part * size, size)
            copy = remote(
                source.at[cut],
                out.at[k * CORES + 1, cut],
                core_s.at[k, part],
                core_r.at[k, part],
                {"seq": here.seq(0, 1)},
            )
            copy.start()
            started.append(copy)

        def over(k, part):
            cut = pl.ds(part * size, size)
            return remote(
                x.at[cut],
                out.at[k * CORES, cut],
                y_s.at[k, part],
                y_r.at[k, part],
                {"seq": here.seq(-k, 0)},
            )

        for part in range(parts):
            for k in range(1, chips):
                copy = over(k, part)
                copy.start()
                started.append(copy)
            to_core(x, 0, part)
        for part in range(parts):
            for k in range(1, chips):
                over(k, part).wait_recv()
                to_core(out.at[k * CORES], k, part)
        for part in range(parts):
            for k in range(chips):
                cut = pl.ds(part * size, size)
                block = out.at[k * CORES + 1, cut]
                remote(
                    block, block, core_s.at[k, part], core_r.at[k, part], {"seq": here.seq(0, 1)}
                ).wait_recv()
        for copy in started:
            copy.wait_send()
        own.wait()

    sems = pltpu.SemaphoreType.DMA
    return pl.pallas_call(
        body,
        out_shape=jax.ShapeDtypeStruct((n_seq,) + block.shape, block.dtype),
        in_specs=[ANY],
        out_specs=ANY,
        scratch_shapes=[sems(())] + [sems((chips, parts))] * 4,
        compiler_params=params(number),
    )(block)


def scatter_group(terms, number):
    n_seq, rows, columns = terms.shape
    chips = n_seq // CORES
    parts = 4 if rows % 64 == 0 else 1
    size = rows // parts

    def body(x, out, near, sums, far, y_s, y_r, core_s, core_r):
        here = Places(1, n_seq)
        here.greet(False)
        started = []

        def cross(k, part):
            cut = pl.ds(part * size, size)
            return remote(
                x.at[k * CORES + 1, cut],
                near.at[k, cut],
                core_s.at[k, part],
                core_r.at[k, part],
                {"seq": here.seq(0, 1)},
            )

        def over(k, part):
            cut = pl.ds(part * size, size)
            return remote(
                sums.at[k, cut],
                far.at[k, cut],
                y_s.at[k, part],
                y_r.at[k, part],
                {"seq": here.seq(k, 0)},
            )

        for k in [*range(1, chips), 0]:
            for part in range(parts):
                copy = cross(k, part)
                copy.start()
                started.append(copy)
        for k in range(1, chips):
            for part in range(parts):
                cut = pl.ds(part * size, size)
                cross(k, part).wait_recv()
                total = x[k * CORES, cut, :].astype(wide) + near[k, cut, :].astype(wide)
                sums[k, cut, :] = total.astype(low)
                copy = over(k, part)
                copy.start()
                started.append(copy)
        for part in range(parts):
            cut = pl.ds(part * size, size)
            cross(0, part).wait_recv()
            out[cut, :] = x[0, cut, :].astype(wide) + near[0, cut, :].astype(wide)
        for part in range(parts):
            cut = pl.ds(part * size, size)
            for k in range(1, chips):
                over(k, part).wait_recv()
                out[cut, :] = out[cut, :] + far[k, cut, :].astype(wide)
        for copy in started:
            copy.wait_send()

    sems = pltpu.SemaphoreType.DMA
    buffer = pltpu.VMEM((chips, rows, columns), low)
    return pl.pallas_call(
        body,
        out_shape=jax.ShapeDtypeStruct((rows, columns), wide),
        in_specs=[VMEM],
        out_specs=VMEM,
        scratch_shapes=[buffer] * 3 + [sems((chips, parts))] * 4,
        compiler_params=params(number),
    )(terms)


def scatter_whole(packs, block, small, number, n_seq):
    wanted = [pack.shape[2] for pack in packs]
    gaps = [-count % (128 * CORES) for count in wanted]
    packs = [
        jnp.pad(pack, ((0, 0), (0, 0), (0, gap))) if gap else pack
        for pack, gap in zip(packs, gaps, strict=True)
    ]
    n_f, count = packs[0].shape[0], len(packs)
    chips = n_seq // CORES
    widths = [pack.shape[2] // CORES for pack in packs]
    steps = ring_steps(n_f)
    offsets = [way * step for step, way in reversed(steps)] + [0]
    last = {way: max(step for step, w in steps if w == way) for way in (1, -1)}

    def body(*refs):
        refs = list(refs)

        def take(n):
            taken, refs[:] = refs[:n], refs[n:]
            return taken

        xs = take(count)
        block_in, small_in = take(2)
        outs = take(count)
        block_out, small_out = take(2)
        nears, terms, moves, parts = (take(count) for _ in range(4))
        (smalls,) = take(1)
        core_s, core_r, ring_s, ring_r, y_s, y_r, side_s, side_r = take(8)
        local, far_s, far_r, near_s, near_r = take(5)
        here = Places(n_f, n_seq)
        own = pltpu.make_async_copy(block_in, block_out.at[0], local)
        own.start()
        smalls[here.me] = small_in[...]
        here.greet(True)
        started = []

        def flip(j):
            return 1 if j == 0 else -1

        def go(copy):
            copy.start()
            started.append(copy)

        def share(j, spot):
            return pl.ds(pl.multiple_of(spot * widths[j], 128), widths[j])

        other = lax.rem(here.core + 1, CORES)

        def cross(j, i):
            return remote(
                xs[j].at[here.at(flip(j) * offsets[i]), :, share(j, other)],
                nears[j].at[i],
                core_s.at[j, i],
                core_r.at[j, i],
                {"seq": here.seq(0, 1)},
            )

        def hop(j, step, way):
            at = steps.index((step, way))
            return remote(
                terms[j].at[at],
                moves[j].at[at],
                ring_s.at[j, at],
                ring_r.at[j, at],
                {"fsdp": here.at(flip(j) * way)},
            )

        def swap(j, k, spot):
            slot = parts[j].at[spot]
            return remote(slot, slot, y_s.at[j, k], y_r.at[j, k], {"seq": here.seq(-k, 0)})

        def far_block(k):
            return remote(
                block_in, block_out.at[k * CORES], far_s.at[k], far_r.at[k], {"seq": here.seq(-k, 0)}
            )

        def near_block(k):
            source = block_in if k == 0 else block_out.at[k * CORES]
            return remote(
                source,
                block_out.at[k * CORES + 1],
                near_s.at[k],
                near_r.at[k],
                {"seq": here.seq(0, 1)},
            )

        def far_small(k, spot):
            slot = smalls.at[spot]
            return remote(
                slot, slot, far_s.at[chips + k], far_r.at[chips + k], {"seq": here.seq(-k, 0)}
            )

        def near_small(k, spot):
            slot = smalls.at[spot]
            return remote(
                slot, slot, near_s.at[chips + k], near_r.at[chips + k], {"seq": here.seq(0, 1)}
            )

        for k in range(1, chips):
            go(far_small(k, here.me))
            go(far_block(k))
        for i in range(n_f):
            for j in range(count):
                go(cross(j, i))
        go(near_small(0, here.me))
        go(near_block(0))
        for i in range(n_f):
            for j in range(count):
                cross(j, i).wait_recv()
                total = xs[j][here.at(flip(j) * offsets[i]), :, share(j, here.core)].astype(wide)
                total = total + nears[j][i].astype(wide)
                if offsets[i]:
                    step, way = abs(offsets[i]), 1 if offsets[i] > 0 else -1
                    if step < last[way]:
                        hop(j, step + 1, way).wait_recv()
                        total = total + moves[j][steps.index((step + 1, way))].astype(wide)
                    terms[j][steps.index((step, way))] = total.astype(low)
                    go(hop(j, step, way))
                else:
                    for way in (1, -1):
                        if last[way] >= 1:
                            hop(j, 1, way).wait_recv()
                            total = total + moves[j][steps.index((1, way))].astype(wide)
                    parts[j][here.y] = total.astype(low)
                    for k in range(1, chips):
                        go(swap(j, k, here.y))

        def side(j, core):
            columns = outs[j].at[:, share(j, core)]
            return remote(columns, columns, side_s.at[j], side_r.at[j], {"seq": here.seq(0, 1)})

        for k in range(1, chips):
            far_small(k, here.seq(k, 0)).wait_recv()
            go(near_small(k, here.seq(k, 0)))
            far_block(k).wait_recv()
            go(near_block(k))
        for j in range(count):
            for k in range(1, chips):
                swap(j, k, lax.rem(here.y + k, chips)).wait_recv()
            total = parts[j][0].astype(wide)
            for y in range(1, chips):
                total = total + parts[j][y].astype(wide)
            outs[j][:, share(j, here.core)] = total.astype(low)
            go(side(j, here.core))
        for k in range(chips):
            near_small(k, here.seq(k, 1)).wait_recv()
        total = smalls[0].astype(wide)
        for spot in range(1, n_seq):
            total = total + smalls[spot].astype(wide)
        small_out[...] = total
        for k in range(chips):
            near_block(k).wait_recv()
        for j in range(count):
            side(j, other).wait_recv()
        for copy in started:
            copy.wait_send()
        own.wait()

    sems = pltpu.SemaphoreType.DMA
    shapes = [(pack.shape[1], width) for pack, width in zip(packs, widths, strict=True)]
    near = [pltpu.VMEM((n_f, *shape), low) for shape in shapes]
    ring = [pltpu.VMEM((len(steps), *shape), low) for shape in shapes]
    part = [pltpu.VMEM((chips, *shape), low) for shape in shapes]
    results = pl.pallas_call(
        body,
        out_shape=tuple(jax.ShapeDtypeStruct(pack.shape[1:], low) for pack in packs)
        + (
            jax.ShapeDtypeStruct((n_seq, *block.shape), low),
            jax.ShapeDtypeStruct(small.shape, wide),
        ),
        in_specs=[VMEM] * count + [ANY, VMEM],
        out_specs=(VMEM,) * count + (ANY, VMEM),
        scratch_shapes=near
        + ring * 2
        + part
        + [pltpu.VMEM((n_seq, *small.shape), low)]
        + [sems((count, n_f))] * 2
        + [sems((count, len(steps)))] * 2
        + [sems((count, chips))] * 2
        + [sems((count,))] * 2
        + [sems(())]
        + [sems((2 * chips,))] * 4,
        compiler_params=params(number),
    )(*packs, block, small)
    sums = [result[:, :size] for result, size in zip(results[:count], wanted, strict=True)]
    return sums, results[count], results[count + 1]


def ring_terms(sides, outs, n_f, n_seq, dtype):
    flat, spots = [], []
    left = 0
    for side in sides:
        top = 0
        for part in side:
            flat.append(part)
            spots.append((top, left))
            top += part.shape[1]
        left += side[0].shape[2]
    moved = [block for _, _, _, came in outs for block, _ in came]

    def body(*refs):
        parts, moves = refs[: len(flat)], list(refs[len(flat) : len(flat) + len(moved)])
        results = refs[len(flat) + len(moved) : len(flat) + len(moved) + len(outs)]
        scratch, sem = refs[len(flat) + len(moved) + len(outs) : -1], refs[-1]
        here = Places(n_f, n_seq)
        copies = []
        for i, (offset, first, stop, _) in enumerate(outs):
            owner = here.at(offset)
            for at, (part, (above, before)) in enumerate(zip(parts, spots, strict=True)):
                start, end = max(first, before), min(stop, before + part.shape[2])
                if start < end:
                    copies.append(
                        pltpu.make_async_copy(
                            part.at[owner, :, start - before : end - before],
                            scratch[i].at[
                                above : above + part.shape[1], start - first : end - first
                            ],
                            sem.at[i, at],
                        )
                    )
        for copy in copies:
            copy.start()
        for copy in copies:
            copy.wait()
        for i, (_, first, stop, came) in enumerate(outs):
            edges = sorted(
                {first, stop}
                | {c for _, c in came}
                | {c + block.shape[1] for block, c in came}
            )
            here_moves = [(moves.pop(0), c) for _, c in came]
            for start, end in zip(edges, edges[1:]):
                total = scratch[i][:, start - first : end - first].astype(wide)
                for ref, c in here_moves:
                    if c <= start and end <= c + ref.shape[1]:
                        total = total + ref[:, start - c : end - c].astype(wide)
                results[i][:, start - first : end - first] = total.astype(dtype)

    rows = sum(part.shape[1] for part in sides[0])
    shapes = [(rows, stop - first) for _, first, stop, _ in outs]
    return pl.pallas_call(
        body,
        out_shape=tuple(jax.ShapeDtypeStruct(shape, dtype) for shape in shapes),
        in_specs=[ANY] * len(flat) + [VMEM] * len(moved),
        out_specs=(VMEM,) * len(outs),
        scratch_shapes=[pltpu.VMEM(shape, low) for shape in shapes]
        + [pltpu.SemaphoreType.DMA((len(outs), len(flat)))],
        cost_estimate=brief(1),
        compiler_params=pltpu.CompilerParams(vmem_limit_bytes=32 * 2**20),
    )(*flat, *moved)


class Ring:
    def __init__(self, count, width):
        self.count = count
        walk = ring_order(count, width)
        self.up = [(walk[i], walk[(i + 1) % count]) for i in range(count)]
        self.down = [(b, a) for a, b in self.up]

    def hop(self, block, way):
        return lax.ppermute(block, "fsdp", self.up if way > 0 else self.down)


class Gathering:
    def __init__(self, ring, block):
        self.ring = ring
        self.step, self.steps = 0, ring.count // 2
        self.moving = (block, block)
        self.places = [(0, 0)]
        self.blocks = [block]

    def advance(self):
        if self.step == self.steps:
            return
        self.step += 1
        first, second = self.moving
        if self.step < self.steps:
            self.moving = (self.ring.hop(first, 1), self.ring.hop(second, -1))
            self.places += [(-self.step, 0), (self.step, 0)]
        else:
            half = first.shape[1] // 256 * 128
            self.moving = (
                self.ring.hop(first[:, :half], 1),
                self.ring.hop(second[:, half:], -1),
            )
            self.places += [(self.step, 0), (self.step, half)]
        self.blocks += list(self.moving)

    def done(self):
        while self.step < self.steps:
            self.advance()
        return [
            (offset, block, column)
            for (offset, column), block in zip(self.places, self.blocks, strict=True)
        ]

    def live(self):
        return (self.moving, self.blocks)

    def restore(self, live):
        self.moving, self.blocks = live


class Scattering:
    def __init__(self, ring, sides, n_seq):
        self.ring, self.sides, self.n_seq = ring, sides, n_seq
        self.width = sum(side[0].shape[2] for side in sides)
        self.half = self.width // 256 * 128
        self.step, self.steps = 0, ring.count // 2
        self.moving = ()

    def terms(self, outs, dtype):
        return ring_terms(self.sides, outs, self.ring.count, self.n_seq, dtype)

    def advance(self):
        if self.step == self.steps:
            return
        self.step += 1
        offset = self.steps - self.step + 1
        if self.step == 1:
            outs = [(offset, 0, self.half, []), (offset, self.half, self.width, [])]
        else:
            ahead, back = self.moving
            right = self.half if self.step == 2 else 0
            outs = [
                (offset, 0, self.width, [(ahead, 0)]),
                (-offset, 0, self.width, [(back, right)]),
            ]
        ahead, back = self.terms(outs, low)
        self.moving = (self.ring.hop(ahead, 1), self.ring.hop(back, -1))

    def done(self, dtype):
        while self.step < self.steps:
            self.advance()
        right = self.half if self.steps == 1 else 0
        ahead, back = self.moving
        (total,) = self.terms([(0, 0, self.width, [(ahead, 0), (back, right)])], dtype)
        return total

    def live(self):
        return self.moving

    def restore(self, live):
        self.moving = live


def tie(movers, values):
    lives, values = lax.optimization_barrier(([mover.live() for mover in movers], values))
    for mover, live in zip(movers, lives, strict=True):
        mover.restore(live)
    return values


class Group:
    def __init__(self, count):
        self.count = count
        self.chips = count // CORES
        me = lax.axis_index("seq")
        self.y, self.core = me // CORES, lax.rem(me, CORES)
        self.sibling = [(i, i ^ 1) for i in range(count)]
        self.order = [(k, c) for k in range(self.chips) for c in range(CORES)]

    def shift(self, k):
        n = self.chips
        return [(i, ((i // CORES + k) % n) * CORES + i % CORES) for i in range(self.count)]

    def index(self, k, c):
        return lax.rem(self.y + k, self.chips) * CORES + (self.core + c) % CORES

    def over(self, block):
        return [block] + [
            lax.ppermute(block, "seq", self.shift(-k)) for k in range(1, self.chips)
        ]

    def across(self, blocks):
        out = []
        for block in blocks:
            out += [block, lax.ppermute(block, "seq", self.sibling)]
        return out

    def swap(self, block):
        return lax.ppermute(block, "seq", self.sibling)

    def cross(self, terms):
        return [
            lax.ppermute(terms[k * CORES + 1], "seq", self.sibling) for k in range(self.chips)
        ]

    def send(self, sums):
        return [
            lax.ppermute(sums[k].astype(low), "seq", self.shift(k)) for k in range(1, self.chips)
        ]

    def laid(self, pieces, axis, dtype):
        width = pieces[0].shape[axis]
        shape = list(pieces[0].shape)
        shape[axis] = width * self.count
        out = jnp.zeros(shape, dtype)
        for (k, c), piece in zip(self.order, pieces, strict=True):
            out = lax.dynamic_update_slice_in_dim(
                out, piece.astype(dtype), self.index(k, c) * width, axis
            )
        return out


class Summing:
    def __init__(self, values, axes):
        self.values = values
        self.steps = [
            (axis, 1 << bit)
            for axis in axes
            for bit in range((lax.axis_size(axis) - 1).bit_length())
        ]
        assert all(lax.axis_size(axis) & (lax.axis_size(axis) - 1) == 0 for axis in axes)

    def advance(self):
        if self.steps:
            axis, step = self.steps.pop(0)
            pairs = [(i, i ^ step) for i in range(lax.axis_size(axis))]
            self.values = self.values + lax.ppermute(self.values, axis, pairs)

    def done(self):
        while self.steps:
            self.advance()
        return self.values

    def live(self):
        return self.values

    def restore(self, live):
        self.values = live


def cut_columns(weights, raises, gains, n_f, n_seq, slab):
    rows, ff = weights[0].shape
    rank_rows = raises[0].shape[0]
    block, cut = ff // n_f, ff // (n_f * n_seq)

    def body(gain_ref, w0, w1, r0, r1, out):
        me = lax.axis_index("seq")

        def run(ref, spot):
            runs = [
                ref[:, f * block + spot * cut : f * block + (spot + 1) * cut] for f in range(n_f)
            ]
            gap = slab - n_f * cut
            if gap:
                runs.append(jnp.zeros((ref.shape[0], gap), ref.dtype))
            return jnp.concatenate(runs, axis=1)

        for spot in range(n_seq):

            @pl.when(me == spot)
            def _():
                for side, (weight, raised) in enumerate(((w0, r0), (w1, r1))):
                    at = side * slab
                    out[:rank_rows, at : at + slab] = run(raised, spot)
                    scaled = run(weight, spot).astype(wide) * gain_ref[...]
                    out[rank_rows:, at : at + slab] = scaled.astype(low)

    return pl.pallas_call(
        body,
        out_shape=jax.ShapeDtypeStruct((rank_rows + rows, 2 * slab), low),
        compiler_params=pltpu.CompilerParams(vmem_limit_bytes=48 * 2**20),
    )(gains, *weights, *raises)


def place_columns(pieces, gains, n_f, n_seq, rank_rows, ff, slab):
    rows = pieces.shape[1] - rank_rows
    cut = ff // (n_f * n_seq)
    chips = n_seq // CORES

    def body(gain_ref, x, w0, w1, r0, r1):
        me = lax.axis_index("seq")
        y, core = me // CORES, lax.rem(me, CORES)

        def spot_of(spot):
            ahead = lax.rem(spot // CORES - y + chips, chips)
            return ahead * CORES + lax.rem(spot % CORES + core, CORES)

        def fill(out, first, count, at, gain):
            whole = [x[spot_of(spot), first : first + count, at : at + slab] for spot in range(n_seq)]
            runs = [
                whole[spot][:, f * cut : (f + 1) * cut] for f in range(n_f) for spot in range(n_seq)
            ]
            result = jnp.concatenate(runs, axis=1).astype(wide)
            out[...] = result if gain is None else result * gain

        for side, (weight, raised) in enumerate(((w0, r0), (w1, r1))):
            fill(raised, 0, rank_rows, side * slab, None)
            fill(weight, rank_rows, rows, side * slab, gain_ref[...])

    return pl.pallas_call(
        body,
        out_shape=(jax.ShapeDtypeStruct((rows, ff), wide),) * 2
        + (jax.ShapeDtypeStruct((rank_rows, ff), wide),) * 2,
        compiler_params=pltpu.CompilerParams(vmem_limit_bytes=56 * 2**20),
    )(gains, pieces)


def gelu_parts(gate):
    scale = (2.0 / jnp.pi) ** 0.5
    cube = 0.044715
    square = gate * gate
    half = 0.5 * jnp.tanh(gate * (scale + scale * cube * square)) + 0.5
    value = gate * half
    slope = half + value * (1.0 - half) * (2.0 * scale + 6.0 * scale * cube * square)
    return value, slope


def project(unit, side, ups, cosine, sine, hq, rank):
    tokens = unit.shape[0]
    lin = hq + 2 * HD
    half = HD // 2

    def body(x, weights, raises, cos, sin, queries, both, inner):
        low_inner = mul(x[...], weights[:, lin:]).astype(low)
        inner[...] = low_inner

        def head(at, own):
            columns = slice(at, at + HD)
            return mul(x[...], weights[:, columns]) + mul(
                low_inner[:, own * rank : (own + 1) * rank], raises[:, columns]
            )

        def turned(values):
            first, second = values[:, :half], values[:, half:]
            c, s = cos[...], sin[...]
            return jnp.concatenate(
                [first * c - second * s, second * c + first * s], axis=1
            ).astype(low)

        for at in range(0, hq, HD):
            queries[:, at : at + HD] = turned(head(at, 0))
        both[:, :HD] = turned(head(hq, 1))
        both[:, HD:] = head(hq + HD, 2).astype(low)

    return pl.pallas_call(
        body,
        out_shape=(
            jax.ShapeDtypeStruct((tokens, hq), low),
            jax.ShapeDtypeStruct((tokens, 2 * HD), low),
            jax.ShapeDtypeStruct((tokens, 3 * rank), low),
        ),
        cost_estimate=brief(2),
        compiler_params=pltpu.CompilerParams(vmem_limit_bytes=48 * 2**20),
    )(unit, side, ups, cosine, sine)


def attention(queries, both, mask, rows):
    n_seq, tokens, _ = both.shape
    length = tokens // rows
    scale = HD ** (-0.5)

    def body(q, kv, hidden, out, log_total):
        for r in range(rows):
            at = slice(r * length, (r + 1) * length)
            keys = kv[:, at, :HD].reshape(n_seq * length, HD)
            values = kv[:, at, HD:].reshape(n_seq * length, HD)
            for h in range(H):
                head = slice(h * HD, (h + 1) * HD)
                scores = mul_t(q[at, head], keys) * scale + hidden[r]
                top = jnp.max(scores, axis=-1, keepdims=True)
                weights = jnp.exp(scores - top)
                total = jnp.sum(weights, axis=-1, keepdims=True)
                out[at, head] = (mul(weights.astype(low), values) / total).astype(low)
                log_total[r, h] = top + jnp.log(total)

    return pl.pallas_call(
        body,
        out_shape=(
            jax.ShapeDtypeStruct(queries.shape, low),
            jax.ShapeDtypeStruct((rows, H, length, 1), wide),
        ),
        cost_estimate=brief(2),
        compiler_params=pltpu.CompilerParams(vmem_limit_bytes=48 * 2**20),
    )(queries, both, mask)


def attention_back(queries, both, mask, log_total, out, g_out, cosine, sine, rows):
    n_seq, tokens, _ = both.shape
    length = tokens // rows
    scale = HD ** (-0.5)
    half = HD // 2

    def body(q, kv, hidden, logs, o, g, cos, sin, g_q, g_both):
        for r in range(rows):
            at = slice(r * length, (r + 1) * length)
            keys = kv[:, at, :HD].reshape(n_seq * length, HD)
            values = kv[:, at, HD:].reshape(n_seq * length, HD)
            d_keys = d_values = None
            for h in range(H):
                head = slice(h * HD, (h + 1) * HD)
                scores = mul_t(q[at, head], keys) * scale + hidden[r]
                probs = jnp.exp(scores - logs[r, h])
                grad = g[at, head]
                dots = jnp.sum(
                    grad.astype(wide) * o[at, head].astype(wide), axis=-1, keepdims=True
                )
                d_scores = (probs * (mul_t(grad, values) - dots)).astype(low)
                d_query = mul(d_scores, keys) * scale
                first, second = d_query[:, :half], d_query[:, half:]
                c, s = cos[at, :], sin[at, :]
                turned = jnp.concatenate([first * c + second * s, second * c - first * s], axis=1)
                g_q[at, head] = turned.astype(low)
                d_key = t_mul(d_scores, q[at, head])
                d_value = t_mul(probs.astype(low), grad)
                d_keys = d_key if d_keys is None else d_keys + d_key
                d_values = d_value if d_values is None else d_values + d_value
            g_both[:, at, :HD] = (d_keys * scale).astype(low).reshape(n_seq, length, HD)
            g_both[:, at, HD:] = d_values.astype(low).reshape(n_seq, length, HD)

    return pl.pallas_call(
        body,
        out_shape=(
            jax.ShapeDtypeStruct(queries.shape, low),
            jax.ShapeDtypeStruct(both.shape, low),
        ),
        cost_estimate=brief(3),
        compiler_params=pltpu.CompilerParams(vmem_limit_bytes=56 * 2**20),
    )(queries, both, mask, log_total, out, g_out, cosine, sine)


def by_owner(out, first, product, n_f):
    rows = product.shape[0] // n_f
    for f in range(n_f):
        out[f, first : first + rows, :] = product[f * rows : (f + 1) * rows].astype(low)
    return first + rows


def output_gradients(attn, inner, g_branch, ready, n_f):
    columns = g_branch.shape[1]
    wide_columns = columns + -columns % (128 * CORES)
    sizes = [part.shape[-2] if part.ndim == 3 else part.shape[1] // n_f for part in (attn, inner, ready)]

    def body(a, b, g, done, out):
        main = out.at[:, :, :columns]
        first = by_owner(main, 0, t_mul(a[...], g[...]), n_f)
        first = by_owner(main, first, t_mul(b[...], g[...]), n_f)
        out[:, first:, :columns] = done[...]
        if columns < wide_columns:
            out[:, :, columns:] = jnp.zeros((n_f, sum(sizes), wide_columns - columns), low)

    return pl.pallas_call(
        body,
        out_shape=jax.ShapeDtypeStruct((n_f, sum(sizes), wide_columns), low),
        cost_estimate=brief(2),
        compiler_params=pltpu.CompilerParams(vmem_limit_bytes=40 * 2**20),
    )(attn, inner, g_branch, ready)


def query_gradients(unit, inner, g_q, raises, side, hq, rank, n_f):
    tokens, width = unit.shape
    lin = hq + 2 * HD
    rows = width // n_f + rank // n_f

    def body(x, low_inner, g, ups, weights, e1, out):
        g_inner = mul_t(g[...], ups[:, :hq]).astype(low)
        e1[...] = mul_t(g[...], weights[:, :hq]) + mul_t(g_inner, weights[:, lin : lin + rank])
        first = by_owner(out, 0, t_mul(x[...], g[...]), n_f)
        by_owner(out, first, t_mul(low_inner[...], g[...]), n_f)

    return pl.pallas_call(
        body,
        out_shape=(
            jax.ShapeDtypeStruct((tokens, width), wide),
            jax.ShapeDtypeStruct((n_f, rows, hq), low),
        ),
        cost_estimate=brief(2),
        compiler_params=pltpu.CompilerParams(vmem_limit_bytes=48 * 2**20),
    )(unit, inner, g_q, raises, side)


def lay_rows(pieces, cut_at, n_seq):
    rows, columns = pieces[0].shape
    chips = n_seq // CORES

    def body(*refs):
        me = lax.axis_index("seq")
        y, core = me // CORES, lax.rem(me, CORES)
        for at, ref in enumerate(refs[:n_seq]):
            spot = lax.rem(y + at // CORES, chips) * CORES + lax.rem(core + at % CORES, CORES)
            refs[n_seq][spot] = ref[:, :cut_at].astype(wide)
            refs[n_seq + 1][spot] = ref[:, cut_at:].astype(wide)

    results = pl.pallas_call(
        body,
        out_shape=(
            jax.ShapeDtypeStruct((n_seq, rows, cut_at), wide),
            jax.ShapeDtypeStruct((n_seq, rows, columns - cut_at), wide),
        ),
        cost_estimate=brief(1),
        compiler_params=pltpu.CompilerParams(vmem_limit_bytes=32 * 2**20),
    )(*pieces)
    return [result.reshape(n_seq * rows, -1) for result in results]


def landing(items, buffers, rows_first, sem, here):
    copies = []
    for at, (offset, ref, column) in enumerate(items):
        owner = here.at(offset)
        first = 0
        for part, buffer in enumerate(buffers):
            count = rows_first[part]
            copies.append(
                pltpu.make_async_copy(
                    ref.at[first : first + count],
                    buffer.at[owner, :, column : column + ref.shape[1]],
                    sem.at[at, part],
                )
            )
            first += count
    for copy in copies:
        copy.start()
    for copy in copies:
        copy.wait()


def mlp_forward(
    items, tokens2, adapters, before, part, n_f, n_seq, rank_rows, own_rows, slab
):
    count, width = tokens2.shape
    rank = rank_rows * n_f
    tile = 256 if slab % 256 == 0 else 128
    chunk = 512
    first, stop = part
    wanted = []
    for side in range(2):
        start, end = side * slab + first * tile, side * slab + stop * tile
        for at, (offset, block, column) in enumerate(items):
            low_end, high_end = max(start, column), min(end, column + block.shape[1])
            if low_end < high_end:
                wanted.append((at, offset, low_end - column, high_end - column, side, low_end - start))

    def body(x, lower_g, lower_u, *refs):
        blocks, refs = refs[: len(items)], refs[len(items) + len(before) :]
        hidden, back_g, back_u, full_g, full_u, raised_g, raised_u = refs[:7]
        raises, weights, merged, sem = refs[7:]
        here = Places(n_f, n_seq)
        step = pl.program_id(0)

        @pl.when(step == 0)
        def _():
            copies = []
            for number, (at, offset, start, end, side, column) in enumerate(wanted):
                owner = here.at(offset)
                for which, (buffer, rows) in enumerate(
                    (
                        (raises, slice(0, rank_rows)),
                        (weights, slice(rank_rows, rank_rows + own_rows)),
                    )
                ):
                    copies.append(
                        pltpu.make_async_copy(
                            blocks[at].at[rows, start:end],
                            buffer.at[side, owner, :, column : column + end - start],
                            sem.at[number, which],
                        )
                    )
            for copy in copies:
                copy.start()
            for copy in copies:
                copy.wait()

        for side, (lower, full, raised) in enumerate(
            ((lower_g, full_g, raised_g), (lower_u, full_u, raised_u))
        ):
            columns = pl.ds(pl.multiple_of(step * tile, 128), tile)
            up_matrix = raises[side, :, :, columns].reshape(rank, tile)
            raised[...] = up_matrix
            for f in range(n_f):
                total = weights[side, f, :, columns].astype(wide) + mul(lower[f], up_matrix)
                total = total.astype(low)
                full[f] = total
                merged[side, f * own_rows : (f + 1) * own_rows, :] = total

        def some(i, carry):
            at = pl.ds(pl.multiple_of(i * chunk, chunk), chunk)
            gate = mul(x[at, :], merged[0])
            up = mul(x[at, :], merged[1])
            value, slope = gelu_parts(gate)
            hidden[at, :] = (value * up).astype(low)
            back_g[at, :] = (up * slope).astype(low)
            back_u[at, :] = value.astype(low)
            return carry

        lax.fori_loop(0, count // chunk, some, 0, unroll=True)

    by_column = pl.BlockSpec((count, tile), lambda j: (0, j + first))
    by_weight = pl.BlockSpec((n_f, own_rows, tile), lambda j: (0, 0, j + first))
    by_raise = pl.BlockSpec((rank, tile), lambda j: (0, j + first))
    return pl.pallas_call(
        body,
        grid=(stop - first,),
        out_shape=(jax.ShapeDtypeStruct((count, slab), low),) * 3
        + (jax.ShapeDtypeStruct((n_f, own_rows, slab), low),) * 2
        + (jax.ShapeDtypeStruct((rank, slab), low),) * 2,
        in_specs=[VMEM] * 3 + [ANY] * (len(items) + len(before)),
        input_output_aliases={3 + len(items) + i: i for i in range(len(before))},
        out_specs=(by_column,) * 3 + (by_weight,) * 2 + (by_raise,) * 2,
        scratch_shapes=[
            pltpu.VMEM((2, n_f, rank_rows, (stop - first) * tile), low),
            pltpu.VMEM((2, n_f, own_rows, (stop - first) * tile), low),
            pltpu.VMEM((2, width, tile), low),
            pltpu.SemaphoreType.DMA((len(wanted), 2)),
        ],
        cost_estimate=brief(3),
        compiler_params=pltpu.CompilerParams(vmem_limit_bytes=56 * 2**20),
    )(tokens2, *adapters, *(block for _, block, _ in items), *before)


def mlp_backward(items, d_raise, g_tokens, back_g, back_u, n_f, n_seq, cut, slab):
    count, width = g_tokens.shape
    rank = d_raise.shape[0]
    tile = 256 if slab % 256 == 0 else 128
    chunk = 512
    offsets = [(offset, column) for offset, _, column in items]

    def body(g, raised, mul_g, mul_u, *refs):
        blocks = refs[: len(items)]
        grad_g, grad_u, full, raw, merged, sem = refs[len(items) :]
        here = Places(n_f, n_seq)
        step = pl.program_id(0)

        @pl.when(step == 0)
        def _():
            landing(
                [(o, ref, c) for (o, c), ref in zip(offsets, blocks, strict=True)],
                (raw,),
                (cut,),
                sem,
                here,
            )
            for f in range(n_f):
                merged[f * cut : (f + 1) * cut, :] = raw[f, :, :width].astype(wide) + mul(
                    raw[f, :, width:], raised[...]
                )
            if slab > n_f * cut:
                merged[n_f * cut :, :] = jnp.zeros((slab - n_f * cut, width), wide)

        weight = merged[pl.ds(pl.multiple_of(step * tile, tile), tile), :].astype(low)
        full[...] = weight

        def some(i, carry):
            at = pl.ds(pl.multiple_of(i * chunk, chunk), chunk)
            g_hidden = mul_t(g[at, :], weight)
            grad_g[at, :] = (g_hidden * mul_g[at, :].astype(wide)).astype(low)
            grad_u[at, :] = (g_hidden * mul_u[at, :].astype(wide)).astype(low)
            return carry

        lax.fori_loop(0, count // chunk, some, 0, unroll=True)

    by_column = pl.BlockSpec((count, tile), lambda j: (0, j))
    return pl.pallas_call(
        body,
        grid=(slab // tile,),
        out_shape=(jax.ShapeDtypeStruct((count, slab), low),) * 2
        + (jax.ShapeDtypeStruct((slab, width), low),),
        in_specs=[VMEM] * 2 + [by_column] * 2 + [ANY] * len(items),
        out_specs=(by_column,) * 2 + (pl.BlockSpec((tile, width), lambda j: (j, 0)),),
        scratch_shapes=[
            pltpu.VMEM((n_f, cut, width + rank), low),
            pltpu.VMEM((slab, width), wide),
            pltpu.SemaphoreType.DMA((len(items), 1)),
        ],
        cost_estimate=brief(3),
        compiler_params=pltpu.CompilerParams(vmem_limit_bytes=56 * 2**20),
    )(g_tokens, d_raise, back_g, back_u, *(block for _, block, _ in items))


def shards(
    inputs,
    cotangent,
    segments,
    exits,
    confidence,
    attn_gain,
    q_weight,
    k_weight,
    v_weight,
    o_weight,
    q_down,
    q_up,
    k_down,
    k_up,
    v_down,
    v_up,
    o_down,
    o_up,
    mlp_gain,
    gate_weight,
    up_weight,
    down_weight,
    gate_down,
    gate_up,
    up_down,
    up_up,
    down_down,
    down_up,
):
    n_seq, n_f = lax.axis_size("seq"), lax.axis_size("fsdp")
    me = lax.axis_index("seq")
    ring = Ring(n_f, n_seq // CORES)
    group = Group(n_seq)
    rows, length, width = inputs.shape
    tokens = rows * length
    rank = q_down.shape[1]
    hq = q_weight.shape[1]
    ff = gate_weight.shape[1]
    own_rows = q_weight.shape[0]
    rank_rows = q_up.shape[0]
    o_rows = o_weight.shape[0]
    cut = ff // (n_f * n_seq)
    slab = -(-n_f * cut // 128) * 128
    scale = HD ** (-0.5)

    gain1 = attn_gain.astype(wide)[:, None]
    gain2 = mlp_gain.astype(wide)[:, None]

    def rows_of(array):
        part = array.shape[0] // n_seq
        return lax.dynamic_slice_in_dim(array, me * part, part, 0)

    small_blocks = pack_small(
        gain1,
        gain2,
        (q_weight, k_weight, v_weight, q_down, k_down, v_down),
        (gate_down, up_down),
        (q_up, k_up, v_up),
        (o_up, down_up),
        (o_weight, o_down),
        n_seq,
    )

    slabs = Gathering(
        ring, cut_columns((gate_weight, up_weight), (gate_up, up_up), gain2, n_f, n_seq, slab)
    )
    d_lower = rows_of(down_down)
    downs = Gathering(ring, jnp.concatenate([rows_of(down_weight), d_lower], axis=1))

    depth_ids = jnp.arange(DEPTHS, dtype=jnp.int32)
    matches = (exits.reshape(tokens)[:, None] == depth_ids[None, :]).astype(wide)
    counted = Summing(
        jnp.concatenate(
            [jnp.sum(matches, axis=0), jnp.sum(matches * confidence.reshape(tokens)[:, None], axis=0)]
        ),
        ("seq", "fsdp"),
    )
    resid = inputs.reshape(tokens, width).astype(wide)
    active = (exits.reshape(tokens) >= LOOP).astype(wide)[:, None]
    cot = cotangent.reshape(tokens, width).astype(wide)
    g_mlp = (active * cot).astype(low)
    places = me * length + jnp.arange(length, dtype=jnp.int32)
    frequency = rope_base ** (-2.0 * jnp.arange(HD // 2, dtype=wide) / HD)
    angles = jnp.tile(places, rows).astype(wide)[:, None] * frequency[None, :]
    cosine, sine = jnp.cos(angles), jnp.sin(angles)
    r1 = lax.rsqrt(jnp.mean(resid * resid, axis=-1, keepdims=True) + epsilon)
    unit1 = (resid * r1).astype(low)

    slabs.advance()
    seg_pieces = group.across(group.over(segments.astype(low)))
    key_seg = jnp.concatenate(seg_pieces, axis=1).astype(jnp.int32)
    key_place = jnp.concatenate(
        [
            group.index(k, c) * length + jnp.arange(length, dtype=jnp.int32)
            for k, c in group.order
        ]
    )
    allowed = (segments[:, :, None] == key_seg[:, None, :]) & (
        key_place[None, None, :] <= places[None, :, None]
    )
    mask = jnp.where(allowed, 0.0, -1e30).astype(wide)
    whole = gather_whole(small_blocks, (False, False, True, True, True), 0, n_f, n_seq)
    whole, mask, unit1, cosine, sine, g_mlp = tie(
        (slabs, downs), (whole, mask, unit1, cosine, sine, g_mlp)
    )
    qkv_side, ups, side_o, ups2, adapters = (part.reshape(-1, part.shape[2]) for part in whole)
    kv = HD
    lin = hq + 2 * kv
    gate_adapter, up_adapter = adapters[:, :rank], adapters[:, rank : 2 * rank]
    side_o = side_o[:, : width + rank]
    q_raise, k_raise, v_raise = ups[:, :hq], ups[:, hq : hq + kv], ups[:, hq + kv : lin]
    o_raise, d_raise = ups2[:, :width], ups2[:, width : 2 * width]

    slabs.advance()
    half = HD // 2
    queries, both, inner = project(unit1, qkv_side, ups, cosine, sine, hq, rank)
    both = gather_group(both, 2, n_seq)
    both, queries, mask, inner, g_mlp = tie((slabs,), (both, queries, mask, inner, g_mlp))
    q_inner, k_inner, v_inner = inner[:, :rank], inner[:, rank : 2 * rank], inner[:, 2 * rank :]

    slabs.advance()
    g_mlp = group.over(g_mlp)
    attn_low, log_total = attention(queries, both, mask, rows)
    projected = mul(attn_low, side_o)
    o_inner = projected[:, width:].astype(low)
    mid = resid + active * (projected[:, :width] + mul(o_inner, o_raise))
    r2 = lax.rsqrt(jnp.mean(mid * mid, axis=-1, keepdims=True) + epsilon)
    unit2 = (mid * r2).astype(low)
    unit2, mid, r2, g_mlp, attn_low, o_inner, log_total, gate_adapter, up_adapter, d_raise = tie(
        (slabs,),
        (
            unit2,
            mid,
            r2,
            g_mlp,
            attn_low,
            o_inner,
            log_total,
            gate_adapter.reshape(n_f, own_rows, rank),
            up_adapter.reshape(n_f, own_rows, rank),
            d_raise,
        ),
    )

    slabs.advance()
    downs.advance()
    unit2 = gather_group(unit2, 3, n_seq).reshape(-1, width)
    unit2, g_mlp = tie((slabs, downs), (unit2, g_mlp))

    downs.advance()
    g_mlp = group.across(g_mlp)
    tiles = slab // (256 if slab % 256 == 0 else 128)
    arrived = slabs.done()

    def forward(first, stop, before):
        return mlp_forward(
            arrived,
            unit2,
            (gate_adapter, up_adapter),
            before,
            (first, stop),
            n_f,
            n_seq,
            rank_rows,
            own_rows,
            slab,
        )

    half_way = forward(0, (tiles + 1) // 2, ())
    half_way, g_mlp = tie((downs,), (half_way, g_mlp))
    downs.advance()
    counted.advance()
    hidden, back_g, back_u, gate_full, up_full, g_raise, u_raise = forward(
        (tiles + 1) // 2, tiles, half_way
    )
    hidden, back_g, back_u, g_mlp = tie((downs, counted), (hidden, back_g, back_u, g_mlp))
    g_mlp = jnp.concatenate(g_mlp, axis=0)

    downs.advance()
    counted.advance()
    g_down = t_mul(hidden, g_mlp).astype(low)
    g_down, g_mlp, back_g, back_u = tie((downs, counted), (g_down, g_mlp, back_g, back_u))

    down_sums = Scattering(ring, [[g_down[: n_f * cut].reshape(n_f, cut, width)]], n_seq)

    down_sums.advance()
    counted.advance()
    g_gate, g_up, down_full = mlp_backward(
        downs.done(), d_raise, g_mlp, back_g, back_u, n_f, n_seq, cut, slab
    )
    g_gate, g_up, down_full = tie((down_sums, counted), (g_gate, g_up, down_full))

    down_sums.advance()
    counted.advance()
    gg = t_mul(unit2, g_gate).astype(low)
    gg_raise = t_mul(gate_adapter.reshape(width, rank), gg).astype(low)
    gg, gg_raise, g_gate, g_up, unit2 = tie(
        (down_sums, counted), (gg, gg_raise, g_gate, g_up, unit2)
    )
    down_sums.advance()
    gu = t_mul(unit2, g_up).astype(low)
    gu_raise = t_mul(up_adapter.reshape(width, rank), gu).astype(low)
    gg, gu, gg_raise, gu_raise, g_gate, g_up = tie(
        (down_sums,), (gg, gu, gg_raise, gu_raise, g_gate, g_up)
    )
    slab_sums = Scattering(
        ring,
        [
            [part.reshape(n_f, -1, slab) for part in side]
            for side in ((gg_raise, gg), (gu_raise, gu))
        ],
        n_seq,
    )
    chips = range(n_seq // CORES)
    here_tokens = CORES * tokens

    def token_gradient(at):
        result = mul_t(g_gate[at], gate_full.reshape(width, slab))
        return (result + mul_t(g_up[at], up_full.reshape(width, slab))).astype(low)

    slab_sums.advance()
    e2_there = token_gradient(slice(here_tokens, None))
    g_down = down_sums.done(low)
    down_rows = jnp.concatenate([g_down, mul_t(g_down, d_raise).astype(low)], axis=1)
    gd_raise = t_mul(d_lower, g_down).astype(low)
    e2_there, g_gate, g_up, down_rows, gd_raise = tie(
        (slab_sums,), (e2_there, g_gate, g_up, down_rows, gd_raise)
    )

    slab_sums.advance()
    there = [e2_there[i * tokens : (i + 1) * tokens] for i in range(n_seq - CORES)]
    e2_near = [group.swap(there[(k - 1) * CORES + 1]) for k in chips[1:]]
    down_rows = group.over(down_rows)
    e2_here = token_gradient(slice(0, here_tokens))
    e2_here, e2_near, hidden, down_rows = tie((slab_sums,), (e2_here, e2_near, hidden, down_rows))

    slab_sums.advance()
    e2_sums = [
        there[(k - 1) * CORES].astype(wide) + e2_near[k - 1].astype(wide) for k in chips[1:]
    ]
    e2_far = group.send([None, *e2_sums])
    e2_own = group.swap(e2_here[tokens:])
    branch = mul(hidden, down_full).astype(low)
    branch, e2_far, e2_own, e2_here = tie((slab_sums,), (branch, e2_far, e2_own, e2_here))
    terms = [branch[i * tokens : (i + 1) * tokens] for i in range(n_seq)]
    e2 = e2_here[:tokens].astype(wide) + e2_own.astype(wide)
    for block in e2_far:
        e2 = e2 + block.astype(wide)

    slab_sums.advance()
    near = group.cross(terms)
    g_mid = cot + r2 * e2 - mid * (r2 * r2 * r2 * jnp.mean(e2 * mid, axis=-1, keepdims=True))
    g_branch = (active * g_mid).astype(low)
    g_inner = mul_t(g_branch, o_raise).astype(low)
    g_attn = mul_t(jnp.concatenate([g_branch, g_inner], axis=1), side_o).astype(low)
    own_full = [
        lax.dynamic_index_in_dim(full, lax.axis_index("fsdp"), 0, False)
        for full in (gate_full, up_full)
    ]
    merged = jnp.concatenate(own_full, axis=1)
    own_q = q_weight.astype(wide) + mul(q_down, q_raise)
    own_kv = jnp.concatenate(
        [
            k_weight.astype(wide) + mul(k_down, k_raise),
            v_weight.astype(wide) + mul(v_down, v_raise),
        ],
        axis=1,
    )
    g_attn, terms, near, g_mid, g_branch, down_rows, merged, own_q, own_kv = tie(
        (slab_sums,),
        (g_attn, terms, near, g_mid, g_branch, down_rows, merged, own_q, own_kv),
    )

    down_rows = group.across(down_rows)
    sums = [terms[k * CORES].astype(wide) + near[k].astype(wide) for k in chips]
    middle = tokens // 2
    far_first = group.send([block[:middle] for block in sums])
    g_q, d_terms = attention_back(
        queries, both, mask, log_total, attn_low, g_attn, cosine, sine, rows
    )
    o_pack = output_gradients(
        attn_low, o_inner, g_branch, gd_raise.reshape(n_f, rank_rows, width), n_f
    )
    d_terms, g_q, g_mid, o_pack, down_rows, sums, far_first = tie(
        (), (d_terms, g_q, g_mid, o_pack, down_rows, sums, far_first)
    )

    d_near = group.cross([d_terms[i] for i in range(n_seq)])
    d_sums = [d_terms[k * CORES].astype(wide) + d_near[k].astype(wide) for k in chips]
    d_far = group.send(d_sums)
    e1, q_pack = query_gradients(unit1, q_inner, g_q, ups, qkv_side, hq, rank, n_f)
    grad_down_weight, grad_down_down = lay_rows(down_rows, width, n_seq)
    d_far, e1, d_both, q_pack, grad_down_weight, grad_down_down = tie(
        (), (d_far, e1, d_sums[0], q_pack, grad_down_weight, grad_down_down)
    )

    for block in d_far:
        d_both = d_both + block.astype(wide)
    first, second = d_both[:, :half], d_both[:, half:HD]
    g_k = jnp.concatenate(
        [first * cosine + second * sine, second * cosine - first * sine], axis=1
    ).astype(low)
    g_v = d_both[:, HD:].astype(low)
    gi_k = mul_t(g_k, k_raise).astype(low)
    gi_v = mul_t(g_v, v_raise).astype(low)
    g_kv = jnp.concatenate([g_k, g_v], axis=1)
    e1 = e1 + mul_t(g_kv, qkv_side[:, hq:lin])
    e1 = e1 + mul_t(jnp.concatenate([gi_k, gi_v], axis=1), qkv_side[:, lin + rank :])
    input_grad = g_mid + r1 * e1 - resid * (
        r1 * r1 * r1 * jnp.mean(e1 * resid, axis=-1, keepdims=True)
    )
    input_grad = input_grad.astype(low).reshape(rows, length, width)
    kv_pack = jnp.concatenate(
        [
            t_mul(unit1, g_kv).astype(low).reshape(n_f, own_rows, 2 * kv),
            jnp.concatenate([t_mul(k_inner, g_k), t_mul(v_inner, g_v)], axis=1)
            .astype(low)
            .reshape(n_f, rank_rows, 2 * kv),
        ],
        axis=1,
    )
    kv_pack, input_grad, sums = tie((), (kv_pack, input_grad, sums))

    g_slab = slab_sums.done(wide)
    unit_grad = g_slab[rank_rows:]
    weight_grad = (unit_grad * gain2).astype(low)
    mlp_small = jnp.concatenate(
        [
            mul_t(weight_grad[:, :slab], g_raise),
            mul_t(weight_grad[:, slab:], u_raise),
            jnp.broadcast_to(
                jnp.sum(unit_grad * merged.astype(wide), axis=1, keepdims=True) / gain2, (own_rows, 128)
            ),
        ],
        axis=1,
    ).astype(low)
    far = group.send([block[middle:] for block in sums])
    packs, slab_pieces, mlp_small = scatter_whole(
        (o_pack, q_pack, kv_pack), g_slab.astype(low), mlp_small, 6, n_seq
    )
    packs, slab_pieces, mlp_small, far = tie((), (packs, slab_pieces, mlp_small, far))
    own_branch = sums[0]
    for first, second in zip(far_first, far, strict=True):
        own_branch = own_branch + jnp.concatenate([first, second], axis=0).astype(wide)
    outputs = (mid + active * own_branch).astype(low).reshape(rows, length, width)
    packs[0] = packs[0][:, :width]
    o_pack, q_pack, kv_pack = (pack.astype(wide) for pack in packs)

    grad_o_weight = o_pack[:o_rows]
    grad_o_up = o_pack[o_rows : o_rows + rank_rows]
    grad_down_up = o_pack[o_rows + rank_rows :]
    grad_o_down = mul_t(packs[0][:o_rows], o_raise)
    grad_q_weight = q_pack[:own_rows] * gain1
    grad_kv = kv_pack[:own_rows] * gain1
    grad_k_weight, grad_v_weight = grad_kv[:, :kv], grad_kv[:, kv:]
    grad_q_up = q_pack[own_rows:]
    grad_k_up, grad_v_up = kv_pack[own_rows:, :kv], kv_pack[own_rows:, kv:]
    grad_q_down = mul_t(grad_q_weight.astype(low), q_raise)
    grad_k_down = mul_t(grad_k_weight.astype(low), k_raise)
    grad_v_down = mul_t(grad_v_weight.astype(low), v_raise)
    grad_attn_gain = jnp.sum(q_pack[:own_rows] * own_q, axis=1) + jnp.sum(
        kv_pack[:own_rows] * own_kv, axis=1
    )

    grad_gate_down, grad_up_down = mlp_small[:, :rank], mlp_small[:, rank : 2 * rank]
    grad_mlp_gain = mlp_small[:, 2 * rank]
    grad_gate_weight, grad_up_weight, grad_gate_up, grad_up_up = place_columns(
        slab_pieces, gain2, n_f, n_seq, rank_rows, ff, slab
    )

    counted = counted.done()
    mean_confidence = counted[DEPTHS:] / counted[:DEPTHS]
    return (
        outputs,
        input_grad,
        grad_attn_gain,
        grad_q_weight,
        grad_k_weight,
        grad_v_weight,
        grad_o_weight,
        grad_q_down,
        grad_q_up,
        grad_k_down,
        grad_k_up,
        grad_v_down,
        grad_v_up,
        grad_o_down,
        grad_o_up,
        grad_mlp_gain,
        grad_gate_weight,
        grad_up_weight,
        grad_down_weight,
        grad_gate_down,
        grad_gate_up,
        grad_up_down,
        grad_up_up,
        grad_down_down,
        grad_down_up,
        counted[:DEPTHS].astype(jnp.int32),
        mean_confidence,
    )


def solution(mesh):
    tokens3 = P("fsdp", "seq", None)
    tokens2 = P("fsdp", "seq")
    vector, matrix = P("fsdp"), P("fsdp", None)
    in_specs = (tokens3,) * 2 + (tokens2,) * 3 + (vector,) + (matrix,) * 12 + (vector,) + (matrix,) * 9
    out_specs = (
        (tokens3,) * 2 + (vector,) + (matrix,) * 12 + (vector,) + (matrix,) * 9 + (P(), P())
    )
    return jax.shard_map(shards, mesh=mesh, in_specs=in_specs, out_specs=out_specs, check_vma=False)
```
